32 devices in a mesh: worker: 4 (over y, x), fsdp: 8 (over z, core).
Axes of the slice: x: 2, y: 2, z: 4, core: 2. Of those that a mesh axis runs over, the one named last changes fastest.
Arguments:
- params: float32 [4, 4096, 128], P('worker', 'fsdp'), may hold values from -6 to 6
- first_moment: float32 [4, 4096, 128], P('worker', 'fsdp'), may hold values from -4 to 4
- second_moment: float32 [4, 4096, 128], P('worker', 'fsdp'), may hold values from 0.05 to 2
- global_fragment: float32 [1024, 128], P('fsdp'), may hold values from -6 to 6
- outer_momentum: float32 [1024, 128], P('fsdp'), may hold values from -6 to 6
- features: bfloat16 [4, 1024, 4096], P('worker', 'fsdp'), may hold values from -6 to 6
- cotangent: bfloat16 [4, 1024, 128], P('worker', 'fsdp'), may hold values from -192 to 192
- token_counts: int32 [4], replicated, may hold values from 128 to 1024
- fragment_index: int32 [1], replicated, may hold values from 0 to 3
Outputs:
- new_params: float32 [4, 4096, 128], P('worker', 'fsdp')
- new_first: float32 [4, 4096, 128], P('worker', 'fsdp')
- new_second: float32 [4, 4096, 128], P('worker', 'fsdp')
- new_global: float32 [1024, 128], P('fsdp')
- new_momentum: float32 [1024, 128], P('fsdp')
The draws below stay inside these ranges and needn't reach their ends.
All inputs are finite; a program needn't handle non-finite values.
Results may differ from the reference program's by a relative error of at most 0.0003.
Values sent between devices are 32-bit elements; how exact they have to be, the bound alone decides.
No kernel may reach another device: no remote copies, remote signals or barrier semaphores. Data moves between devices by JAX's collectives and lax.ppermute only.
A program may use at most 64 MiB of HBM per device.

```python
import math
import jax
import jax.numpy as jnp
from jax import lax

D = 4096
KVW = 128
FRAGS = 4
TOK_W = 1024
WORKERS = 4
FROWS = 1024


def touch_ends(entries, rng, smallest, high):
    longest = entries.shape.index(max(entries.shape))
    spots = []
    for shift in (0, 1):
        where = [jax.random.randint(jax.random.fold_in(rng, axis), (), 0, length) for axis, length in enumerate(entries.shape)]
        where[longest] = (where[longest] + shift) % entries.shape[longest]
        spots.append(tuple(where))
    return entries.at[spots[0]].set(smallest).at[spots[1]].set(high)


def block_levels(own_key, extent, shards, least, largest):
    def one(axis_at, shards_of):
        draws = jax.random.uniform(jax.random.fold_in(jax.random.fold_in(own_key, 6), axis_at), (shards_of,), jnp.float32, least / len(shards), largest / len(shards))
        return jnp.repeat(jnp.exp(draws), extent[axis_at] // shards_of).reshape((-1,) + (1,) * (len(extent) - axis_at - 1))

    factor_of = one(*shards[0])
    for cut in shards[1:]:
        factor_of = factor_of * one(*cut)
    return factor_of


def bell_draw(own_key, shape, scale, bound, cuts=(), kind=jnp.bfloat16):
    entries = scale * jax.random.normal(own_key, shape, jnp.float32)
    if cuts:
        entries = entries * block_levels(own_key, shape, cuts, -0.22, 0.18)
    return jnp.clip(entries, -bound, bound).astype(kind)


def setup_inputs(seed: int = 0) -> dict:
    keys = jax.random.split(jax.random.key(seed), 10)
    return {
        "params": bell_draw(keys[0], (WORKERS, D, KVW), 1.0, 6.0, ((0, 4), (1, 8)), jnp.float32),
        "first_moment": bell_draw(keys[1], (WORKERS, D, KVW), 0.3, 4.0, ((0, 4), (1, 8)), jnp.float32),
        "second_moment": jnp.clip(jnp.exp(math.log(2.0) - 3.6888794 * jax.random.uniform(keys[2], (WORKERS, D, KVW), jnp.float32) ** block_levels(keys[2], (WORKERS, D, KVW), ((0, 4), (1, 8)), -0.2, 0.2)), 0.05, 2.0),
        "global_fragment": bell_draw(keys[3], (FROWS, KVW), 1.0, 6.0, ((0, 8),), jnp.float32),
        "outer_momentum": bell_draw(keys[4], (FROWS, KVW), 0.5, 6.0, ((0, 8),), jnp.float32),
        "features": bell_draw(keys[5], (WORKERS, TOK_W, D), 1.0, 6.0, ((0, 4), (1, 8))),
        "cotangent": bell_draw(keys[6], (WORKERS, TOK_W, KVW), (TOK_W ** 0.5), 192.0, ((0, 4), (1, 8))),
        "token_counts": touch_ends(jax.random.randint(keys[7], (WORKERS,), TOK_W // 8, TOK_W + 1), jax.random.fold_in(keys[7], 1), TOK_W // 8, TOK_W).astype(jnp.int32),
        "fragment_index": jax.random.randint(keys[8], (1,), 0, FRAGS).astype(jnp.int32),
    }


BETA_ONE = 0.9
BETA_TWO = 0.95
CORRECT_ONE = 0.6513216
CORRECT_TWO = 0.401263
ADAM_EPS = 1e-08
LEARN_RATE = 0.02
DECAY_RATE = 0.1
NESTEROV = 0.9
OUTER_RATE = 0.7
MIXING = 0.5

def reference(params, first_moment, second_moment, global_fragment, outer_momentum, features, cotangent, token_counts, fragment_index):
    fragment = fragment_index[0].astype(jnp.int32)
    token_total = jnp.sum(token_counts).astype(jnp.float32)
    positions = jnp.arange(TOK_W, dtype=jnp.int32)
    drift_sum = jnp.zeros((FROWS, KVW), jnp.float32)
    inner_list, first_list, second_list = ([], [], [])
    for worker in range(WORKERS):
        live_count = token_counts[worker]
        valid_rows = (positions < live_count)[:, None]
        masked = jnp.where(valid_rows, cotangent[worker], jnp.zeros_like(cotangent[worker]))
        gradient = jnp.dot(features[worker].T, masked, preferred_element_type=jnp.float32) / live_count.astype(jnp.float32)
        before = params[worker]
        old_piece = lax.dynamic_index_in_dim(before.reshape(FROWS, FRAGS, KVW), fragment, 1, keepdims=False)
        drift_sum = drift_sum + live_count.astype(jnp.float32) * (global_fragment - old_piece)
        first_new = BETA_ONE * first_moment[worker] + (1.0 - BETA_ONE) * gradient
        second_new = BETA_TWO * second_moment[worker] + (1.0 - BETA_TWO) * gradient * gradient
        update = first_new / CORRECT_ONE / (jnp.sqrt(second_new / CORRECT_TWO) + ADAM_EPS)
        inner_list.append(before - LEARN_RATE * (update + DECAY_RATE * before))
        first_list.append(first_new)
        second_list.append(second_new)
    pseudo_grad = drift_sum / token_total
    momentum = NESTEROV * outer_momentum + pseudo_grad
    fresh_global = global_fragment - OUTER_RATE * (pseudo_grad + NESTEROV * momentum)
    result_list = []
    for worker in range(WORKERS):
        inner_three = inner_list[worker].reshape(FROWS, FRAGS, KVW)
        inner_piece = lax.dynamic_index_in_dim(inner_three, fragment, 1, keepdims=False)
        mixed_piece = MIXING * fresh_global + (1.0 - MIXING) * inner_piece
        merged = lax.dynamic_update_index_in_dim(inner_three, mixed_piece, fragment, 1)
        result_list.append(merged.reshape(D, KVW))
    return (jnp.stack(result_list), jnp.stack(first_list), jnp.stack(second_list), fresh_global, momentum)
```

```python
import jax
import jax.numpy as jnp
from jax import lax
from jax.sharding import PartitionSpec as P

FRAGS = 4
CORES = 2

BETA_ONE = 0.9
BETA_TWO = 0.95
CORRECT_ONE = 0.6513216
CORRECT_TWO = 0.401263
ADAM_EPS = 1e-08
LEARN_RATE = 0.02
DECAY_RATE = 0.1
NESTEROV = 0.9
OUTER_RATE = 0.7
MIXING = 0.5


def contract_rows(left_rows, right_rows):
    return lax.dot_general(
        left_rows, right_rows, (((0,), (0,)), ((), ())), preferred_element_type=jnp.float32
    )


def chip_hop(chips, step, first, last):
    pairs = []
    for chip in range(first, last + 1):
        if 0 <= chip + step < chips:
            for core in range(CORES):
                pairs.append((chip * CORES + core, (chip + step) * CORES + core))
    return pairs


def line_scatter(term, devices):
    chips = devices // CORES
    place = lax.axis_index("fsdp")
    chip, core = place // CORES, place % CORES
    rows, width = term.shape[0] // devices, term.shape[1]
    blocks = term.reshape(chips, CORES, rows, width)
    away = lax.dynamic_index_in_dim(blocks, 1 - core, 1, keepdims=False)
    kept = lax.dynamic_index_in_dim(blocks, core, 1, keepdims=False)
    swap = [(d, d ^ 1) for d in range(devices)]
    both = kept + lax.ppermute(away, "fsdp", swap)
    up = down = None
    for turn in range(1, chips):
        send_up = lax.dynamic_index_in_dim(both, jnp.minimum(chip + chips - turn, chips - 1), 0, keepdims=False)
        send_down = lax.dynamic_index_in_dim(both, jnp.maximum(chip - chips + turn, 0), 0, keepdims=False)
        if up is not None:
            send_up, send_down = send_up + up, send_down + down
        up = lax.ppermute(send_up, "fsdp", chip_hop(chips, 1, 0, turn - 1))
        down = lax.ppermute(send_down, "fsdp", chip_hop(chips, -1, chips - turn, chips - 1))
    own = lax.dynamic_index_in_dim(both, chip, 0, keepdims=False)
    return own + up + down


def doubling_sum(value, axis, devices):
    reach = devices // 2
    while reach:
        value = value + lax.ppermute(value, axis, [(d, d ^ reach) for d in range(devices)])
        reach //= 2
    return value


def make_body(mesh):
    workers, shards = mesh.shape["worker"], mesh.shape["fsdp"]

    def body(
        params,
        first_moment,
        second_moment,
        global_fragment,
        outer_momentum,
        features,
        cotangent,
        token_counts,
        fragment_index,
    ):
        worker = lax.axis_index("worker")
        live_count = lax.dynamic_index_in_dim(token_counts, worker, 0, keepdims=False)
        tok_local = features.shape[1]
        positions = lax.axis_index("fsdp") * tok_local + lax.iota(jnp.int32, tok_local)
        valid_rows = (positions < live_count)[:, None]
        masked = jnp.where(valid_rows, cotangent[0], jnp.zeros_like(cotangent[0]))
        local_rows = params.shape[1]
        term = contract_rows(features[0], masked)
        summed = line_scatter(term, shards)
        gradient = summed / live_count.astype(jnp.float32)
        fragment = fragment_index[0]
        width = params.shape[2]
        before = params[0]
        before_three = before.reshape(local_rows // FRAGS, FRAGS, width)
        old_piece = lax.dynamic_index_in_dim(before_three, fragment, 1, keepdims=False)
        token_total = jnp.sum(token_counts).astype(jnp.float32)
        drift_term = live_count.astype(jnp.float32) * (global_fragment - old_piece)
        pseudo_grad = doubling_sum(drift_term, "worker", workers) / token_total
        momentum = NESTEROV * outer_momentum + pseudo_grad
        fresh_global = global_fragment - OUTER_RATE * (pseudo_grad + NESTEROV * momentum)
        first_new = BETA_ONE * first_moment[0] + (1.0 - BETA_ONE) * gradient
        second_new = BETA_TWO * second_moment[0] + (1.0 - BETA_TWO) * gradient * gradient
        update = first_new / CORRECT_ONE / (jnp.sqrt(second_new / CORRECT_TWO) + ADAM_EPS)
        inner_params = before - LEARN_RATE * (update + DECAY_RATE * before)
        inner_three = inner_params.reshape(local_rows // FRAGS, FRAGS, width)
        inner_piece = lax.dynamic_index_in_dim(inner_three, fragment, 1, keepdims=False)
        mixed_piece = MIXING * fresh_global + (1.0 - MIXING) * inner_piece
        result = lax.dynamic_update_index_in_dim(inner_three, mixed_piece, fragment, 1).reshape(
            local_rows, width
        )
        return (result[None], first_new[None], second_new[None], fresh_global, momentum)

    return body


def solution(mesh):
    state = P("worker", "fsdp", None)
    piece = P("fsdp", None)
    return jax.shard_map(
        make_body(mesh),
        mesh=mesh,
        in_specs=(state, state, state, piece, piece, state, state, P(), P()),
        out_specs=(state, state, state, piece, piece),
        check_vma=False,
    )
```

```python
import functools

import jax
import jax.numpy as jnp
from jax import lax
from jax.experimental import pallas as pl
from jax.experimental.pallas import tpu as pltpu
from jax.sharding import PartitionSpec as P

FRAGS = 4
LANES = 128

BETA_ONE = 0.9
BETA_TWO = 0.95
CORRECT_ONE = 0.6513216
CORRECT_TWO = 0.401263
ADAM_EPS = 1e-08
LEARN_RATE = 0.02
DECAY_RATE = 0.1
NESTEROV = 0.9
OUTER_RATE = 0.7
MIXING = 0.5

VMEM = pl.BlockSpec(memory_space=pltpu.VMEM)
SMEM = pl.BlockSpec(memory_space=pltpu.SMEM)
HBM = pl.BlockSpec(memory_space=pl.ANY)
ROOM = 8 << 20


def masked_rows(counts, cot_ref):
    tokens = cot_ref.shape[1]
    live = counts[lax.axis_index("worker")] - lax.axis_index("fsdp") * tokens
    cot = cot_ref[0].astype(jnp.float32)
    rows = lax.broadcasted_iota(jnp.int32, cot.shape, 0)
    return jnp.where(rows < live, cot, 0.0).astype(jnp.bfloat16)


def products(order, counts, cot_ref, features, held, sems, put):
    rows = held.shape[2]
    me = lax.axis_index("fsdp")
    copies = []
    for slot, q in enumerate(order):
        columns = pl.ds(pl.multiple_of((me ^ q) * rows, LANES), rows)
        copies.append(pltpu.make_async_copy(features.at[0, :, columns], held.at[slot], sems.at[slot]))
        copies[-1].start()
    masked = masked_rows(counts, cot_ref)
    for slot, q in enumerate(order):
        copies[slot].wait()
        put(q, lax.dot_general(masked, held[slot], (((0,), (0,)), ((), ())), preferred_element_type=jnp.float32))


def first_kernel(order, counts, cot_ref, features, away, kept, held, sems):
    def put(q, value):
        (away if q & 1 else kept)[0] = value

    products(order, counts, cot_ref, features, held, sems, put)


def rest_kernel(order, counts, fragment, cot_ref, params, global_fragment, features, away, kept, drift, held, sems):
    def put(q, value):
        (away if q & 1 else kept)[q // 2] = value

    products(order, counts, cot_ref, features, held, sems, put)
    pieces = global_fragment.shape[0]
    old = params[0, pl.ds(fragment[0], pieces, stride=FRAGS), :]
    drift[...] = counts[lax.axis_index("worker")].astype(jnp.float32) * (global_fragment[...] - old)


def adam(before, first, second, gradient):
    first_new = BETA_ONE * first + (1.0 - BETA_ONE) * gradient
    second_new = BETA_TWO * second + (1.0 - BETA_TWO) * gradient * gradient
    update = first_new / CORRECT_ONE / (jnp.sqrt(second_new / CORRECT_TWO) + ADAM_EPS)
    return before - LEARN_RATE * (update + DECAY_RATE * before), first_new, second_new


def outer(pseudo_grad, global_fragment, outer_momentum):
    momentum = NESTEROV * outer_momentum + pseudo_grad
    return global_fragment - OUTER_RATE * (pseudo_grad + NESTEROV * momentum), momentum


def last_kernel(
    workers, terms, counts, fragment, params, first, second, global_fragment, outer_momentum, drift_sum, *refs
):
    parts, (new_params, new_first, new_second, new_global, new_momentum) = refs[:terms], refs[terms:]
    live = counts[lax.axis_index("worker")].astype(jnp.float32)
    total = counts[0]
    for other in range(1, workers):
        total = total + counts[other]
    fresh, momentum = outer(drift_sum[...] / total.astype(jnp.float32), global_fragment[...], outer_momentum[...])
    new_global[...] = fresh
    new_momentum[...] = momentum
    rows = params.shape[1]
    for at in range(0, rows, LANES):
        here = pl.ds(at, LANES)
        summed = parts[0][0, :, here]
        for part in parts[1:]:
            summed = summed + part[0, :, here]
        gradient = summed.T / live
        new_params[0, here, :], new_first[0, here, :], new_second[0, here, :] = adam(
            params[0, here, :], first[0, here, :], second[0, here, :], gradient
        )
    mine = pl.ds(fragment[0], rows // FRAGS, stride=FRAGS)
    new_params[0, mine, :] = MIXING * fresh + (1.0 - MIXING) * new_params[0, mine, :]


def hop(value, axis, devices, bit):
    return lax.ppermute(value, axis, [(d, d ^ bit) for d in range(devices)])


def doubling_sum(value, axis, devices):
    bit = devices // 2
    while bit:
        value = value + hop(value, axis, devices, bit)
        bit //= 2
    return value


def fast_body(mesh):
    workers, devices = mesh.shape["worker"], mesh.shape["fsdp"]

    def body(
        params, first, second, global_fragment, outer_momentum, features, cotangent, token_counts, fragment_index
    ):
        rows, width = params.shape[1:]
        pieces, tokens = global_fragment.shape[0], features.shape[1]
        far = devices - 2
        orders = ([far + 1, far], [q + s for q in range(far - 2, -1, -2) for s in (1, 0)])
        block = functools.partial(jax.ShapeDtypeStruct, dtype=jnp.float32)

        def scratch(count):
            return [pltpu.VMEM((count, tokens, rows), jnp.bfloat16), pltpu.SemaphoreType.DMA((count,))]

        def cost(count):
            return pl.CostEstimate(
                flops=2 * count * tokens * rows * width,
                bytes_accessed=count * rows * (2 * tokens + 4 * width),
                transcendentals=0,
            )

        room = pltpu.CompilerParams(vmem_limit_bytes=ROOM)
        away_far, kept_far = pl.pallas_call(
            functools.partial(first_kernel, orders[0]),
            out_shape=[block((1, width, rows))] * 2,
            in_specs=[SMEM, VMEM, HBM],
            out_specs=[VMEM] * 2,
            scratch_shapes=scratch(2),
            compiler_params=room,
            cost_estimate=cost(2),
        )(token_counts, cotangent, features)
        come_far = hop(away_far, "fsdp", devices, 1)
        near = devices // 2 - 1
        away, kept, drift = pl.pallas_call(
            functools.partial(rest_kernel, orders[1]),
            out_shape=[block((near, width, rows))] * 2 + [block((pieces, width))],
            in_specs=[SMEM, SMEM, VMEM, VMEM, VMEM, HBM],
            out_specs=[VMEM] * 3,
            scratch_shapes=scratch(2 * near),
            compiler_params=room,
            cost_estimate=cost(2 * near),
        )(token_counts, fragment_index, cotangent, params, global_fragment, features)
        come = hop(away, "fsdp", devices, 1)
        step_far = hop(kept_far + come_far, "fsdp", devices, 2)
        step_near = hop(kept[1:2] + come[1:2], "fsdp", devices, 2)
        last = hop(kept[2:3] + come[2:3] + step_far, "fsdp", devices, 4)
        drift_sum = doubling_sum(drift, "worker", workers)
        parts = (kept[0:1], come[0:1], step_near, last)
        state = block(params.shape)
        piece = block(global_fragment.shape)
        return pl.pallas_call(
            functools.partial(last_kernel, workers, len(parts)),
            out_shape=[state] * 3 + [piece] * 2,
            in_specs=[SMEM] * 2 + [VMEM] * (6 + len(parts)),
            out_specs=[VMEM] * 5,
            compiler_params=room,
            cost_estimate=pl.CostEstimate(
                flops=30 * rows * width, bytes_accessed=40 * rows * width, transcendentals=2 * rows * width
            ),
        )(
            token_counts,
            fragment_index,
            params,
            first,
            second,
            global_fragment,
            outer_momentum,
            drift_sum,
            *parts,
        )

    return body


def plain_body(mesh):
    workers, devices = mesh.shape["worker"], mesh.shape["fsdp"]

    def body(
        params, first, second, global_fragment, outer_momentum, features, cotangent, token_counts, fragment_index
    ):
        rows, width = params.shape[1:]
        tokens = features.shape[1]
        me = lax.axis_index("fsdp")
        count = lax.dynamic_index_in_dim(token_counts, lax.axis_index("worker"), 0, keepdims=False)
        live = count.astype(jnp.float32)
        valid = (me * tokens + lax.iota(jnp.int32, tokens) < count)[:, None]
        masked = jnp.where(valid, cotangent[0], jnp.zeros_like(cotangent[0]))
        term = lax.dot_general(features[0], masked, (((0,), (0,)), ((), ())), preferred_element_type=jnp.float32)
        blocks = jnp.take(term.reshape(devices, rows, width), me ^ jnp.arange(devices, dtype=jnp.int32), axis=0)
        bit = 1
        while bit < devices:
            blocks = blocks.reshape(-1, 2, rows, width)
            blocks = blocks[:, 0] + hop(blocks[:, 1], "fsdp", devices, bit)
            bit *= 2
        gradient = blocks[0] / live
        grouped = (rows // FRAGS, FRAGS, width)
        old = lax.dynamic_index_in_dim(params[0].reshape(grouped), fragment_index[0], 1, keepdims=False)
        drift_sum = doubling_sum(live * (global_fragment - old), "worker", workers)
        total = jnp.sum(token_counts).astype(jnp.float32)
        fresh, momentum = outer(drift_sum / total, global_fragment, outer_momentum)
        inner, first_new, second_new = adam(params[0], first[0], second[0], gradient)
        inner = inner.reshape(grouped)
        piece = lax.dynamic_index_in_dim(inner, fragment_index[0], 1, keepdims=False)
        mixed = MIXING * fresh + (1.0 - MIXING) * piece
        merged = lax.dynamic_update_index_in_dim(inner, mixed, fragment_index[0], 1).reshape(rows, width)
        return merged[None], first_new[None], second_new[None], fresh, momentum

    return body


def solution(mesh):
    devices = mesh.shape["fsdp"]

    def pick(*arrays):
        rows = arrays[0].shape[1]
        body = fast_body(mesh) if devices == 8 and rows % LANES == 0 else plain_body(mesh)
        return body(*arrays)

    state = P("worker", "fsdp", None)
    piece = P("fsdp", None)
    return jax.shard_map(
        pick,
        mesh=mesh,
        in_specs=(state, state, state, piece, piece, state, state, P(), P()),
        out_specs=(state, state, state, piece, piece),
        check_vma=False,
    )
```

```python
import functools

import jax
import jax.numpy as jnp
from jax import lax
from jax.experimental import pallas as pl
from jax.experimental.pallas import tpu as pltpu
from jax.sharding import PartitionSpec as P

FRAGS = 4
LANES = 128

BETA_ONE = 0.9
BETA_TWO = 0.95
CORRECT_ONE = 0.6513216
CORRECT_TWO = 0.401263
ADAM_EPS = 1e-08
LEARN_RATE = 0.02
DECAY_RATE = 0.1
NESTEROV = 0.9
OUTER_RATE = 0.7
MIXING = 0.5

VMEM = pl.BlockSpec(memory_space=pltpu.VMEM)
SMEM = pl.BlockSpec(memory_space=pltpu.SMEM)
HBM = pl.BlockSpec(memory_space=pltpu.HBM)
ANY = pl.BlockSpec(memory_space=pl.ANY)
ROOM = 8 << 20


def masked_rows(live, cotangent):
    rows = lax.broadcasted_iota(jnp.int32, cotangent.shape, 0)
    return jnp.where(rows < live, cotangent.astype(jnp.float32), 0.0).astype(jnp.bfloat16)


def columns_of(relative, rows):
    return pl.ds(pl.multiple_of((lax.axis_index("fsdp") ^ relative) * rows, LANES), rows)


def product_halves(masked, features):
    value = lax.dot_general(masked, features, (((0,), (0,)), ((), ())), preferred_element_type=jnp.float32)
    half = value.shape[1] // 2
    return value[:, :half], value[:, half:]


def first_kernel(order, counts, cotangent, features, away, kept, counts_held, cot_held, held, sems):
    small = [
        pltpu.make_async_copy(counts, counts_held, sems.at[0]),
        pltpu.make_async_copy(cotangent, cot_held, sems.at[1]),
    ]
    blocks = [
        pltpu.make_async_copy(features.at[0, :, columns_of(q, held.shape[2])], held.at[slot], sems.at[2 + slot])
        for slot, q in enumerate(order)
    ]
    for copy in small + blocks:
        copy.start()
    for copy in small:
        copy.wait()
    tokens = cot_held.shape[1]
    live = counts_held[lax.axis_index("worker")] - lax.axis_index("fsdp") * tokens
    masked = masked_rows(live, cot_held[0])
    for slot, q in enumerate(order):
        blocks[slot].wait()
        into = away if q & 1 else kept
        into[0], into[1] = product_halves(masked, held[slot])


def rest_kernel(
    order, counts, fragment, cotangent, params, global_fragment, features, after, away, kept, drift
):
    del after
    tokens = cotangent.shape[1]
    count = counts[lax.axis_index("worker")]
    masked = masked_rows(count - lax.axis_index("fsdp") * tokens, cotangent[0])
    for q in order:
        into, at = (away if q & 1 else kept), 2 * (q // 2)
        into[at], into[at + 1] = product_halves(masked, features[0, :, columns_of(q, params.shape[1])])
    old = params[0, pl.ds(fragment[0], global_fragment.shape[0], stride=FRAGS), :]
    drift[...] = count.astype(jnp.float32) * (global_fragment[...] - old)


def adam(before, first, second, gradient):
    first_new = BETA_ONE * first + (1.0 - BETA_ONE) * gradient
    second_new = BETA_TWO * second + (1.0 - BETA_TWO) * gradient * gradient
    update = first_new / CORRECT_ONE / (jnp.sqrt(second_new / CORRECT_TWO) + ADAM_EPS)
    return before - LEARN_RATE * (update + DECAY_RATE * before), first_new, second_new


def outer(pseudo_grad, global_fragment, outer_momentum):
    momentum = NESTEROV * outer_momentum + pseudo_grad
    return global_fragment - OUTER_RATE * (pseudo_grad + NESTEROV * momentum), momentum


def last_kernel(
    workers,
    counts,
    fragment,
    params,
    first,
    second,
    global_fragment,
    outer_momentum,
    drift_sum,
    kept,
    come,
    near,
    *refs,
):
    far, (new_params, new_first, new_second, new_global, new_momentum, *held), sems = refs[:2], refs[2:-1], refs[-1]
    held_params, held_first, held_second, held_global, held_momentum = held
    live = counts[lax.axis_index("worker")].astype(jnp.float32)
    total = counts[0]
    for other in range(1, workers):
        total = total + counts[other]
    fresh, momentum = outer(drift_sum[...] / total.astype(jnp.float32), global_fragment[...], outer_momentum[...])
    held_global[...] = fresh
    held_momentum[...] = momentum
    copies = [
        pltpu.make_async_copy(held_global, new_global, sems.at[0]),
        pltpu.make_async_copy(held_momentum, new_momentum, sems.at[1]),
    ]
    for copy in copies:
        copy.start()
    half = kept.shape[2]
    group = LANES // FRAGS
    for number, at in enumerate(range(0, params.shape[1], LANES)):
        which, lanes = at // half, pl.ds(at % half, LANES)
        here = pl.ds(at, LANES)
        summed = kept[which, :, lanes] + come[which, :, lanes] + near[which, :, lanes] + far[which][0, :, lanes]
        gradient = summed.T / live
        inner, held_first[here, :], held_second[here, :] = adam(
            params[0, here, :], first[0, here, :], second[0, here, :], gradient
        )
        held_params[here, :] = inner
        mine = pl.ds(at + fragment[0], group, stride=FRAGS)
        piece = held_global[pl.ds(number * group, group), :]
        held_params[mine, :] = MIXING * piece + (1.0 - MIXING) * held_params[mine, :]
        for slot, (source, target) in enumerate(
            ((held_first, new_first), (held_second, new_second), (held_params, new_params))
        ):
            copies.append(
                pltpu.make_async_copy(source.at[here], target.at[0, here], sems.at[2 + 3 * number + slot])
            )
            copies[-1].start()
    for copy in copies:
        copy.wait()


def hop(value, axis, devices, bit):
    return lax.ppermute(value, axis, [(d, d ^ bit) for d in range(devices)])


def doubling_sum(value, axis, devices):
    bit = devices // 2
    while bit:
        value = value + hop(value, axis, devices, bit)
        bit //= 2
    return value


def fast_body(mesh):
    workers, devices = mesh.shape["worker"], mesh.shape["fsdp"]

    def body(
        params, first, second, global_fragment, outer_momentum, features, cotangent, token_counts, fragment_index
    ):
        rows, width = params.shape[1:]
        pieces, tokens = global_fragment.shape[0], features.shape[1]
        block = functools.partial(jax.ShapeDtypeStruct, dtype=jnp.float32)
        halves = lambda count: block((2 * count, width, rows // 2))

        def cost(count):
            return pl.CostEstimate(
                flops=2 * count * tokens * rows * width,
                bytes_accessed=count * rows * (2 * tokens + 4 * width),
                transcendentals=0,
            )

        room = pltpu.CompilerParams(vmem_limit_bytes=ROOM)
        away_far, kept_far = pl.pallas_call(
            functools.partial(first_kernel, (7, 6)),
            out_shape=[halves(1)] * 2,
            in_specs=[HBM] * 3,
            out_specs=[VMEM] * 2,
            scratch_shapes=[
                pltpu.SMEM(token_counts.shape, token_counts.dtype),
                pltpu.VMEM(cotangent.shape, cotangent.dtype),
                pltpu.VMEM((2, tokens, rows), features.dtype),
                pltpu.SemaphoreType.DMA((4,)),
            ],
            compiler_params=room,
            cost_estimate=cost(2),
        )(token_counts, cotangent, features)
        come_far = hop(away_far, "fsdp", devices, 1)
        away, kept, drift = pl.pallas_call(
            functools.partial(rest_kernel, (5, 4, 3, 2, 1, 0)),
            out_shape=[halves(3)] * 2 + [block((pieces, width))],
            in_specs=[SMEM, SMEM, VMEM, VMEM, VMEM, VMEM, ANY],
            out_specs=[VMEM] * 3,
            compiler_params=room,
            cost_estimate=cost(6),
        )(token_counts, fragment_index, cotangent, params, global_fragment, features, kept_far)
        come = hop(away, "fsdp", devices, 1)
        far = [hop(kept_far[h : h + 1] + come_far[h : h + 1], "fsdp", devices, 2) for h in (0, 1)]
        near, pass_on = lax.optimization_barrier((kept[2:4] + come[2:4], kept[4:6] + come[4:6]))
        near = hop(near, "fsdp", devices, 2)
        far = [hop(pass_on[h : h + 1] + far[h], "fsdp", devices, 4) for h in (0, 1)]
        drift_sum = doubling_sum(drift, "worker", workers)
        state = block(params.shape)
        piece = block(global_fragment.shape)
        return pl.pallas_call(
            functools.partial(last_kernel, workers),
            out_shape=[state] * 3 + [piece] * 2,
            in_specs=[SMEM] * 2 + [VMEM] * 11,
            out_specs=[HBM] * 5,
            scratch_shapes=[pltpu.VMEM((rows, width), jnp.float32)] * 3
            + [pltpu.VMEM((pieces, width), jnp.float32)] * 2
            + [pltpu.SemaphoreType.DMA((2 + 3 * rows // LANES,))],
            compiler_params=room,
            cost_estimate=pl.CostEstimate(
                flops=30 * rows * width, bytes_accessed=40 * rows * width, transcendentals=2 * rows * width
            ),
        )(
            token_counts,
            fragment_index,
            params,
            first,
            second,
            global_fragment,
            outer_momentum,
            drift_sum,
            kept,
            come,
            near,
            *far,
        )

    return body


def plain_body(mesh):
    workers, devices = mesh.shape["worker"], mesh.shape["fsdp"]

    def body(
        params, first, second, global_fragment, outer_momentum, features, cotangent, token_counts, fragment_index
    ):
        rows, width = params.shape[1:]
        tokens = features.shape[1]
        me = lax.axis_index("fsdp")
        count = lax.dynamic_index_in_dim(token_counts, lax.axis_index("worker"), 0, keepdims=False)
        live = count.astype(jnp.float32)
        valid = (me * tokens + lax.iota(jnp.int32, tokens) < count)[:, None]
        masked = jnp.where(valid, cotangent[0], jnp.zeros_like(cotangent[0]))
        term = lax.dot_general(features[0], masked, (((0,), (0,)), ((), ())), preferred_element_type=jnp.float32)
        blocks = jnp.take(term.reshape(devices, rows, width), me ^ jnp.arange(devices, dtype=jnp.int32), axis=0)
        bit = 1
        while bit < devices:
            blocks = blocks.reshape(-1, 2, rows, width)
            blocks = blocks[:, 0] + hop(blocks[:, 1], "fsdp", devices, bit)
            bit *= 2
        gradient = blocks[0] / live
        grouped = (rows // FRAGS, FRAGS, width)
        old = lax.dynamic_index_in_dim(params[0].reshape(grouped), fragment_index[0], 1, keepdims=False)
        drift_sum = doubling_sum(live * (global_fragment - old), "worker", workers)
        total = jnp.sum(token_counts).astype(jnp.float32)
        fresh, momentum = outer(drift_sum / total, global_fragment, outer_momentum)
        inner, first_new, second_new = adam(params[0], first[0], second[0], gradient)
        inner = inner.reshape(grouped)
        piece = lax.dynamic_index_in_dim(inner, fragment_index[0], 1, keepdims=False)
        mixed = MIXING * fresh + (1.0 - MIXING) * piece
        merged = lax.dynamic_update_index_in_dim(inner, mixed, fragment_index[0], 1).reshape(rows, width)
        return merged[None], first_new[None], second_new[None], fresh, momentum

    return body


def solution(mesh):
    devices = mesh.shape["fsdp"]

    def pick(*arrays):
        rows = arrays[0].shape[1]
        body = fast_body(mesh) if devices == 8 and rows % LANES == 0 else plain_body(mesh)
        return body(*arrays)

    state = P("worker", "fsdp", None)
    piece = P("fsdp", None)
    return jax.shard_map(
        pick,
        mesh=mesh,
        in_specs=(state, state, state, piece, piece, state, state, P(), P()),
        out_specs=(state, state, state, piece, piece),
        check_vma=False,
    )
```

```python
import functools

import jax
import jax.numpy as jnp
from jax import lax
from jax.experimental import pallas as pl
from jax.experimental.pallas import tpu as pltpu
from jax.sharding import PartitionSpec as P

FRAGS = 4
LANES = 128

BETA_ONE = 0.9
BETA_TWO = 0.95
CORRECT_ONE = 0.6513216
CORRECT_TWO = 0.401263
ADAM_EPS = 1e-08
LEARN_RATE = 0.02
DECAY_RATE = 0.1
NESTEROV = 0.9
OUTER_RATE = 0.7
MIXING = 0.5

VMEM = pl.BlockSpec(memory_space=pltpu.VMEM)
SMEM = pl.BlockSpec(memory_space=pltpu.SMEM)
HBM = pl.BlockSpec(memory_space=pltpu.HBM)
ANY = pl.BlockSpec(memory_space=pl.ANY)
ROOM = 8 << 20


def masked_rows(live, cotangent):
    rows = lax.broadcasted_iota(jnp.int32, cotangent.shape, 0)
    return jnp.where(rows < live, cotangent.astype(jnp.float32), 0.0).astype(jnp.bfloat16)


def columns_of(relative, rows):
    return pl.ds(pl.multiple_of((lax.axis_index("fsdp") ^ relative) * rows, LANES), rows)


def product_halves(masked, features):
    value = lax.dot_general(masked, features, (((0,), (0,)), ((), ())), preferred_element_type=jnp.float32)
    half = value.shape[1] // 2
    return value[:, :half], value[:, half:]


def product_kernel(
    order,
    counts,
    cotangent,
    features,
    away_far,
    kept_far,
    away,
    kept,
    masked,
    counts_held,
    cot_held,
    held,
    sems,
):
    targets = [(away_far, 0), (kept_far, 0)]
    targets += [((away if q & 1 else kept), 2 * (q // 2)) for q in order[2:]]
    small = [
        pltpu.make_async_copy(counts, counts_held, sems.at[0]),
        pltpu.make_async_copy(cotangent, cot_held, sems.at[1]),
    ]
    blocks = [
        pltpu.make_async_copy(features.at[0, :, columns_of(q, held.shape[2])], held.at[slot], sems.at[2 + slot])
        for slot, q in enumerate(order)
    ]
    for copy in small + blocks:
        copy.start()
    for copy in small:
        copy.wait()
    tokens = cot_held.shape[1]
    live = counts_held[lax.axis_index("worker")] - lax.axis_index("fsdp") * tokens
    masked[...] = masked_rows(live, cot_held[0])
    for slot, q in enumerate(order):
        blocks[slot].wait()
        into, at = targets[slot]
        into[at], into[at + 1] = product_halves(masked[...], held[slot])


def drift_kernel(counts, fragment, params, global_fragment, after, drift, inverse, *held_and_sems):
    del after
    held, sems = held_and_sems[:-1], held_and_sems[-1]
    copies = [
        pltpu.make_async_copy(source, target, sems.at[slot])
        for slot, (source, target) in enumerate(zip((counts, fragment, params, global_fragment), held))
    ]
    for copy in copies:
        copy.start()
    for copy in copies:
        copy.wait()
    counts_held, fragment_held, params_held, global_held = held
    count = counts_held[lax.axis_index("worker")].astype(jnp.float32)
    old = params_held[0, pl.ds(fragment_held[0], drift.shape[0], stride=FRAGS), :]
    drift[...] = count * (global_held[...] - old)
    inverse[...] = jnp.ones_like(inverse) / count


def add_kernel(picks, *refs):
    total = None
    for ref, pick in zip(refs, picks):
        if pick is not None:
            total = ref[pick] if total is None else total + ref[pick]
    refs[-1][...] = total


def outer_kernel(
    workers,
    counts,
    fragment,
    global_fragment,
    outer_momentum,
    drift_sum,
    new_global,
    new_momentum,
    scale,
    mix,
    *held_and_sems,
):
    held, sems = held_and_sems[:-1], held_and_sems[-1]
    copies = [
        pltpu.make_async_copy(source, target, sems.at[slot])
        for slot, (source, target) in enumerate(zip((counts, fragment, global_fragment, outer_momentum), held))
    ]
    for copy in copies:
        copy.start()
    scale[...] = jnp.ones_like(scale)
    mix[...] = jnp.zeros_like(mix)
    for copy in copies:
        copy.wait()
    counts_held, fragment_held, global_held, momentum_held = held
    total = counts_held[0]
    for other in range(1, workers):
        total = total + counts_held[other]
    fresh, momentum = outer(drift_sum[...] / total.astype(jnp.float32), global_held[...], momentum_held[...])
    new_global[...] = fresh
    new_momentum[...] = momentum
    mine = pl.ds(fragment_held[0], fresh.shape[0], stride=FRAGS)
    mix[mine, :] = MIXING * fresh
    scale[mine, :] = jnp.full_like(fresh, 1.0 - MIXING)


def adam(before, first, second, gradient):
    first_new = BETA_ONE * first + (1.0 - BETA_ONE) * gradient
    second_new = BETA_TWO * second + (1.0 - BETA_TWO) * gradient * gradient
    update = first_new * (1.0 / CORRECT_ONE) / (jnp.sqrt(second_new * (1.0 / CORRECT_TWO)) + ADAM_EPS)
    return before - LEARN_RATE * (update + DECAY_RATE * before), first_new, second_new


def outer(pseudo_grad, global_fragment, outer_momentum):
    momentum = NESTEROV * outer_momentum + pseudo_grad
    return global_fragment - OUTER_RATE * (pseudo_grad + NESTEROV * momentum), momentum


def half_step(half, states, sums, inverse, held):
    params, first, second = states
    kept, come, far, near = sums
    held_first, held_second = held
    rows = kept.shape[2]
    for lane in range(0, rows, LANES):
        lanes, there = pl.ds(lane, LANES), pl.ds(half * rows + lane, LANES)
        summed = kept[half, :, lanes] + come[half, :, lanes] + near[0, :, lanes] + far[0, :, lanes]
        inner, held_first[lanes, :], held_second[lanes, :] = adam(
            params[0, there, :], first[0, there, :], second[0, there, :], summed.T * inverse[0:1, :]
        )
        yield lanes, there, inner


def left_kernel(
    params, first, second, kept, come, far, near, inverse, inner, new_first, new_second, held_first, held_second, sems
):
    copies = []
    for lanes, there, value in half_step(
        0, (params, first, second), (kept, come, far, near), inverse, (held_first, held_second)
    ):
        inner[lanes, :] = value
        for source, target in ((held_first, new_first), (held_second, new_second)):
            copies.append(pltpu.make_async_copy(source.at[lanes], target.at[0, there], sems.at[len(copies)]))
            copies[-1].start()
    for copy in copies:
        copy.wait()


def right_kernel(
    params,
    first,
    second,
    kept,
    come,
    far,
    near,
    inverse,
    scale,
    mix,
    inner,
    left_first,
    left_second,
    new_params,
    new_first,
    new_second,
    held_left,
    held_right,
    held_first,
    held_second,
    sems,
):
    del left_first, left_second
    left = pl.ds(0, inner.shape[0])
    held_left[...] = scale[left, :] * inner[...] + mix[left, :]
    copies = [pltpu.make_async_copy(held_left, new_params.at[0, left], sems.at[0])]
    copies[-1].start()
    for lanes, there, value in half_step(
        1, (params, first, second), (kept, come, far, near), inverse, (held_first, held_second)
    ):
        held_right[lanes, :] = scale[there, :] * value + mix[there, :]
        for source, target in ((held_first, new_first), (held_second, new_second), (held_right, new_params)):
            copies.append(pltpu.make_async_copy(source.at[lanes], target.at[0, there], sems.at[len(copies)]))
            copies[-1].start()
    for copy in copies:
        copy.wait()


def hop(value, axis, devices, bit):
    return lax.ppermute(value, axis, [(d, d ^ bit) for d in range(devices)])


def doubling_sum(value, axis, devices):
    bit = devices // 2
    while bit:
        value = value + hop(value, axis, devices, bit)
        bit //= 2
    return value


def fast_body(mesh):
    workers, devices = mesh.shape["worker"], mesh.shape["fsdp"]

    def body(
        params, first, second, global_fragment, outer_momentum, features, cotangent, token_counts, fragment_index
    ):
        rows, width = params.shape[1:]
        pieces, tokens = global_fragment.shape[0], features.shape[1]
        block = functools.partial(jax.ShapeDtypeStruct, dtype=jnp.float32)
        halves = lambda count: block((2 * count, width, rows // 2))

        def cost(count):
            return pl.CostEstimate(
                flops=2 * count * tokens * rows * width,
                bytes_accessed=count * rows * (2 * tokens + 4 * width),
                transcendentals=0,
            )

        room = pltpu.CompilerParams(vmem_limit_bytes=ROOM)
        free = pl.CostEstimate(flops=0, bytes_accessed=0, transcendentals=0)
        far_fragment = fragment_index
        far_counts, far_features, far_cotangent, far_params, far_global, far_momentum = (
            pltpu.with_memory_space_constraint(array, pltpu.HBM)
            for array in (
                token_counts,
                features,
                cotangent,
                params,
                global_fragment,
                outer_momentum,
            )
        )
        held_counts = pltpu.SMEM(token_counts.shape, token_counts.dtype)
        held_fragment = pltpu.SMEM(fragment_index.shape, fragment_index.dtype)
        held_piece = pltpu.VMEM(global_fragment.shape, global_fragment.dtype)

        order = tuple(q + s for q in range(devices - 2, -1, -2) for s in (1, 0))
        away_far, kept_far, away, kept = pl.pallas_call(
            functools.partial(product_kernel, order),
            out_shape=[halves(1)] * 2 + [halves(devices // 2 - 1)] * 2,
            in_specs=[HBM] * 3,
            out_specs=[VMEM] * 4,
            scratch_shapes=[
                pltpu.VMEM((tokens, width), jnp.bfloat16),
                held_counts,
                pltpu.VMEM(cotangent.shape, cotangent.dtype),
                pltpu.VMEM((devices, tokens, rows), features.dtype),
                pltpu.SemaphoreType.DMA((2 + devices,)),
            ],
            compiler_params=room,
            cost_estimate=cost(devices),
        )(far_counts, far_cotangent, far_features)

        def add(*terms):
            picks = [pick for _, pick in terms]
            return pl.pallas_call(
                functools.partial(add_kernel, picks),
                out_shape=block((1, width, rows // 2)),
                in_specs=[ANY if pick is None else VMEM for pick in picks],
                out_specs=VMEM,
                compiler_params=room,
                cost_estimate=free,
            )(*(array for array, _ in terms))

        def part(number):
            return slice(number, number + 1)

        come_far = hop(away_far, "fsdp", devices, 1)
        sent = add((kept_far, part(0)), (come_far, part(0)), (far_fragment, None))
        far_left = hop(sent, "fsdp", devices, 2)
        away, _ = lax.optimization_barrier((away, sent))
        come = hop(away, "fsdp", devices, 1)
        drift, inverse = pl.pallas_call(
            drift_kernel,
            out_shape=[block((pieces, width)), block((8, width))],
            in_specs=[HBM] * 4 + [ANY],
            out_specs=[VMEM] * 2,
            scratch_shapes=[
                held_counts,
                held_fragment,
                pltpu.VMEM(params.shape, params.dtype),
                held_piece,
                pltpu.SemaphoreType.DMA((4,)),
            ],
            compiler_params=room,
            cost_estimate=free,
        )(far_counts, far_fragment, far_params, far_global, sent)
        sent = add((kept_far, part(1)), (come_far, part(1)), (drift, None))
        far_right = hop(sent, "fsdp", devices, 2)
        passed = add((kept, part(4)), (come, part(4)), (far_left, part(0)))
        far_left = hop(passed, "fsdp", devices, 4)
        near_left = add((kept, part(2)), (come, part(2)), (passed, None))
        far_right = add((kept, part(5)), (come, part(5)), (far_right, part(0)), (near_left, None))
        near_right = add((kept, part(3)), (come, part(3)), (far_right, None))
        drift, _ = lax.optimization_barrier((drift, sent))
        bit = workers // 2
        while bit:
            drift = drift + hop(drift, "worker", workers, bit)
            drift, _ = lax.optimization_barrier((drift, near_right))
            bit //= 2
        near_left = hop(near_left, "fsdp", devices, 2)
        far_right = hop(far_right, "fsdp", devices, 4)
        near_right = hop(near_right, "fsdp", devices, 2)
        state = block(params.shape)
        piece = block(global_fragment.shape)
        whole = block((rows, width))
        new_global, new_momentum, scale, mix = pl.pallas_call(
            functools.partial(outer_kernel, workers),
            out_shape=[piece, piece, whole, whole],
            in_specs=[HBM] * 4 + [VMEM],
            out_specs=[VMEM] * 4,
            scratch_shapes=[held_counts, held_fragment, held_piece, held_piece, pltpu.SemaphoreType.DMA((4,))],
            compiler_params=room,
            cost_estimate=free,
        )(far_counts, far_fragment, far_global, far_momentum, drift)
        half = rows // 2
        groups = half // LANES
        held_half = pltpu.VMEM((half, width), jnp.float32)
        inner, new_first, new_second = pl.pallas_call(
            left_kernel,
            out_shape=[block((half, width)), state, state],
            in_specs=[VMEM] * 8,
            out_specs=[VMEM, HBM, HBM],
            scratch_shapes=[held_half] * 2 + [pltpu.SemaphoreType.DMA((2 * groups,))],
            compiler_params=room,
            cost_estimate=pl.CostEstimate(
                flops=30 * half * width, bytes_accessed=40 * half * width, transcendentals=2 * half * width
            ),
        )(params, first, second, kept, come, far_left, near_left, inverse)
        new_params, new_first, new_second = pl.pallas_call(
            right_kernel,
            out_shape=[state] * 3,
            in_specs=[VMEM] * 11 + [HBM] * 2,
            out_specs=[HBM] * 3,
            input_output_aliases={11: 1, 12: 2},
            scratch_shapes=[held_half] * 4 + [pltpu.SemaphoreType.DMA((1 + 3 * groups,))],
            compiler_params=room,
            cost_estimate=free,
        )(params, first, second, kept, come, far_right, near_right, inverse, scale, mix, inner, new_first, new_second)
        return new_params, new_first, new_second, new_global, new_momentum

    return body


def plain_body(mesh):
    workers, devices = mesh.shape["worker"], mesh.shape["fsdp"]

    def body(
        params, first, second, global_fragment, outer_momentum, features, cotangent, token_counts, fragment_index
    ):
        rows, width = params.shape[1:]
        tokens = features.shape[1]
        me = lax.axis_index("fsdp")
        count = lax.dynamic_index_in_dim(token_counts, lax.axis_index("worker"), 0, keepdims=False)
        live = count.astype(jnp.float32)
        valid = (me * tokens + lax.iota(jnp.int32, tokens) < count)[:, None]
        masked = jnp.where(valid, cotangent[0], jnp.zeros_like(cotangent[0]))
        term = lax.dot_general(features[0], masked, (((0,), (0,)), ((), ())), preferred_element_type=jnp.float32)
        blocks = jnp.take(term.reshape(devices, rows, width), me ^ jnp.arange(devices, dtype=jnp.int32), axis=0)
        bit = 1
        while bit < devices:
            blocks = blocks.reshape(-1, 2, rows, width)
            blocks = blocks[:, 0] + hop(blocks[:, 1], "fsdp", devices, bit)
            bit *= 2
        gradient = blocks[0] / live
        grouped = (rows // FRAGS, FRAGS, width)
        old = lax.dynamic_index_in_dim(params[0].reshape(grouped), fragment_index[0], 1, keepdims=False)
        drift_sum = doubling_sum(live * (global_fragment - old), "worker", workers)
        total = jnp.sum(token_counts).astype(jnp.float32)
        fresh, momentum = outer(drift_sum / total, global_fragment, outer_momentum)
        inner, first_new, second_new = adam(params[0], first[0], second[0], gradient)
        inner = inner.reshape(grouped)
        piece = lax.dynamic_index_in_dim(inner, fragment_index[0], 1, keepdims=False)
        mixed = MIXING * fresh + (1.0 - MIXING) * piece
        merged = lax.dynamic_update_index_in_dim(inner, mixed, fragment_index[0], 1).reshape(rows, width)
        return merged[None], first_new[None], second_new[None], fresh, momentum

    return body


def solution(mesh):
    devices = mesh.shape["fsdp"]

    def pick(*arrays):
        rows = arrays[0].shape[1]
        body = fast_body(mesh) if devices == 8 and rows % LANES == 0 else plain_body(mesh)
        return body(*arrays)

    state = P("worker", "fsdp", None)
    piece = P("fsdp", None)
    return jax.shard_map(
        pick,
        mesh=mesh,
        in_specs=(state, state, state, piece, piece, state, state, P(), P()),
        out_specs=(state, state, state, piece, piece),
        check_vma=False,
    )
```

```python
import functools

import jax
import jax.numpy as jnp
from jax import lax
from jax.experimental import pallas as pl
from jax.experimental.pallas import tpu as pltpu
from jax.sharding import PartitionSpec as P

FRAGS = 4
LANES = 128

BETA_ONE = 0.9
BETA_TWO = 0.95
CORRECT_ONE = 0.6513216
CORRECT_TWO = 0.401263
ADAM_EPS = 1e-08
LEARN_RATE = 0.02
DECAY_RATE = 0.1
NESTEROV = 0.9
OUTER_RATE = 0.7
MIXING = 0.5

VMEM = pl.BlockSpec(memory_space=pltpu.VMEM)
SMEM = pl.BlockSpec(memory_space=pltpu.SMEM)
HBM = pl.BlockSpec(memory_space=pltpu.HBM)
ANY = pl.BlockSpec(memory_space=pl.ANY)
ROOM = 8 << 20


def masked_rows(live, cotangent):
    rows = lax.broadcasted_iota(jnp.int32, cotangent.shape, 0)
    return jnp.where(rows < live, cotangent.astype(jnp.float32), 0.0).astype(jnp.bfloat16)


def columns_of(relative, rows):
    return pl.ds(pl.multiple_of((lax.axis_index("fsdp") ^ relative) * rows, LANES), rows)


def product_halves(masked, features):
    value = lax.dot_general(masked, features, (((0,), (0,)), ((), ())), preferred_element_type=jnp.float32)
    half = value.shape[1] // 2
    return value[:, :half], value[:, half:]


def fetch(sources, targets, sems, start=0):
    copies = [
        pltpu.make_async_copy(source, target, sems.at[start + slot])
        for slot, (source, target) in enumerate(zip(sources, targets))
    ]
    for copy in copies:
        copy.start()
    return copies


def fetch_blocks(order, features, held, sems, start):
    rows = held.shape[2]
    sources = [features.at[0, :, columns_of(q, rows)] for q in order]
    return fetch(sources, [held.at[slot] for slot in range(len(order))], sems, start)


def first_kernel(order, counts, cotangent, features, away, kept, masked, counts_held, cot_held, held, sems):
    small = fetch((counts, cotangent), (counts_held, cot_held), sems)
    blocks = fetch_blocks(order, features, held, sems, len(small))
    for copy in small:
        copy.wait()
    tokens = cot_held.shape[1]
    live = counts_held[lax.axis_index("worker")] - lax.axis_index("fsdp") * tokens
    masked[...] = masked_rows(live, cot_held[0])
    for block, slot, into in zip(blocks, range(len(order)), (away, kept)):
        block.wait()
        into[0], into[1] = product_halves(masked[...], held[slot])


def rest_kernel(order, masked, features, away_pass, kept_pass, away, kept):
    targets = ((away_pass, 0), (kept_pass, 0), (away, 2), (kept, 2), (away, 0), (kept, 0))
    for q, (into, at) in zip(order, targets):
        columns = columns_of(q, 2 * kept.shape[2])
        into[at], into[at + 1] = product_halves(masked[...], features[0, :, columns])


def drift_kernel(counts, fragment, params, global_fragment, after, drift, inverse, *held_and_sems):
    del after
    held, sems = held_and_sems[:-1], held_and_sems[-1]
    copies = [
        pltpu.make_async_copy(source, target, sems.at[slot])
        for slot, (source, target) in enumerate(zip((counts, fragment, params, global_fragment), held))
    ]
    for copy in copies:
        copy.start()
    for copy in copies:
        copy.wait()
    counts_held, fragment_held, params_held, global_held = held
    count = counts_held[lax.axis_index("worker")].astype(jnp.float32)
    old = params_held[0, pl.ds(fragment_held[0], drift.shape[0], stride=FRAGS), :]
    drift[...] = count * (global_held[...] - old)
    inverse[...] = jnp.ones_like(inverse) / count


def add_kernel(picks, *refs):
    total = None
    for ref, pick in zip(refs, picks):
        if pick is not None:
            total = ref[pick] if total is None else total + ref[pick]
    refs[-1][...] = total


def outer_kernel(
    workers,
    counts,
    fragment,
    global_fragment,
    outer_momentum,
    drift_sum,
    new_global,
    new_momentum,
    scale,
    mix,
    *held_and_sems,
):
    held, sems = held_and_sems[:-1], held_and_sems[-1]
    copies = [
        pltpu.make_async_copy(source, target, sems.at[slot])
        for slot, (source, target) in enumerate(zip((counts, fragment, global_fragment, outer_momentum), held))
    ]
    for copy in copies:
        copy.start()
    scale[...] = jnp.ones_like(scale)
    mix[...] = jnp.zeros_like(mix)
    for copy in copies:
        copy.wait()
    counts_held, fragment_held, global_held, momentum_held = held
    total = counts_held[0]
    for other in range(1, workers):
        total = total + counts_held[other]
    fresh, momentum = outer(drift_sum[...] / total.astype(jnp.float32), global_held[...], momentum_held[...])
    new_global[...] = fresh
    new_momentum[...] = momentum
    mine = pl.ds(fragment_held[0], fresh.shape[0], stride=FRAGS)
    mix[mine, :] = MIXING * fresh
    scale[mine, :] = jnp.full_like(fresh, 1.0 - MIXING)


def adam(before, first, second, gradient):
    first_new = BETA_ONE * first + (1.0 - BETA_ONE) * gradient
    second_new = BETA_TWO * second + (1.0 - BETA_TWO) * gradient * gradient
    update = first_new * (1.0 / CORRECT_ONE) / (jnp.sqrt(second_new * (1.0 / CORRECT_TWO)) + ADAM_EPS)
    return before - LEARN_RATE * (update + DECAY_RATE * before), first_new, second_new


def outer(pseudo_grad, global_fragment, outer_momentum):
    momentum = NESTEROV * outer_momentum + pseudo_grad
    return global_fragment - OUTER_RATE * (pseudo_grad + NESTEROV * momentum), momentum


def half_step(half, states, sums, inverse, held):
    params, first, second = states
    kept, come, far, near = sums
    held_first, held_second = held
    rows = kept.shape[2]
    for lane in range(0, rows, LANES):
        lanes, there = pl.ds(lane, LANES), pl.ds(half * rows + lane, LANES)
        summed = kept[half, :, lanes] + come[half, :, lanes] + near[0, :, lanes] + far[0, :, lanes]
        inner, held_first[lanes, :], held_second[lanes, :] = adam(
            params[0, there, :], first[0, there, :], second[0, there, :], summed.T * inverse[0:1, :]
        )
        yield lanes, there, inner


def left_kernel(
    params, first, second, kept, come, far, near, inverse, inner, new_first, new_second, held_first, held_second, sems
):
    copies = []
    for lanes, there, value in half_step(
        0, (params, first, second), (kept, come, far, near), inverse, (held_first, held_second)
    ):
        inner[lanes, :] = value
        for source, target in ((held_first, new_first), (held_second, new_second)):
            copies.append(pltpu.make_async_copy(source.at[lanes], target.at[0, there], sems.at[len(copies)]))
            copies[-1].start()
    for copy in copies:
        copy.wait()


def right_kernel(
    params,
    first,
    second,
    kept,
    come,
    far,
    near,
    inverse,
    scale,
    mix,
    inner,
    left_first,
    left_second,
    new_params,
    new_first,
    new_second,
    held_left,
    held_right,
    held_first,
    held_second,
    sems,
):
    del left_first, left_second
    left = pl.ds(0, inner.shape[0])
    held_left[...] = scale[left, :] * inner[...] + mix[left, :]
    copies = [pltpu.make_async_copy(held_left, new_params.at[0, left], sems.at[0])]
    copies[-1].start()
    for lanes, there, value in half_step(
        1, (params, first, second), (kept, come, far, near), inverse, (held_first, held_second)
    ):
        held_right[lanes, :] = scale[there, :] * value + mix[there, :]
        for source, target in ((held_first, new_first), (held_second, new_second), (held_right, new_params)):
            copies.append(pltpu.make_async_copy(source.at[lanes], target.at[0, there], sems.at[len(copies)]))
            copies[-1].start()
    for copy in copies:
        copy.wait()


def hop(value, axis, devices, bit):
    return lax.ppermute(value, axis, [(d, d ^ bit) for d in range(devices)])


def doubling_sum(value, axis, devices):
    bit = devices // 2
    while bit:
        value = value + hop(value, axis, devices, bit)
        bit //= 2
    return value


def fast_body(mesh):
    workers, devices = mesh.shape["worker"], mesh.shape["fsdp"]

    def body(
        params, first, second, global_fragment, outer_momentum, features, cotangent, token_counts, fragment_index
    ):
        rows, width = params.shape[1:]
        pieces, tokens = global_fragment.shape[0], features.shape[1]
        block = functools.partial(jax.ShapeDtypeStruct, dtype=jnp.float32)
        halves = lambda count: block((2 * count, width, rows // 2))

        def cost(count):
            return pl.CostEstimate(
                flops=2 * count * tokens * rows * width,
                bytes_accessed=count * rows * (2 * tokens + 4 * width),
                transcendentals=0,
            )

        room = pltpu.CompilerParams(vmem_limit_bytes=ROOM)
        free = pl.CostEstimate(flops=0, bytes_accessed=0, transcendentals=0)
        far_fragment = fragment_index
        far_counts, far_features, far_cotangent, far_params, far_global, far_momentum = (
            pltpu.with_memory_space_constraint(array, pltpu.HBM)
            for array in (
                token_counts,
                features,
                cotangent,
                params,
                global_fragment,
                outer_momentum,
            )
        )
        held_counts = pltpu.SMEM(token_counts.shape, token_counts.dtype)
        held_fragment = pltpu.SMEM(fragment_index.shape, fragment_index.dtype)
        held_piece = pltpu.VMEM(global_fragment.shape, global_fragment.dtype)

        away_far, kept_far, masked = pl.pallas_call(
            functools.partial(first_kernel, (7, 6)),
            out_shape=[halves(1)] * 2 + [jax.ShapeDtypeStruct((tokens, width), jnp.bfloat16)],
            in_specs=[HBM] * 3,
            out_specs=[VMEM] * 3,
            scratch_shapes=[
                held_counts,
                pltpu.VMEM(cotangent.shape, cotangent.dtype),
                pltpu.VMEM((2, tokens, rows), features.dtype),
                pltpu.SemaphoreType.DMA((4,)),
            ],
            compiler_params=room,
            cost_estimate=cost(2),
            name="far_products",
        )(far_counts, far_cotangent, far_features)
        away_pass, kept_pass, away, kept = pl.pallas_call(
            functools.partial(rest_kernel, (5, 4, 3, 2, 1, 0)),
            out_shape=[halves(1)] * 2 + [halves(2)] * 2,
            in_specs=[VMEM] * 2,
            out_specs=[VMEM] * 4,
            compiler_params=room,
            cost_estimate=free,
            name="rest_products",
        )(masked, features)

        def add(*terms, name):
            picks = [pick for _, pick in terms]
            return pl.pallas_call(
                functools.partial(add_kernel, picks),
                out_shape=block((1, width, rows // 2)),
                in_specs=[ANY if pick is None else VMEM for pick in picks],
                out_specs=VMEM,
                compiler_params=room,
                cost_estimate=free,
                name=name,
            )(*(array for array, _ in terms))

        def part(number):
            return slice(number, number + 1)

        come_far = hop(away_far, "fsdp", devices, 1)
        sent = add((kept_far, part(0)), (come_far, part(0)), (far_fragment, None), name="add_a1")
        far_left = hop(sent, "fsdp", devices, 2)
        away_pass, away, _ = lax.optimization_barrier((away_pass, away, sent))
        come_pass = hop(away_pass, "fsdp", devices, 1)
        come = hop(away, "fsdp", devices, 1)
        drift, inverse = pl.pallas_call(
            drift_kernel,
            name="drift",
            out_shape=[block((pieces, width)), block((8, width))],
            in_specs=[HBM] * 4 + [ANY],
            out_specs=[VMEM] * 2,
            scratch_shapes=[
                held_counts,
                held_fragment,
                pltpu.VMEM(params.shape, params.dtype),
                held_piece,
                pltpu.SemaphoreType.DMA((4,)),
            ],
            compiler_params=room,
            cost_estimate=free,
        )(far_counts, far_fragment, far_params, far_global, sent)
        sent = add((kept_far, part(1)), (come_far, part(1)), (drift, None), name="add_a2")
        far_right = hop(sent, "fsdp", devices, 2)
        passed = add((kept_pass, part(0)), (come_pass, part(0)), (far_left, part(0)), name="add_c1")
        far_left = hop(passed, "fsdp", devices, 4)
        near_left = add((kept, part(2)), (come, part(2)), (passed, None), name="add_n1")
        far_right = add((kept_pass, part(1)), (come_pass, part(1)), (far_right, part(0)), (passed, None), name="add_c2")
        near_right = add((kept, part(3)), (come, part(3)), (far_right, None), name="add_n2")
        drift, _ = lax.optimization_barrier((drift, sent))
        bit = workers // 2
        while bit:
            drift = drift + hop(drift, "worker", workers, bit)
            drift, _ = lax.optimization_barrier((drift, near_right))
            bit //= 2
        near_left = hop(near_left, "fsdp", devices, 2)
        far_right = hop(far_right, "fsdp", devices, 4)
        near_right = hop(near_right, "fsdp", devices, 2)
        state = block(params.shape)
        piece = block(global_fragment.shape)
        whole = block((rows, width))
        new_global, new_momentum, scale, mix = pl.pallas_call(
            functools.partial(outer_kernel, workers),
            name="outer_step",
            out_shape=[piece, piece, whole, whole],
            in_specs=[HBM] * 4 + [VMEM],
            out_specs=[VMEM] * 4,
            scratch_shapes=[held_counts, held_fragment, held_piece, held_piece, pltpu.SemaphoreType.DMA((4,))],
            compiler_params=room,
            cost_estimate=free,
        )(far_counts, far_fragment, far_global, far_momentum, drift)
        half = rows // 2
        groups = half // LANES
        held_half = pltpu.VMEM((half, width), jnp.float32)
        inner, new_first, new_second = pl.pallas_call(
            left_kernel,
            name="left_step",
            out_shape=[block((half, width)), state, state],
            in_specs=[VMEM] * 8,
            out_specs=[VMEM, HBM, HBM],
            scratch_shapes=[held_half] * 2 + [pltpu.SemaphoreType.DMA((2 * groups,))],
            compiler_params=room,
            cost_estimate=pl.CostEstimate(
                flops=30 * half * width, bytes_accessed=40 * half * width, transcendentals=2 * half * width
            ),
        )(params, first, second, kept, come, far_left, near_left, inverse)
        new_params, new_first, new_second = pl.pallas_call(
            right_kernel,
            name="right_step",
            out_shape=[state] * 3,
            in_specs=[VMEM] * 11 + [HBM] * 2,
            out_specs=[HBM] * 3,
            input_output_aliases={11: 1, 12: 2},
            scratch_shapes=[held_half] * 4 + [pltpu.SemaphoreType.DMA((1 + 3 * groups,))],
            compiler_params=room,
            cost_estimate=free,
        )(params, first, second, kept, come, far_right, near_right, inverse, scale, mix, inner, new_first, new_second)
        return new_params, new_first, new_second, new_global, new_momentum

    return body


def plain_body(mesh):
    workers, devices = mesh.shape["worker"], mesh.shape["fsdp"]

    def body(
        params, first, second, global_fragment, outer_momentum, features, cotangent, token_counts, fragment_index
    ):
        rows, width = params.shape[1:]
        tokens = features.shape[1]
        me = lax.axis_index("fsdp")
        count = lax.dynamic_index_in_dim(token_counts, lax.axis_index("worker"), 0, keepdims=False)
        live = count.astype(jnp.float32)
        valid = (me * tokens + lax.iota(jnp.int32, tokens) < count)[:, None]
        masked = jnp.where(valid, cotangent[0], jnp.zeros_like(cotangent[0]))
        term = lax.dot_general(features[0], masked, (((0,), (0,)), ((), ())), preferred_element_type=jnp.float32)
        blocks = jnp.take(term.reshape(devices, rows, width), me ^ jnp.arange(devices, dtype=jnp.int32), axis=0)
        bit = 1
        while bit < devices:
            blocks = blocks.reshape(-1, 2, rows, width)
            blocks = blocks[:, 0] + hop(blocks[:, 1], "fsdp", devices, bit)
            bit *= 2
        gradient = blocks[0] / live
        grouped = (rows // FRAGS, FRAGS, width)
        old = lax.dynamic_index_in_dim(params[0].reshape(grouped), fragment_index[0], 1, keepdims=False)
        drift_sum = doubling_sum(live * (global_fragment - old), "worker", workers)
        total = jnp.sum(token_counts).astype(jnp.float32)
        fresh, momentum = outer(drift_sum / total, global_fragment, outer_momentum)
        inner, first_new, second_new = adam(params[0], first[0], second[0], gradient)
        inner = inner.reshape(grouped)
        piece = lax.dynamic_index_in_dim(inner, fragment_index[0], 1, keepdims=False)
        mixed = MIXING * fresh + (1.0 - MIXING) * piece
        merged = lax.dynamic_update_index_in_dim(inner, mixed, fragment_index[0], 1).reshape(rows, width)
        return merged[None], first_new[None], second_new[None], fresh, momentum

    return body


def solution(mesh):
    devices = mesh.shape["fsdp"]

    def pick(*arrays):
        rows = arrays[0].shape[1]
        body = fast_body(mesh) if devices == 8 and rows % LANES == 0 else plain_body(mesh)
        return body(*arrays)

    state = P("worker", "fsdp", None)
    piece = P("fsdp", None)
    return jax.shard_map(
        pick,
        mesh=mesh,
        in_specs=(state, state, state, piece, piece, state, state, P(), P()),
        out_specs=(state, state, state, piece, piece),
        check_vma=False,
    )
```

```python
import functools

import jax
import jax.numpy as jnp
from jax import lax
from jax.experimental import pallas as pl
from jax.experimental.pallas import tpu as pltpu
from jax.sharding import PartitionSpec as P

FRAGS = 4
LANES = 128

BETA_ONE = 0.9
BETA_TWO = 0.95
CORRECT_ONE = 0.6513216
CORRECT_TWO = 0.401263
ADAM_EPS = 1e-08
LEARN_RATE = 0.02
DECAY_RATE = 0.1
NESTEROV = 0.9
OUTER_RATE = 0.7
MIXING = 0.5

VMEM = pl.BlockSpec(memory_space=pltpu.VMEM)
SMEM = pl.BlockSpec(memory_space=pltpu.SMEM)
HBM = pl.BlockSpec(memory_space=pltpu.HBM)
ANY = pl.BlockSpec(memory_space=pl.ANY)
ROOM = 8 << 20


def masked_rows(live, cotangent):
    rows = lax.broadcasted_iota(jnp.int32, cotangent.shape, 0)
    return jnp.where(rows < live, cotangent.astype(jnp.float32), 0.0).astype(jnp.bfloat16)


def columns_of(relative, rows, start, size):
    return pl.ds(pl.multiple_of((lax.axis_index("fsdp") ^ relative) * rows + start, LANES), size)


def product(masked, features):
    return lax.dot_general(masked, features, (((0,), (0,)), ((), ())), preferred_element_type=jnp.float32)


def fetch(sources, targets, sems, start=0):
    copies = [
        pltpu.make_async_copy(source, target, sems.at[start + slot])
        for slot, (source, target) in enumerate(zip(sources, targets))
    ]
    for copy in copies:
        copy.start()
    return copies


def first_kernel(order, counts, cotangent, features, away, kept, masked, counts_held, cot_held, held, sems):
    half = held.shape[2]
    small = fetch((counts, cotangent), (counts_held, cot_held), sems)
    columns = [columns_of(q, 2 * half, 0, half) for q in order]
    blocks = fetch([features.at[0, :, c] for c in columns], [held.at[n] for n in range(len(order))], sems, len(small))
    for copy in small:
        copy.wait()
    tokens = cot_held.shape[1]
    live = counts_held[lax.axis_index("worker")] - lax.axis_index("fsdp") * tokens
    masked[...] = masked_rows(live, cot_held[0])
    for slot, into in enumerate((away, kept)):
        blocks[slot].wait()
        into[0] = product(masked[...], held[slot])


def rest_kernel(masked, features, away_mid, kept_mid, away, kept):
    half = kept.shape[2]
    places = [(6, 1, 0), (4, 0, 1), (4, 1, 2), (2, 0, 3), (2, 1, 4), (0, 0, 0), (0, 1, 1)]
    for q, side, at in places:
        for core, into in ((1, away_mid if q else away), (0, kept_mid if q else kept)):
            into[at] = product(masked[...], features[0, :, columns_of(q + core, 2 * half, side * half, half)])


def drift_kernel(
    workers, counts, fragment, params, global_fragment, after, drift, scale, inverse, share, *held_and_sems
):
    del after
    held, sems = held_and_sems[:-1], held_and_sems[-1]
    copies = fetch((counts, fragment, params, global_fragment), held, sems)
    scale[...] = jnp.ones_like(scale)
    for copy in copies:
        copy.wait()
    counts_held, fragment_held, params_held, global_held = held
    mine = pl.ds(fragment_held[0], drift.shape[0], stride=FRAGS)
    count = counts_held[lax.axis_index("worker")].astype(jnp.float32)
    drift[...] = count * (global_held[...] - params_held[0, mine, :])
    scale[mine, :] = jnp.full_like(drift, 1.0 - MIXING)
    total = counts_held[0]
    for other in range(1, workers):
        total = total + counts_held[other]
    inverse[...] = jnp.ones_like(inverse) / count
    share[...] = jnp.ones_like(share) / total.astype(jnp.float32)


def add_kernel(picks, *refs):
    total = None
    for ref, pick in zip(refs, picks):
        if pick is not None:
            total = ref[pick] if total is None else total + ref[pick]
    refs[-1][...] = total


def adam(before, first, second, gradient):
    first_new = BETA_ONE * first + (1.0 - BETA_ONE) * gradient
    second_new = BETA_TWO * second + (1.0 - BETA_TWO) * gradient * gradient
    update = first_new * (1.0 / CORRECT_ONE) / (jnp.sqrt(second_new * (1.0 / CORRECT_TWO)) + ADAM_EPS)
    return before - LEARN_RATE * (update + DECAY_RATE * before), first_new, second_new


def outer(pseudo_grad, global_fragment, outer_momentum):
    momentum = NESTEROV * outer_momentum + pseudo_grad
    return global_fragment - OUTER_RATE * (pseudo_grad + NESTEROV * momentum), momentum


def half_step(half, states, sums, inverse, held):
    params, first, second = states
    kept, come, far, near = sums
    held_first, held_second = held
    rows = kept.shape[2]
    for lane in range(0, rows, LANES):
        lanes, there = pl.ds(lane, LANES), pl.ds(half * rows + lane, LANES)
        summed = kept[half, :, lanes] + come[half, :, lanes] + near[half, :, lanes] + far[0, :, lanes]
        inner, held_first[lanes, :], held_second[lanes, :] = adam(
            params[0, there, :], first[0, there, :], second[0, there, :], summed.T * inverse[0:1, :]
        )
        yield lanes, there, inner


def send(copies, sems, source, target):
    copies.append(pltpu.make_async_copy(source, target, sems.at[len(copies)]))
    copies[-1].start()


def left_kernel(
    params,
    first,
    second,
    kept,
    come,
    far,
    near,
    inverse,
    scale,
    share,
    global_fragment,
    outer_momentum,
    drift,
    other_drift,
    mix,
    new_params,
    new_first,
    new_second,
    new_global,
    new_momentum,
    held_params,
    held_first,
    held_second,
    held_global,
    held_momentum,
    spread,
    sems,
):
    copies = []
    fresh, momentum = outer((drift[...] + other_drift[...]) * share[0:1, :], global_fragment[...], outer_momentum[...])
    held_global[...] = fresh
    held_momentum[...] = momentum
    send(copies, sems, held_global, new_global)
    send(copies, sems, held_momentum, new_momentum)
    for at in range(FRAGS):
        spread[pl.ds(at, fresh.shape[0], stride=FRAGS), :] = fresh
    for lanes, there, value in half_step(
        0, (params, first, second), (kept, come, far, near), inverse, (held_first, held_second)
    ):
        held_params[lanes, :] = scale[there, :] * value + (1.0 - scale[there, :]) * spread[there, :]
        for source, target in ((held_first, new_first), (held_second, new_second), (held_params, new_params)):
            send(copies, sems, source.at[lanes], target.at[0, there])
    right = pl.ds(mix.shape[0], mix.shape[0])
    mix[...] = (1.0 - scale[right, :]) * spread[right, :]
    for copy in copies:
        copy.wait()


def right_kernel(
    params,
    first,
    second,
    kept,
    come,
    far,
    near,
    inverse,
    scale,
    mix,
    left_params,
    left_first,
    left_second,
    new_params,
    new_first,
    new_second,
    held_params,
    held_first,
    held_second,
    sems,
):
    del left_params, left_first, left_second
    copies = []
    for lanes, there, value in half_step(
        1, (params, first, second), (kept, come, far, near), inverse, (held_first, held_second)
    ):
        held_params[lanes, :] = scale[there, :] * value + mix[lanes, :]
        for source, target in ((held_first, new_first), (held_second, new_second), (held_params, new_params)):
            send(copies, sems, source.at[lanes], target.at[0, there])
    for copy in copies:
        copy.wait()


def hop(value, axis, devices, bit):
    return lax.ppermute(value, axis, [(d, d ^ bit) for d in range(devices)])


def doubling_sum(value, axis, devices):
    bit = devices // 2
    while bit:
        value = value + hop(value, axis, devices, bit)
        bit //= 2
    return value


def fast_body(mesh):
    workers, devices = mesh.shape["worker"], mesh.shape["fsdp"]

    def body(
        params, first, second, global_fragment, outer_momentum, features, cotangent, token_counts, fragment_index
    ):
        rows, width = params.shape[1:]
        pieces, tokens = global_fragment.shape[0], features.shape[1]
        block = functools.partial(jax.ShapeDtypeStruct, dtype=jnp.float32)

        def cost(count):
            return pl.CostEstimate(
                flops=2 * count * tokens * rows * width,
                bytes_accessed=count * rows * (2 * tokens + 4 * width),
                transcendentals=0,
            )

        room = pltpu.CompilerParams(vmem_limit_bytes=ROOM)
        free = pl.CostEstimate(flops=0, bytes_accessed=0, transcendentals=0)
        far_fragment = fragment_index
        far_counts, far_features, far_cotangent, far_params, far_global, far_momentum = (
            pltpu.with_memory_space_constraint(array, pltpu.HBM)
            for array in (
                token_counts,
                features,
                cotangent,
                params,
                global_fragment,
                outer_momentum,
            )
        )
        held_counts = pltpu.SMEM(token_counts.shape, token_counts.dtype)
        held_fragment = pltpu.SMEM(fragment_index.shape, fragment_index.dtype)
        held_piece = pltpu.VMEM(global_fragment.shape, global_fragment.dtype)

        half = rows // 2
        away_far, kept_far, masked = pl.pallas_call(
            functools.partial(first_kernel, (7, 6)),
            out_shape=[block((1, width, half))] * 2 + [jax.ShapeDtypeStruct((tokens, width), jnp.bfloat16)],
            in_specs=[HBM] * 3,
            out_specs=[VMEM] * 3,
            scratch_shapes=[
                held_counts,
                pltpu.VMEM(cotangent.shape, cotangent.dtype),
                pltpu.VMEM((2, tokens, half), features.dtype),
                pltpu.SemaphoreType.DMA((4,)),
            ],
            compiler_params=room,
            cost_estimate=cost(1),
            name="far_products",
        )(far_counts, far_cotangent, far_features)
        away_mid, kept_mid, away, kept = pl.pallas_call(
            rest_kernel,
            out_shape=[block((5, width, half))] * 2 + [block((2, width, half))] * 2,
            in_specs=[VMEM] * 2,
            out_specs=[VMEM] * 4,
            compiler_params=room,
            cost_estimate=free,
            name="rest_products",
        )(masked, features)

        def add(*terms, name, count=1):
            picks = [pick for _, pick in terms]
            return pl.pallas_call(
                functools.partial(add_kernel, picks),
                out_shape=block((count, width, half)),
                in_specs=[ANY if pick is None else VMEM for pick in picks],
                out_specs=VMEM,
                compiler_params=room,
                cost_estimate=free,
                name=name,
            )(*(array for array, _ in terms))

        def part(number, count=1):
            return slice(number, number + count)

        state, piece = block(params.shape), block(global_fragment.shape)
        come_far = hop(away_far, "fsdp", devices, 1)
        sent = add((kept_far, part(0)), (come_far, part(0)), (far_fragment, None), name="add_a1")
        far_left = hop(sent, "fsdp", devices, 2)
        away_mid, _ = lax.optimization_barrier((away_mid, sent))
        come_mid = hop(away_mid, "fsdp", devices, 1)
        drift, scale, inverse, share = pl.pallas_call(
            functools.partial(drift_kernel, workers),
            out_shape=[piece, block((rows, width)), block((8, width)), block((8, width))],
            in_specs=[HBM] * 4 + [ANY],
            out_specs=[VMEM] * 4,
            scratch_shapes=[
                held_counts,
                held_fragment,
                pltpu.VMEM(params.shape, params.dtype),
                held_piece,
                pltpu.SemaphoreType.DMA((4,)),
            ],
            compiler_params=room,
            cost_estimate=free,
            name="drift",
        )(far_counts, far_fragment, far_params, far_global, sent)
        sent = add((kept_mid, part(0)), (come_mid, part(0)), (drift, None), name="add_a2")
        far_right = hop(sent, "fsdp", devices, 2)
        near = add((kept_mid, part(3, 2)), (come_mid, part(3, 2)), (sent, None), name="add_n", count=2)
        near = hop(near, "fsdp", devices, 2)
        away, _ = lax.optimization_barrier((away, sent))
        come = hop(away, "fsdp", devices, 1)
        passed = add((kept_mid, part(1)), (come_mid, part(1)), (far_left, part(0)), name="add_c1")
        far_left = hop(passed, "fsdp", devices, 4)
        far_right = add((kept_mid, part(2)), (come_mid, part(2)), (far_right, part(0)), (passed, None), name="add_c2")
        drift, _ = lax.optimization_barrier((drift, sent))
        bit = workers // 2
        drifts = (drift, hop(drift, "worker", workers, bit))
        while bit > 1:
            bit //= 2
            drift = drifts[0] + drifts[1]
            drift, _ = lax.optimization_barrier((drift, far_right))
            drifts = (drift, hop(drift, "worker", workers, bit))
        far_right = hop(far_right, "fsdp", devices, 4)
        groups = half // LANES
        held_half = pltpu.VMEM((half, width), jnp.float32)
        mix, *results, new_global, new_momentum = pl.pallas_call(
            left_kernel,
            out_shape=[block((half, width)), state, state, state, piece, piece],
            in_specs=[VMEM] * 14,
            out_specs=[VMEM] + [HBM] * 5,
            scratch_shapes=[held_half] * 3
            + [held_piece] * 2
            + [pltpu.VMEM((rows, width), jnp.float32), pltpu.SemaphoreType.DMA((2 + 3 * groups,))],
            compiler_params=room,
            cost_estimate=pl.CostEstimate(
                flops=30 * half * width, bytes_accessed=40 * half * width, transcendentals=2 * half * width
            ),
            name="left_step",
        )(
            params,
            first,
            second,
            kept,
            come,
            far_left,
            near,
            inverse,
            scale,
            share,
            global_fragment,
            outer_momentum,
            *drifts,
        )
        new_params, new_first, new_second = pl.pallas_call(
            right_kernel,
            out_shape=[state] * 3,
            in_specs=[VMEM] * 10 + [HBM] * 3,
            out_specs=[HBM] * 3,
            input_output_aliases={10: 0, 11: 1, 12: 2},
            scratch_shapes=[held_half] * 3 + [pltpu.SemaphoreType.DMA((3 * groups,))],
            compiler_params=room,
            cost_estimate=free,
            name="right_step",
        )(params, first, second, kept, come, far_right, near, inverse, scale, mix, *results)
        return new_params, new_first, new_second, new_global, new_momentum

    return body


def plain_body(mesh):
    workers, devices = mesh.shape["worker"], mesh.shape["fsdp"]

    def body(
        params, first, second, global_fragment, outer_momentum, features, cotangent, token_counts, fragment_index
    ):
        rows, width = params.shape[1:]
        tokens = features.shape[1]
        me = lax.axis_index("fsdp")
        count = lax.dynamic_index_in_dim(token_counts, lax.axis_index("worker"), 0, keepdims=False)
        live = count.astype(jnp.float32)
        valid = (me * tokens + lax.iota(jnp.int32, tokens) < count)[:, None]
        masked = jnp.where(valid, cotangent[0], jnp.zeros_like(cotangent[0]))
        term = lax.dot_general(features[0], masked, (((0,), (0,)), ((), ())), preferred_element_type=jnp.float32)
        blocks = jnp.take(term.reshape(devices, rows, width), me ^ jnp.arange(devices, dtype=jnp.int32), axis=0)
        bit = 1
        while bit < devices:
            blocks = blocks.reshape(-1, 2, rows, width)
            blocks = blocks[:, 0] + hop(blocks[:, 1], "fsdp", devices, bit)
            bit *= 2
        gradient = blocks[0] / live
        grouped = (rows // FRAGS, FRAGS, width)
        old = lax.dynamic_index_in_dim(params[0].reshape(grouped), fragment_index[0], 1, keepdims=False)
        drift_sum = doubling_sum(live * (global_fragment - old), "worker", workers)
        total = jnp.sum(token_counts).astype(jnp.float32)
        fresh, momentum = outer(drift_sum / total, global_fragment, outer_momentum)
        inner, first_new, second_new = adam(params[0], first[0], second[0], gradient)
        inner = inner.reshape(grouped)
        piece = lax.dynamic_index_in_dim(inner, fragment_index[0], 1, keepdims=False)
        mixed = MIXING * fresh + (1.0 - MIXING) * piece
        merged = lax.dynamic_update_index_in_dim(inner, mixed, fragment_index[0], 1).reshape(rows, width)
        return merged[None], first_new[None], second_new[None], fresh, momentum

    return body


def solution(mesh):
    devices = mesh.shape["fsdp"]

    def pick(*arrays):
        rows = arrays[0].shape[1]
        body = fast_body(mesh) if devices == 8 and rows % LANES == 0 else plain_body(mesh)
        return body(*arrays)

    state = P("worker", "fsdp", None)
    piece = P("fsdp", None)
    return jax.shard_map(
        pick,
        mesh=mesh,
        in_specs=(state, state, state, piece, piece, state, state, P(), P()),
        out_specs=(state, state, state, piece, piece),
        check_vma=False,
    )
```

```python
import functools

import jax
import jax.numpy as jnp
from jax import lax
from jax.experimental import pallas as pl
from jax.experimental.pallas import tpu as pltpu
from jax.sharding import PartitionSpec as P

FRAGS = 4
LANES = 128

BETA_ONE = 0.9
BETA_TWO = 0.95
CORRECT_ONE = 0.6513216
CORRECT_TWO = 0.401263
ADAM_EPS = 1e-08
LEARN_RATE = 0.02
DECAY_RATE = 0.1
NESTEROV = 0.9
OUTER_RATE = 0.7
MIXING = 0.5

VMEM = pl.BlockSpec(memory_space=pltpu.VMEM)
SMEM = pl.BlockSpec(memory_space=pltpu.SMEM)
HBM = pl.BlockSpec(memory_space=pltpu.HBM)
ANY = pl.BlockSpec(memory_space=pl.ANY)
ROOM = 8 << 20


def masked_rows(live, cotangent):
    rows = lax.broadcasted_iota(jnp.int32, cotangent.shape, 0)
    return jnp.where(rows < live, cotangent.astype(jnp.float32), 0.0).astype(jnp.bfloat16)


def columns_of(relative, rows, start, size):
    return pl.ds(pl.multiple_of((lax.axis_index("fsdp") ^ relative) * rows + start, LANES), size)


def product(masked, features):
    return lax.dot_general(masked, features, (((0,), (0,)), ((), ())), preferred_element_type=jnp.float32)


def fetch(sources, targets, sems, start=0):
    copies = [
        pltpu.make_async_copy(source, target, sems.at[start + slot])
        for slot, (source, target) in enumerate(zip(sources, targets))
    ]
    for copy in copies:
        copy.start()
    return copies


def first_kernel(order, counts, cotangent, features, away, kept, masked, counts_held, cot_held, held, sems):
    half = away.shape[2]
    small = fetch((counts, cotangent), (counts_held, cot_held), sems)
    columns = [columns_of(q, 2 * half, 0, 2 * half) for q in order]
    blocks = fetch([features.at[0, :, c] for c in columns], [held.at[n] for n in range(len(order))], sems, len(small))
    for copy in small:
        copy.wait()
    tokens = cot_held.shape[1]
    live = counts_held[lax.axis_index("worker")] - lax.axis_index("fsdp") * tokens
    masked[...] = masked_rows(live, cot_held[0])
    for slot, into in enumerate((away, kept)):
        blocks[slot].wait()
        for side in (0, 1):
            into[side] = product(masked[...], held[slot, :, side * half : (side + 1) * half])


def rest_kernel(masked, features, *targets):
    half = targets[0].shape[2]
    places = [(4, 0, 0, 0), (4, 1, 0, 1), (2, 0, 2, 2), (2, 1, 2, 3), (0, 0, 2, 0), (0, 1, 2, 1)]
    for q, side, into, at in places:
        for core in (1, 0):
            columns = columns_of(q + core, 2 * half, side * half, half)
            targets[into + 1 - core][at] = product(masked[...], features[0, :, columns])


def drift_kernel(
    workers, counts, fragment, params, global_fragment, after, drift, scale, inverse, share, *held_and_sems
):
    del after
    held, sems = held_and_sems[:-1], held_and_sems[-1]
    copies = fetch((counts, fragment, params, global_fragment), held, sems)
    scale[...] = jnp.ones_like(scale)
    for copy in copies:
        copy.wait()
    counts_held, fragment_held, params_held, global_held = held
    mine = pl.ds(fragment_held[0], drift.shape[0], stride=FRAGS)
    count = counts_held[lax.axis_index("worker")].astype(jnp.float32)
    drift[...] = count * (global_held[...] - params_held[0, mine, :])
    scale[mine, :] = jnp.full_like(drift, 1.0 - MIXING)
    total = counts_held[0]
    for other in range(1, workers):
        total = total + counts_held[other]
    inverse[...] = jnp.ones_like(inverse) / count
    share[...] = jnp.ones_like(share) / total.astype(jnp.float32)


def add_kernel(picks, *refs):
    total = None
    for ref, pick in zip(refs, picks):
        if pick is not None:
            total = ref[pick] if total is None else total + ref[pick]
    refs[-1][...] = total


def adam(before, first, second, gradient):
    first_new = BETA_ONE * first + (1.0 - BETA_ONE) * gradient
    second_new = BETA_TWO * second + (1.0 - BETA_TWO) * gradient * gradient
    update = first_new * (1.0 / CORRECT_ONE) / (jnp.sqrt(second_new * (1.0 / CORRECT_TWO)) + ADAM_EPS)
    return before - LEARN_RATE * (update + DECAY_RATE * before), first_new, second_new


def outer(pseudo_grad, global_fragment, outer_momentum):
    momentum = NESTEROV * outer_momentum + pseudo_grad
    return global_fragment - OUTER_RATE * (pseudo_grad + NESTEROV * momentum), momentum


def half_step(half, states, sums, inverse, held):
    params, first, second = states
    kept, come, far, near = sums
    held_first, held_second = held
    rows = kept.shape[2]
    for lane in range(0, rows, LANES):
        lanes, there = pl.ds(lane, LANES), pl.ds(half * rows + lane, LANES)
        summed = kept[half, :, lanes] + come[half, :, lanes] + near[0, :, lanes] + far[0, :, lanes]
        inner, held_first[lanes, :], held_second[lanes, :] = adam(
            params[0, there, :], first[0, there, :], second[0, there, :], summed.T * inverse[0:1, :]
        )
        yield lanes, there, inner


def send(copies, sems, source, target):
    copies.append(pltpu.make_async_copy(source, target, sems.at[len(copies)]))
    copies[-1].start()


def left_kernel(
    params,
    first,
    second,
    kept,
    come,
    far,
    near,
    inverse,
    scale,
    share,
    global_fragment,
    outer_momentum,
    drift,
    other_drift,
    mix,
    new_params,
    new_first,
    new_second,
    new_global,
    new_momentum,
    held_params,
    held_first,
    held_second,
    held_global,
    held_momentum,
    spread,
    sems,
):
    copies = []
    fresh, momentum = outer((drift[...] + other_drift[...]) * share[0:1, :], global_fragment[...], outer_momentum[...])
    held_global[...] = fresh
    held_momentum[...] = momentum
    send(copies, sems, held_global, new_global)
    send(copies, sems, held_momentum, new_momentum)
    for at in range(FRAGS):
        spread[pl.ds(at, fresh.shape[0], stride=FRAGS), :] = fresh
    for lanes, there, value in half_step(
        0, (params, first, second), (kept, come, far, near), inverse, (held_first, held_second)
    ):
        held_params[lanes, :] = scale[there, :] * value + (1.0 - scale[there, :]) * spread[there, :]
        for source, target in ((held_first, new_first), (held_second, new_second), (held_params, new_params)):
            send(copies, sems, source.at[lanes], target.at[0, there])
    right = pl.ds(mix.shape[0], mix.shape[0])
    mix[...] = (1.0 - scale[right, :]) * spread[right, :]
    for copy in copies:
        copy.wait()


def right_kernel(
    params,
    first,
    second,
    kept,
    come,
    far,
    near,
    inverse,
    scale,
    mix,
    left_params,
    left_first,
    left_second,
    new_params,
    new_first,
    new_second,
    held_params,
    held_first,
    held_second,
    sems,
):
    del left_params, left_first, left_second
    copies = []
    for lanes, there, value in half_step(
        1, (params, first, second), (kept, come, far, near), inverse, (held_first, held_second)
    ):
        held_params[lanes, :] = scale[there, :] * value + mix[lanes, :]
        for source, target in ((held_first, new_first), (held_second, new_second), (held_params, new_params)):
            send(copies, sems, source.at[lanes], target.at[0, there])
    for copy in copies:
        copy.wait()


def hop(value, axis, devices, bit):
    return lax.ppermute(value, axis, [(d, d ^ bit) for d in range(devices)])


def doubling_sum(value, axis, devices):
    bit = devices // 2
    while bit:
        value = value + hop(value, axis, devices, bit)
        bit //= 2
    return value


def fast_body(mesh):
    workers, devices = mesh.shape["worker"], mesh.shape["fsdp"]

    def body(
        params, first, second, global_fragment, outer_momentum, features, cotangent, token_counts, fragment_index
    ):
        rows, width = params.shape[1:]
        pieces, tokens = global_fragment.shape[0], features.shape[1]
        block = functools.partial(jax.ShapeDtypeStruct, dtype=jnp.float32)

        def cost(count):
            return pl.CostEstimate(
                flops=2 * count * tokens * rows * width,
                bytes_accessed=count * rows * (2 * tokens + 4 * width),
                transcendentals=0,
            )

        room = pltpu.CompilerParams(vmem_limit_bytes=ROOM)
        free = pl.CostEstimate(flops=0, bytes_accessed=0, transcendentals=0)
        far_fragment = fragment_index
        far_counts, far_features, far_cotangent, far_params, far_global, far_momentum = (
            pltpu.with_memory_space_constraint(array, pltpu.HBM)
            for array in (
                token_counts,
                features,
                cotangent,
                params,
                global_fragment,
                outer_momentum,
            )
        )
        held_counts = pltpu.SMEM(token_counts.shape, token_counts.dtype)
        held_fragment = pltpu.SMEM(fragment_index.shape, fragment_index.dtype)
        held_piece = pltpu.VMEM(global_fragment.shape, global_fragment.dtype)

        half = rows // 2
        away_far, kept_far, masked = pl.pallas_call(
            functools.partial(first_kernel, (7, 6)),
            out_shape=[block((2, width, half))] * 2 + [jax.ShapeDtypeStruct((tokens, width), jnp.bfloat16)],
            in_specs=[HBM] * 3,
            out_specs=[VMEM] * 3,
            scratch_shapes=[
                held_counts,
                pltpu.VMEM(cotangent.shape, cotangent.dtype),
                pltpu.VMEM((2, tokens, rows), features.dtype),
                pltpu.SemaphoreType.DMA((4,)),
            ],
            compiler_params=room,
            cost_estimate=cost(2),
            name="far_products",
        )(far_counts, far_cotangent, far_features)
        away_pass, kept_pass, away, kept = pl.pallas_call(
            rest_kernel,
            out_shape=[block((2, width, half))] * 2 + [block((4, width, half))] * 2,
            in_specs=[VMEM] * 2,
            out_specs=[VMEM] * 4,
            compiler_params=room,
            cost_estimate=free,
            name="rest_products",
        )(masked, features)

        def add(*terms, name, count=1):
            picks = [pick for _, pick in terms]
            return pl.pallas_call(
                functools.partial(add_kernel, picks),
                out_shape=block((count, width, half)),
                in_specs=[ANY if pick is None else VMEM for pick in picks],
                out_specs=VMEM,
                compiler_params=room,
                cost_estimate=free,
                name=name,
            )(*(array for array, _ in terms))

        def part(number, count=1):
            return slice(number, number + count)

        state, piece = block(params.shape), block(global_fragment.shape)
        come_far = hop(away_far, "fsdp", devices, 1)
        sent = add((kept_far, part(0)), (come_far, part(0)), (far_fragment, None), name="add_a1")
        far_left = hop(sent, "fsdp", devices, 2)
        away_pass, away, _ = lax.optimization_barrier((away_pass, away, sent))
        come_pass = hop(away_pass, "fsdp", devices, 1)
        come = hop(away, "fsdp", devices, 1)
        drift, scale, inverse, share = pl.pallas_call(
            functools.partial(drift_kernel, workers),
            out_shape=[piece, block((rows, width)), block((8, width)), block((8, width))],
            in_specs=[HBM] * 4 + [ANY],
            out_specs=[VMEM] * 4,
            scratch_shapes=[
                held_counts,
                held_fragment,
                pltpu.VMEM(params.shape, params.dtype),
                held_piece,
                pltpu.SemaphoreType.DMA((4,)),
            ],
            compiler_params=room,
            cost_estimate=free,
            name="drift",
        )(far_counts, far_fragment, far_params, far_global, sent)
        sent = add((kept_far, part(1)), (come_far, part(1)), (drift, None), name="add_a2")
        far_right = hop(sent, "fsdp", devices, 2)
        passed = add((kept_pass, part(0)), (come_pass, part(0)), (far_left, part(0)), name="add_c1")
        far_left = hop(passed, "fsdp", devices, 4)
        near_left = add((kept, part(2)), (come, part(2)), (passed, None), name="add_n1")
        far_right = add((kept_pass, part(1)), (come_pass, part(1)), (far_right, part(0)), (passed, None), name="add_c2")
        near_right = add((kept, part(3)), (come, part(3)), (far_right, None), name="add_n2")
        drift, _ = lax.optimization_barrier((drift, sent))
        bit = workers // 2
        drifts = (drift, hop(drift, "worker", workers, bit))
        while bit > 1:
            bit //= 2
            drift = drifts[0] + drifts[1]
            drift, _ = lax.optimization_barrier((drift, near_right))
            drifts = (drift, hop(drift, "worker", workers, bit))
        near_left = hop(near_left, "fsdp", devices, 2)
        far_right = hop(far_right, "fsdp", devices, 4)
        near_right = hop(near_right, "fsdp", devices, 2)
        groups = half // LANES
        held_half = pltpu.VMEM((half, width), jnp.float32)
        mix, *results, new_global, new_momentum = pl.pallas_call(
            left_kernel,
            out_shape=[block((half, width)), state, state, state, piece, piece],
            in_specs=[VMEM] * 14,
            out_specs=[VMEM] + [HBM] * 5,
            scratch_shapes=[held_half] * 3
            + [held_piece] * 2
            + [pltpu.VMEM((rows, width), jnp.float32), pltpu.SemaphoreType.DMA((2 + 3 * groups,))],
            compiler_params=room,
            cost_estimate=pl.CostEstimate(
                flops=30 * half * width, bytes_accessed=40 * half * width, transcendentals=2 * half * width
            ),
            name="left_step",
        )(
            params,
            first,
            second,
            kept,
            come,
            far_left,
            near_left,
            inverse,
            scale,
            share,
            global_fragment,
            outer_momentum,
            *drifts,
        )
        new_params, new_first, new_second = pl.pallas_call(
            right_kernel,
            out_shape=[state] * 3,
            in_specs=[VMEM] * 10 + [HBM] * 3,
            out_specs=[HBM] * 3,
            input_output_aliases={10: 0, 11: 1, 12: 2},
            scratch_shapes=[held_half] * 3 + [pltpu.SemaphoreType.DMA((3 * groups,))],
            compiler_params=room,
            cost_estimate=free,
            name="right_step",
        )(params, first, second, kept, come, far_right, near_right, inverse, scale, mix, *results)
        return new_params, new_first, new_second, new_global, new_momentum

    return body


def plain_body(mesh):
    workers, devices = mesh.shape["worker"], mesh.shape["fsdp"]

    def body(
        params, first, second, global_fragment, outer_momentum, features, cotangent, token_counts, fragment_index
    ):
        rows, width = params.shape[1:]
        tokens = features.shape[1]
        me = lax.axis_index("fsdp")
        count = lax.dynamic_index_in_dim(token_counts, lax.axis_index("worker"), 0, keepdims=False)
        live = count.astype(jnp.float32)
        valid = (me * tokens + lax.iota(jnp.int32, tokens) < count)[:, None]
        masked = jnp.where(valid, cotangent[0], jnp.zeros_like(cotangent[0]))
        term = lax.dot_general(features[0], masked, (((0,), (0,)), ((), ())), preferred_element_type=jnp.float32)
        blocks = jnp.take(term.reshape(devices, rows, width), me ^ jnp.arange(devices, dtype=jnp.int32), axis=0)
        bit = 1
        while bit < devices:
            blocks = blocks.reshape(-1, 2, rows, width)
            blocks = blocks[:, 0] + hop(blocks[:, 1], "fsdp", devices, bit)
            bit *= 2
        gradient = blocks[0] / live
        grouped = (rows // FRAGS, FRAGS, width)
        old = lax.dynamic_index_in_dim(params[0].reshape(grouped), fragment_index[0], 1, keepdims=False)
        drift_sum = doubling_sum(live * (global_fragment - old), "worker", workers)
        total = jnp.sum(token_counts).astype(jnp.float32)
        fresh, momentum = outer(drift_sum / total, global_fragment, outer_momentum)
        inner, first_new, second_new = adam(params[0], first[0], second[0], gradient)
        inner = inner.reshape(grouped)
        piece = lax.dynamic_index_in_dim(inner, fragment_index[0], 1, keepdims=False)
        mixed = MIXING * fresh + (1.0 - MIXING) * piece
        merged = lax.dynamic_update_index_in_dim(inner, mixed, fragment_index[0], 1).reshape(rows, width)
        return merged[None], first_new[None], second_new[None], fresh, momentum

    return body


def solution(mesh):
    devices = mesh.shape["fsdp"]

    def pick(*arrays):
        rows = arrays[0].shape[1]
        body = fast_body(mesh) if devices == 8 and rows % LANES == 0 else plain_body(mesh)
        return body(*arrays)

    state = P("worker", "fsdp", None)
    piece = P("fsdp", None)
    return jax.shard_map(
        pick,
        mesh=mesh,
        in_specs=(state, state, state, piece, piece, state, state, P(), P()),
        out_specs=(state, state, state, piece, piece),
        check_vma=False,
    )
```

```python
import functools

import jax
import jax.numpy as jnp
from jax import lax
from jax.experimental import pallas as pl
from jax.experimental.pallas import tpu as pltpu
from jax.sharding import PartitionSpec as P

FRAGS = 4
LANES = 128

BETA_ONE = 0.9
BETA_TWO = 0.95
CORRECT_ONE = 0.6513216
CORRECT_TWO = 0.401263
ADAM_EPS = 1e-08
LEARN_RATE = 0.02
DECAY_RATE = 0.1
NESTEROV = 0.9
OUTER_RATE = 0.7
MIXING = 0.5

VMEM = pl.BlockSpec(memory_space=pltpu.VMEM)
SMEM = pl.BlockSpec(memory_space=pltpu.SMEM)
HBM = pl.BlockSpec(memory_space=pltpu.HBM)
ANY = pl.BlockSpec(memory_space=pl.ANY)
ROOM = 8 << 20


def masked_rows(live, cotangent):
    rows = lax.broadcasted_iota(jnp.int32, cotangent.shape, 0)
    return jnp.where(rows < live, cotangent.astype(jnp.float32), 0.0).astype(jnp.bfloat16)


def columns_of(relative, rows, start, size):
    return pl.ds(pl.multiple_of((lax.axis_index("fsdp") ^ relative) * rows + start, LANES), size)


def product(masked, features):
    return lax.dot_general(masked, features, (((0,), (0,)), ((), ())), preferred_element_type=jnp.float32)


def fetch(sources, targets, sems, start=0):
    copies = [
        pltpu.make_async_copy(source, target, sems.at[start + slot])
        for slot, (source, target) in enumerate(zip(sources, targets))
    ]
    for copy in copies:
        copy.start()
    return copies


def first_kernel(order, counts, cotangent, features, away, kept, masked, counts_held, cot_held, held, sems):
    half = away.shape[2]
    small = fetch((counts, cotangent), (counts_held, cot_held), sems)
    columns = [columns_of(q, 2 * half, 0, 2 * half) for q in order]
    blocks = fetch([features.at[0, :, c] for c in columns], [held.at[n] for n in range(len(order))], sems, len(small))
    for copy in small:
        copy.wait()
    tokens = cot_held.shape[1]
    live = counts_held[lax.axis_index("worker")] - lax.axis_index("fsdp") * tokens
    masked[...] = masked_rows(live, cot_held[0])
    for slot, into in enumerate((away, kept)):
        blocks[slot].wait()
        for side in (0, 1):
            into[side] = product(masked[...], held[slot, :, side * half : (side + 1) * half])


def rest_kernel(masked, features, *targets):
    half = targets[0].shape[2]
    places = [(4, 0, 0, 4), (4, 1, 0, 5), (2, 0, 0, 2), (2, 1, 0, 3), (0, 0, 0, 0), (0, 1, 0, 1)]
    for q, side, into, at in places:
        for core in (1, 0):
            columns = columns_of(q + core, 2 * half, side * half, half)
            targets[into + 1 - core][at] = product(masked[...], features[0, :, columns])


def drift_kernel(
    workers, counts, fragment, params, global_fragment, after, drift, scale, inverse, share, *held_and_sems
):
    del after
    held, sems = held_and_sems[:-1], held_and_sems[-1]
    copies = fetch((counts, fragment, params, global_fragment), held, sems)
    scale[...] = jnp.ones_like(scale)
    for copy in copies:
        copy.wait()
    counts_held, fragment_held, params_held, global_held = held
    mine = pl.ds(fragment_held[0], drift.shape[0], stride=FRAGS)
    count = counts_held[lax.axis_index("worker")].astype(jnp.float32)
    drift[...] = count * (global_held[...] - params_held[0, mine, :])
    scale[mine, :] = jnp.full_like(drift, 1.0 - MIXING)
    total = counts_held[0]
    for other in range(1, workers):
        total = total + counts_held[other]
    inverse[...] = jnp.ones_like(inverse) / count
    share[...] = jnp.ones_like(share) / total.astype(jnp.float32)


def add_kernel(picks, *refs):
    total = None
    for ref, pick in zip(refs, picks):
        if pick is not None:
            total = ref[pick] if total is None else total + ref[pick]
    refs[-1][...] = total


def adam(before, first, second, gradient):
    first_new = BETA_ONE * first + (1.0 - BETA_ONE) * gradient
    second_new = BETA_TWO * second + (1.0 - BETA_TWO) * gradient * gradient
    update = first_new * (1.0 / CORRECT_ONE) / (jnp.sqrt(second_new * (1.0 / CORRECT_TWO)) + ADAM_EPS)
    return before - LEARN_RATE * (update + DECAY_RATE * before), first_new, second_new


def outer(pseudo_grad, global_fragment, outer_momentum):
    momentum = NESTEROV * outer_momentum + pseudo_grad
    return global_fragment - OUTER_RATE * (pseudo_grad + NESTEROV * momentum), momentum


def half_step(half, states, sums, inverse, held):
    params, first, second = states
    kept, come, far, near = sums
    held_first, held_second = held
    rows = kept.shape[2]
    for lane in range(0, rows, LANES):
        lanes, there = pl.ds(lane, LANES), pl.ds(half * rows + lane, LANES)
        summed = kept[half, :, lanes] + come[half, :, lanes] + near[0, :, lanes] + far[0, :, lanes]
        inner, held_first[lanes, :], held_second[lanes, :] = adam(
            params[0, there, :], first[0, there, :], second[0, there, :], summed.T * inverse[0:1, :]
        )
        yield lanes, there, inner


def send(copies, sems, source, target):
    copies.append(pltpu.make_async_copy(source, target, sems.at[len(copies)]))
    copies[-1].start()


def left_kernel(
    params,
    first,
    second,
    kept,
    come,
    far,
    near,
    inverse,
    scale,
    share,
    global_fragment,
    outer_momentum,
    drift,
    other_drift,
    mix,
    new_params,
    new_first,
    new_second,
    new_global,
    new_momentum,
    held_params,
    held_first,
    held_second,
    held_global,
    held_momentum,
    spread,
    sems,
):
    copies = []
    fresh, momentum = outer((drift[...] + other_drift[...]) * share[0:1, :], global_fragment[...], outer_momentum[...])
    held_global[...] = fresh
    held_momentum[...] = momentum
    send(copies, sems, held_global, new_global)
    send(copies, sems, held_momentum, new_momentum)
    for at in range(FRAGS):
        spread[pl.ds(at, fresh.shape[0], stride=FRAGS), :] = fresh
    for lanes, there, value in half_step(
        0, (params, first, second), (kept, come, far, near), inverse, (held_first, held_second)
    ):
        held_params[lanes, :] = scale[there, :] * value + (1.0 - scale[there, :]) * spread[there, :]
        for source, target in ((held_first, new_first), (held_second, new_second), (held_params, new_params)):
            send(copies, sems, source.at[lanes], target.at[0, there])
    right = pl.ds(mix.shape[0], mix.shape[0])
    mix[...] = (1.0 - scale[right, :]) * spread[right, :]
    for copy in copies:
        copy.wait()


def right_kernel(
    params,
    first,
    second,
    kept,
    come,
    far,
    near,
    inverse,
    scale,
    mix,
    left_params,
    left_first,
    left_second,
    new_params,
    new_first,
    new_second,
    held_params,
    held_first,
    held_second,
    sems,
):
    del left_params, left_first, left_second
    copies = []
    for lanes, there, value in half_step(
        1, (params, first, second), (kept, come, far, near), inverse, (held_first, held_second)
    ):
        held_params[lanes, :] = scale[there, :] * value + mix[lanes, :]
        for source, target in ((held_first, new_first), (held_second, new_second), (held_params, new_params)):
            send(copies, sems, source.at[lanes], target.at[0, there])
    for copy in copies:
        copy.wait()


def hop(value, axis, devices, bit):
    return lax.ppermute(value, axis, [(d, d ^ bit) for d in range(devices)])


def doubling_sum(value, axis, devices):
    bit = devices // 2
    while bit:
        value = value + hop(value, axis, devices, bit)
        bit //= 2
    return value


def fast_body(mesh):
    workers, devices = mesh.shape["worker"], mesh.shape["fsdp"]

    def body(
        params, first, second, global_fragment, outer_momentum, features, cotangent, token_counts, fragment_index
    ):
        rows, width = params.shape[1:]
        pieces, tokens = global_fragment.shape[0], features.shape[1]
        block = functools.partial(jax.ShapeDtypeStruct, dtype=jnp.float32)

        def cost(count):
            return pl.CostEstimate(
                flops=2 * count * tokens * rows * width,
                bytes_accessed=count * rows * (2 * tokens + 4 * width),
                transcendentals=0,
            )

        room = pltpu.CompilerParams(vmem_limit_bytes=ROOM)
        free = pl.CostEstimate(flops=0, bytes_accessed=0, transcendentals=0)
        far_fragment = fragment_index
        far_counts, far_features, far_cotangent, far_params, far_global, far_momentum = (
            pltpu.with_memory_space_constraint(array, pltpu.HBM)
            for array in (
                token_counts,
                features,
                cotangent,
                params,
                global_fragment,
                outer_momentum,
            )
        )
        held_counts = pltpu.SMEM(token_counts.shape, token_counts.dtype)
        held_fragment = pltpu.SMEM(fragment_index.shape, fragment_index.dtype)
        held_piece = pltpu.VMEM(global_fragment.shape, global_fragment.dtype)

        half = rows // 2
        away_far, kept_far, masked = pl.pallas_call(
            functools.partial(first_kernel, (7, 6)),
            out_shape=[block((2, width, half))] * 2 + [jax.ShapeDtypeStruct((tokens, width), jnp.bfloat16)],
            in_specs=[HBM] * 3,
            out_specs=[VMEM] * 3,
            scratch_shapes=[
                held_counts,
                pltpu.VMEM(cotangent.shape, cotangent.dtype),
                pltpu.VMEM((2, tokens, rows), features.dtype),
                pltpu.SemaphoreType.DMA((4,)),
            ],
            compiler_params=room,
            cost_estimate=cost(2),
            name="far_products",
        )(far_counts, far_cotangent, far_features)
        away, kept = pl.pallas_call(
            rest_kernel,
            out_shape=[block((6, width, half))] * 2,
            in_specs=[VMEM] * 2,
            out_specs=[VMEM] * 2,
            compiler_params=room,
            cost_estimate=free,
            name="rest_products",
        )(masked, features)

        def add(*terms, name, count=1):
            picks = [pick for _, pick in terms]
            return pl.pallas_call(
                functools.partial(add_kernel, picks),
                out_shape=block((count, width, half)),
                in_specs=[ANY if pick is None else VMEM for pick in picks],
                out_specs=VMEM,
                compiler_params=room,
                cost_estimate=free,
                name=name,
            )(*(array for array, _ in terms))

        def part(number, count=1):
            return slice(number, number + count)

        state, piece = block(params.shape), block(global_fragment.shape)
        come_far = hop(away_far, "fsdp", devices, 1)
        sent = add((kept_far, part(0)), (come_far, part(0)), name="add_a1")
        far_left = hop(sent, "fsdp", devices, 2)
        away, _ = lax.optimization_barrier((away, sent))
        come = hop(away, "fsdp", devices, 1)
        drift, scale, inverse, share = pl.pallas_call(
            functools.partial(drift_kernel, workers),
            out_shape=[piece, block((rows, width)), block((8, width)), block((8, width))],
            in_specs=[HBM] * 4 + [ANY],
            out_specs=[VMEM] * 4,
            scratch_shapes=[
                held_counts,
                held_fragment,
                pltpu.VMEM(params.shape, params.dtype),
                held_piece,
                pltpu.SemaphoreType.DMA((4,)),
            ],
            compiler_params=room,
            cost_estimate=free,
            name="drift",
        )(far_counts, far_fragment, far_params, far_global, sent)
        sent = add((kept_far, part(1)), (come_far, part(1)), (drift, None), name="add_a2")
        far_right = hop(sent, "fsdp", devices, 2)
        passed = add((kept, part(4)), (come, part(4)), (far_left, part(0)), name="add_c1")
        far_left = hop(passed, "fsdp", devices, 4)
        near_left = add((kept, part(2)), (come, part(2)), (sent, None), name="add_n1")
        far_right = add((kept, part(5)), (come, part(5)), (far_right, part(0)), (passed, None), name="add_c2")
        near_right = add((kept, part(3)), (come, part(3)), (passed, None), name="add_n2")
        drift, _ = lax.optimization_barrier((drift, sent))
        bit = workers // 2
        drifts = (drift, hop(drift, "worker", workers, bit))
        while bit > 1:
            bit //= 2
            drift = drifts[0] + drifts[1]
            drift, _ = lax.optimization_barrier((drift, near_right))
            drifts = (drift, hop(drift, "worker", workers, bit))
        near_left = hop(near_left, "fsdp", devices, 2)
        far_right = hop(far_right, "fsdp", devices, 4)
        near_right = hop(near_right, "fsdp", devices, 2)
        groups = half // LANES
        held_half = pltpu.VMEM((half, width), jnp.float32)
        mix, *results, new_global, new_momentum = pl.pallas_call(
            left_kernel,
            out_shape=[block((half, width)), state, state, state, piece, piece],
            in_specs=[VMEM] * 14,
            out_specs=[VMEM] + [HBM] * 5,
            scratch_shapes=[held_half] * 3
            + [held_piece] * 2
            + [pltpu.VMEM((rows, width), jnp.float32), pltpu.SemaphoreType.DMA((2 + 3 * groups,))],
            compiler_params=room,
            cost_estimate=pl.CostEstimate(
                flops=30 * half * width, bytes_accessed=40 * half * width, transcendentals=2 * half * width
            ),
            name="left_step",
        )(
            params,
            first,
            second,
            kept,
            come,
            far_left,
            near_left,
            inverse,
            scale,
            share,
            global_fragment,
            outer_momentum,
            *drifts,
        )
        new_params, new_first, new_second = pl.pallas_call(
            right_kernel,
            out_shape=[state] * 3,
            in_specs=[VMEM] * 10 + [HBM] * 3,
            out_specs=[HBM] * 3,
            input_output_aliases={10: 0, 11: 1, 12: 2},
            scratch_shapes=[held_half] * 3 + [pltpu.SemaphoreType.DMA((3 * groups,))],
            compiler_params=room,
            cost_estimate=free,
            name="right_step",
        )(params, first, second, kept, come, far_right, near_right, inverse, scale, mix, *results)
        return new_params, new_first, new_second, new_global, new_momentum

    return body


def plain_body(mesh):
    workers, devices = mesh.shape["worker"], mesh.shape["fsdp"]

    def body(
        params, first, second, global_fragment, outer_momentum, features, cotangent, token_counts, fragment_index
    ):
        rows, width = params.shape[1:]
        tokens = features.shape[1]
        me = lax.axis_index("fsdp")
        count = lax.dynamic_index_in_dim(token_counts, lax.axis_index("worker"), 0, keepdims=False)
        live = count.astype(jnp.float32)
        valid = (me * tokens + lax.iota(jnp.int32, tokens) < count)[:, None]
        masked = jnp.where(valid, cotangent[0], jnp.zeros_like(cotangent[0]))
        term = lax.dot_general(features[0], masked, (((0,), (0,)), ((), ())), preferred_element_type=jnp.float32)
        blocks = jnp.take(term.reshape(devices, rows, width), me ^ jnp.arange(devices, dtype=jnp.int32), axis=0)
        bit = 1
        while bit < devices:
            blocks = blocks.reshape(-1, 2, rows, width)
            blocks = blocks[:, 0] + hop(blocks[:, 1], "fsdp", devices, bit)
            bit *= 2
        gradient = blocks[0] / live
        grouped = (rows // FRAGS, FRAGS, width)
        old = lax.dynamic_index_in_dim(params[0].reshape(grouped), fragment_index[0], 1, keepdims=False)
        drift_sum = doubling_sum(live * (global_fragment - old), "worker", workers)
        total = jnp.sum(token_counts).astype(jnp.float32)
        fresh, momentum = outer(drift_sum / total, global_fragment, outer_momentum)
        inner, first_new, second_new = adam(params[0], first[0], second[0], gradient)
        inner = inner.reshape(grouped)
        piece = lax.dynamic_index_in_dim(inner, fragment_index[0], 1, keepdims=False)
        mixed = MIXING * fresh + (1.0 - MIXING) * piece
        merged = lax.dynamic_update_index_in_dim(inner, mixed, fragment_index[0], 1).reshape(rows, width)
        return merged[None], first_new[None], second_new[None], fresh, momentum

    return body


def solution(mesh):
    devices = mesh.shape["fsdp"]

    def pick(*arrays):
        rows = arrays[0].shape[1]
        body = fast_body(mesh) if devices == 8 and rows % LANES == 0 else plain_body(mesh)
        return body(*arrays)

    state = P("worker", "fsdp", None)
    piece = P("fsdp", None)
    return jax.shard_map(
        pick,
        mesh=mesh,
        in_specs=(state, state, state, piece, piece, state, state, P(), P()),
        out_specs=(state, state, state, piece, piece),
        check_vma=False,
    )
```

```python
import functools

import jax
import jax.numpy as jnp
from jax import lax
from jax.experimental import pallas as pl
from jax.experimental.pallas import tpu as pltpu
from jax.sharding import PartitionSpec as P

FRAGS = 4
LANES = 128

BETA_ONE = 0.9
BETA_TWO = 0.95
CORRECT_ONE = 0.6513216
CORRECT_TWO = 0.401263
ADAM_EPS = 1e-08
LEARN_RATE = 0.02
DECAY_RATE = 0.1
NESTEROV = 0.9
OUTER_RATE = 0.7
MIXING = 0.5

VMEM = pl.BlockSpec(memory_space=pltpu.VMEM)
SMEM = pl.BlockSpec(memory_space=pltpu.SMEM)
HBM = pl.BlockSpec(memory_space=pltpu.HBM)
ANY = pl.BlockSpec(memory_space=pl.ANY)
ROOM = 8 << 20


def masked_rows(live, cotangent):
    rows = lax.broadcasted_iota(jnp.int32, cotangent.shape, 0)
    return jnp.where(rows < live, cotangent.astype(jnp.float32), 0.0).astype(jnp.bfloat16)


def columns_of(relative, rows, start, size):
    return pl.ds(pl.multiple_of((lax.axis_index("fsdp") ^ relative) * rows + start, LANES), size)


def product(masked, features):
    return lax.dot_general(masked, features, (((0,), (0,)), ((), ())), preferred_element_type=jnp.float32)


def fetch(sources, targets, sems, start=0):
    copies = [
        pltpu.make_async_copy(source, target, sems.at[start + slot])
        for slot, (source, target) in enumerate(zip(sources, targets))
    ]
    for copy in copies:
        copy.start()
    return copies


def first_kernel(
    workers, order, counts, cotangent, features, away, kept, masked, info, counts_held, cot_held, held, sems
):
    half = away.shape[2]
    small = fetch((counts, cotangent), (counts_held, cot_held), sems)
    columns = [columns_of(q, 2 * half, 0, 2 * half) for q in order]
    blocks = fetch([features.at[0, :, c] for c in columns], [held.at[n] for n in range(len(order))], sems, len(small))
    for copy in small:
        copy.wait()
    tokens = cot_held.shape[1]
    live = counts_held[lax.axis_index("worker")] - lax.axis_index("fsdp") * tokens
    masked[...] = masked_rows(live, cot_held[0])
    count, total = counts_held[lax.axis_index("worker")], counts_held[0]
    for other in range(1, workers):
        total = total + counts_held[other]
    info[0:1, :] = jnp.full((1, info.shape[1]), count.astype(jnp.float32))
    info[1:2, :] = 1.0 / info[0:1, :]
    info[2:3, :] = 1.0 / jnp.full((1, info.shape[1]), total.astype(jnp.float32))
    for slot, into in enumerate((away, kept)):
        blocks[slot].wait()
        for side in (0, 1):
            into[side] = product(masked[...], held[slot, :, side * half : (side + 1) * half])


def rest_kernel(masked, features, *targets):
    half = targets[0].shape[2]
    places = [(4, 0, 0, 4), (4, 1, 0, 5), (2, 0, 0, 2), (2, 1, 0, 3), (0, 0, 0, 0), (0, 1, 0, 1)]
    for q, side, into, at in places:
        for core in (1, 0):
            columns = columns_of(q + core, 2 * half, side * half, half)
            targets[into + 1 - core][at] = product(masked[...], features[0, :, columns])


def drift_kernel(info, fragment, params, global_fragment, after, drift, scale):
    del after
    mine = pl.ds(fragment[0], drift.shape[0], stride=FRAGS)
    drift[...] = info[0:1, :] * (global_fragment[...] - params[0, mine, :])
    scale[...] = jnp.ones_like(scale)
    scale[mine, :] = jnp.full_like(drift, 1.0 - MIXING)


def add_kernel(picks, *refs):
    total = None
    for ref, pick in zip(refs, picks):
        if pick is not None:
            total = ref[pick] if total is None else total + ref[pick]
    refs[-1][...] = total


def adam(before, first, second, gradient):
    first_new = BETA_ONE * first + (1.0 - BETA_ONE) * gradient
    second_new = BETA_TWO * second + (1.0 - BETA_TWO) * gradient * gradient
    update = first_new * (1.0 / CORRECT_ONE) / (jnp.sqrt(second_new * (1.0 / CORRECT_TWO)) + ADAM_EPS)
    return before - LEARN_RATE * (update + DECAY_RATE * before), first_new, second_new


def outer(pseudo_grad, global_fragment, outer_momentum):
    momentum = NESTEROV * outer_momentum + pseudo_grad
    return global_fragment - OUTER_RATE * (pseudo_grad + NESTEROV * momentum), momentum


def half_step(half, states, sums, info, held):
    params, first, second = states
    kept, come, far, near = sums
    held_first, held_second = held
    rows = kept.shape[2]
    for lane in range(0, rows, LANES):
        lanes, there = pl.ds(lane, LANES), pl.ds(half * rows + lane, LANES)
        summed = kept[half, :, lanes] + come[half, :, lanes] + near[0, :, lanes] + far[0, :, lanes]
        inner, held_first[lanes, :], held_second[lanes, :] = adam(
            params[0, there, :], first[0, there, :], second[0, there, :], summed.T * info[1:2, :]
        )
        yield lanes, there, inner


def send(copies, sems, source, target):
    copies.append(pltpu.make_async_copy(source, target, sems.at[len(copies)]))
    copies[-1].start()


def left_kernel(
    params,
    first,
    second,
    kept,
    come,
    far,
    near,
    info,
    scale,
    global_fragment,
    outer_momentum,
    drift,
    other_drift,
    mix,
    new_params,
    new_first,
    new_second,
    new_global,
    new_momentum,
    held_params,
    held_first,
    held_second,
    held_global,
    held_momentum,
    spread,
    sems,
):
    copies = []
    fresh, momentum = outer((drift[...] + other_drift[...]) * info[2:3, :], global_fragment[...], outer_momentum[...])
    held_global[...] = fresh
    held_momentum[...] = momentum
    send(copies, sems, held_global, new_global)
    send(copies, sems, held_momentum, new_momentum)
    for at in range(FRAGS):
        spread[pl.ds(at, fresh.shape[0], stride=FRAGS), :] = fresh
    for lanes, there, value in half_step(
        0, (params, first, second), (kept, come, far, near), info, (held_first, held_second)
    ):
        held_params[lanes, :] = scale[there, :] * value + (1.0 - scale[there, :]) * spread[there, :]
        for source, target in ((held_first, new_first), (held_second, new_second), (held_params, new_params)):
            send(copies, sems, source.at[lanes], target.at[0, there])
    right = pl.ds(mix.shape[0], mix.shape[0])
    mix[...] = (1.0 - scale[right, :]) * spread[right, :]
    for copy in copies:
        copy.wait()


def right_kernel(
    params,
    first,
    second,
    kept,
    come,
    far,
    near,
    info,
    scale,
    mix,
    left_params,
    left_first,
    left_second,
    new_params,
    new_first,
    new_second,
    held_params,
    held_first,
    held_second,
    sems,
):
    del left_params, left_first, left_second
    copies = []
    for lanes, there, value in half_step(
        1, (params, first, second), (kept, come, far, near), info, (held_first, held_second)
    ):
        held_params[lanes, :] = scale[there, :] * value + mix[lanes, :]
        for source, target in ((held_first, new_first), (held_second, new_second), (held_params, new_params)):
            send(copies, sems, source.at[lanes], target.at[0, there])
    for copy in copies:
        copy.wait()


def hop(value, axis, devices, bit):
    return lax.ppermute(value, axis, [(d, d ^ bit) for d in range(devices)])


def doubling_sum(value, axis, devices):
    bit = devices // 2
    while bit:
        value = value + hop(value, axis, devices, bit)
        bit //= 2
    return value


def fast_body(mesh):
    workers, devices = mesh.shape["worker"], mesh.shape["fsdp"]

    def body(
        params, first, second, global_fragment, outer_momentum, features, cotangent, token_counts, fragment_index
    ):
        rows, width = params.shape[1:]
        pieces, tokens = global_fragment.shape[0], features.shape[1]
        block = functools.partial(jax.ShapeDtypeStruct, dtype=jnp.float32)

        def cost(count):
            return pl.CostEstimate(
                flops=2 * count * tokens * rows * width,
                bytes_accessed=count * rows * (2 * tokens + 4 * width),
                transcendentals=0,
            )

        room = pltpu.CompilerParams(vmem_limit_bytes=ROOM)
        free = pl.CostEstimate(flops=0, bytes_accessed=0, transcendentals=0)
        far_counts, far_features, far_cotangent = (
            pltpu.with_memory_space_constraint(array, pltpu.HBM) for array in (token_counts, features, cotangent)
        )
        held_counts = pltpu.SMEM(token_counts.shape, token_counts.dtype)
        held_piece = pltpu.VMEM(global_fragment.shape, global_fragment.dtype)

        half = rows // 2
        away_far, kept_far, masked, info = pl.pallas_call(
            functools.partial(first_kernel, workers, (7, 6)),
            out_shape=[block((2, width, half))] * 2 + [jax.ShapeDtypeStruct((tokens, width), jnp.bfloat16), block((8, width))],
            in_specs=[HBM] * 3,
            out_specs=[VMEM] * 4,
            scratch_shapes=[
                held_counts,
                pltpu.VMEM(cotangent.shape, cotangent.dtype),
                pltpu.VMEM((2, tokens, rows), features.dtype),
                pltpu.SemaphoreType.DMA((4,)),
            ],
            compiler_params=room,
            cost_estimate=cost(2),
            name="far_products",
        )(far_counts, far_cotangent, far_features)
        away, kept = pl.pallas_call(
            rest_kernel,
            out_shape=[block((6, width, half))] * 2,
            in_specs=[VMEM] * 2,
            out_specs=[VMEM] * 2,
            compiler_params=room,
            cost_estimate=free,
            name="rest_products",
        )(masked, features)

        def add(*terms, name, count=1):
            picks = [pick for _, pick in terms]
            return pl.pallas_call(
                functools.partial(add_kernel, picks),
                out_shape=block((count, width, half)),
                in_specs=[ANY if pick is None else VMEM for pick in picks],
                out_specs=VMEM,
                compiler_params=room,
                cost_estimate=free,
                name=name,
            )(*(array for array, _ in terms))

        def part(number, count=1):
            return slice(number, number + count)

        state, piece = block(params.shape), block(global_fragment.shape)
        come_far = hop(away_far, "fsdp", devices, 1)
        sent = add((kept_far, part(0)), (come_far, part(0)), name="add_a1")
        far_left = hop(sent, "fsdp", devices, 2)
        away, _ = lax.optimization_barrier((away, sent))
        come = hop(away, "fsdp", devices, 1)
        drift, scale = pl.pallas_call(
            drift_kernel,
            out_shape=[piece, block((rows, width))],
            in_specs=[VMEM, SMEM, VMEM, VMEM, ANY],
            out_specs=[VMEM] * 2,
            compiler_params=room,
            cost_estimate=free,
            name="drift",
        )(info, fragment_index, params, global_fragment, sent)
        sent = add((kept_far, part(1)), (come_far, part(1)), (drift, None), name="add_a2")
        far_right = hop(sent, "fsdp", devices, 2)
        passed = add((kept, part(4)), (come, part(4)), (far_left, part(0)), name="add_c1")
        far_left = hop(passed, "fsdp", devices, 4)
        near_left = add((kept, part(2)), (come, part(2)), (sent, None), name="add_n1")
        far_right = add((kept, part(5)), (come, part(5)), (far_right, part(0)), (passed, None), name="add_c2")
        near_right = add((kept, part(3)), (come, part(3)), (passed, None), name="add_n2")
        drift, _ = lax.optimization_barrier((drift, sent))
        bit = workers // 2
        drifts = (drift, hop(drift, "worker", workers, bit))
        while bit > 1:
            bit //= 2
            drift = drifts[0] + drifts[1]
            drift, _ = lax.optimization_barrier((drift, near_right))
            drifts = (drift, hop(drift, "worker", workers, bit))
        near_left = hop(near_left, "fsdp", devices, 2)
        far_right = hop(far_right, "fsdp", devices, 4)
        near_right = hop(near_right, "fsdp", devices, 2)
        groups = half // LANES
        held_half = pltpu.VMEM((half, width), jnp.float32)
        mix, *results, new_global, new_momentum = pl.pallas_call(
            left_kernel,
            out_shape=[block((half, width)), state, state, state, piece, piece],
            in_specs=[VMEM] * 13,
            out_specs=[VMEM] + [HBM] * 5,
            scratch_shapes=[held_half] * 3
            + [held_piece] * 2
            + [pltpu.VMEM((rows, width), jnp.float32), pltpu.SemaphoreType.DMA((2 + 3 * groups,))],
            compiler_params=room,
            cost_estimate=pl.CostEstimate(
                flops=30 * half * width, bytes_accessed=40 * half * width, transcendentals=2 * half * width
            ),
            name="left_step",
        )(
            params,
            first,
            second,
            kept,
            come,
            far_left,
            near_left,
            info,
            scale,
            global_fragment,
            outer_momentum,
            *drifts,
        )
        new_params, new_first, new_second = pl.pallas_call(
            right_kernel,
            out_shape=[state] * 3,
            in_specs=[VMEM] * 10 + [HBM] * 3,
            out_specs=[HBM] * 3,
            input_output_aliases={10: 0, 11: 1, 12: 2},
            scratch_shapes=[held_half] * 3 + [pltpu.SemaphoreType.DMA((3 * groups,))],
            compiler_params=room,
            cost_estimate=free,
            name="right_step",
        )(params, first, second, kept, come, far_right, near_right, info, scale, mix, *results)
        return new_params, new_first, new_second, new_global, new_momentum

    return body


def plain_body(mesh):
    workers, devices = mesh.shape["worker"], mesh.shape["fsdp"]

    def body(
        params, first, second, global_fragment, outer_momentum, features, cotangent, token_counts, fragment_index
    ):
        rows, width = params.shape[1:]
        tokens = features.shape[1]
        me = lax.axis_index("fsdp")
        count = lax.dynamic_index_in_dim(token_counts, lax.axis_index("worker"), 0, keepdims=False)
        live = count.astype(jnp.float32)
        valid = (me * tokens + lax.iota(jnp.int32, tokens) < count)[:, None]
        masked = jnp.where(valid, cotangent[0], jnp.zeros_like(cotangent[0]))
        term = lax.dot_general(features[0], masked, (((0,), (0,)), ((), ())), preferred_element_type=jnp.float32)
        blocks = jnp.take(term.reshape(devices, rows, width), me ^ jnp.arange(devices, dtype=jnp.int32), axis=0)
        bit = 1
        while bit < devices:
            blocks = blocks.reshape(-1, 2, rows, width)
            blocks = blocks[:, 0] + hop(blocks[:, 1], "fsdp", devices, bit)
            bit *= 2
        gradient = blocks[0] / live
        grouped = (rows // FRAGS, FRAGS, width)
        old = lax.dynamic_index_in_dim(params[0].reshape(grouped), fragment_index[0], 1, keepdims=False)
        drift_sum = doubling_sum(live * (global_fragment - old), "worker", workers)
        total = jnp.sum(token_counts).astype(jnp.float32)
        fresh, momentum = outer(drift_sum / total, global_fragment, outer_momentum)
        inner, first_new, second_new = adam(params[0], first[0], second[0], gradient)
        inner = inner.reshape(grouped)
        piece = lax.dynamic_index_in_dim(inner, fragment_index[0], 1, keepdims=False)
        mixed = MIXING * fresh + (1.0 - MIXING) * piece
        merged = lax.dynamic_update_index_in_dim(inner, mixed, fragment_index[0], 1).reshape(rows, width)
        return merged[None], first_new[None], second_new[None], fresh, momentum

    return body


def solution(mesh):
    devices = mesh.shape["fsdp"]

    def pick(*arrays):
        rows = arrays[0].shape[1]
        body = fast_body(mesh) if devices == 8 and rows % LANES == 0 else plain_body(mesh)
        return body(*arrays)

    state = P("worker", "fsdp", None)
    piece = P("fsdp", None)
    return jax.shard_map(
        pick,
        mesh=mesh,
        in_specs=(state, state, state, piece, piece, state, state, P(), P()),
        out_specs=(state, state, state, piece, piece),
        check_vma=False,
    )
```

```python
import functools

import jax
import jax.numpy as jnp
from jax import lax
from jax.experimental import pallas as pl
from jax.experimental.pallas import tpu as pltpu
from jax.sharding import PartitionSpec as P

FRAGS = 4
LANES = 128

BETA_ONE = 0.9
BETA_TWO = 0.95
CORRECT_ONE = 0.6513216
CORRECT_TWO = 0.401263
ADAM_EPS = 1e-08
LEARN_RATE = 0.02
DECAY_RATE = 0.1
NESTEROV = 0.9
OUTER_RATE = 0.7
MIXING = 0.5

VMEM = pl.BlockSpec(memory_space=pltpu.VMEM)
SMEM = pl.BlockSpec(memory_space=pltpu.SMEM)
HBM = pl.BlockSpec(memory_space=pltpu.HBM)
ANY = pl.BlockSpec(memory_space=pl.ANY)
ROOM = 8 << 20


def masked_rows(live, cotangent):
    rows = lax.broadcasted_iota(jnp.int32, cotangent.shape, 0)
    return jnp.where(rows < live, cotangent.astype(jnp.float32), 0.0).astype(jnp.bfloat16)


def columns_of(relative, rows, start, size):
    return pl.ds(pl.multiple_of((lax.axis_index("fsdp") ^ relative) * rows + start, LANES), size)


def product(masked, features):
    return lax.dot_general(masked, features, (((0,), (0,)), ((), ())), preferred_element_type=jnp.float32)


def fetch(sources, targets, sems, start=0):
    copies = [
        pltpu.make_async_copy(source, target, sems.at[start + slot])
        for slot, (source, target) in enumerate(zip(sources, targets))
    ]
    for copy in copies:
        copy.start()
    return copies


def first_kernel(order, counts, cotangent, features, away, kept, masked, counts_held, cot_held, held, sems):
    half = away.shape[2]
    small = fetch((counts, cotangent), (counts_held, cot_held), sems)
    columns = [columns_of(q, 2 * half, 0, 2 * half) for q in order]
    blocks = fetch([features.at[0, :, c] for c in columns], [held.at[n] for n in range(len(order))], sems, len(small))
    for copy in small:
        copy.wait()
    tokens = cot_held.shape[1]
    live = counts_held[lax.axis_index("worker")] - lax.axis_index("fsdp") * tokens
    masked[...] = masked_rows(live, cot_held[0])
    for slot, into in enumerate((away, kept)):
        blocks[slot].wait()
        for side in (0, 1):
            into[side] = product(masked[...], held[slot, :, side * half : (side + 1) * half])


def rest_kernel(masked, features, away, kept, held, sems):
    half = away.shape[2]
    order = [(q + core, at) for q, at in ((4, 4), (2, 2), (0, 0)) for core in (1, 0)]
    sources = [features.at[0, :, columns_of(q, 2 * half, 0, 2 * half)] for q, _ in order]
    blocks = fetch(sources, [held.at[slot] for slot in range(len(order))], sems)
    for slot, (q, at) in enumerate(order):
        blocks[slot].wait()
        for side in (0, 1):
            value = product(masked[...], held[slot, :, side * half : (side + 1) * half])
            (away if q & 1 else kept)[at + side] = value


def drift_kernel(
    workers, counts, fragment, params, global_fragment, after, drift, scale, inverse, share, *held_and_sems
):
    del after
    held, sems = held_and_sems[:-1], held_and_sems[-1]
    copies = fetch((counts, fragment, params, global_fragment), held, sems)
    scale[...] = jnp.ones_like(scale)
    for copy in copies:
        copy.wait()
    counts_held, fragment_held, params_held, global_held = held
    mine = pl.ds(fragment_held[0], drift.shape[0], stride=FRAGS)
    count = counts_held[lax.axis_index("worker")].astype(jnp.float32)
    drift[...] = count * (global_held[...] - params_held[0, mine, :])
    scale[mine, :] = jnp.full_like(drift, 1.0 - MIXING)
    total = counts_held[0]
    for other in range(1, workers):
        total = total + counts_held[other]
    inverse[...] = jnp.ones_like(inverse) / count
    share[...] = jnp.ones_like(share) / total.astype(jnp.float32)


def add_kernel(picks, *refs):
    total = None
    for ref, pick in zip(refs, picks):
        if pick is not None:
            total = ref[pick] if total is None else total + ref[pick]
    refs[-1][...] = total


def adam(before, first, second, gradient):
    first_new = BETA_ONE * first + (1.0 - BETA_ONE) * gradient
    second_new = BETA_TWO * second + (1.0 - BETA_TWO) * gradient * gradient
    update = first_new * (1.0 / CORRECT_ONE) / (jnp.sqrt(second_new * (1.0 / CORRECT_TWO)) + ADAM_EPS)
    return before - LEARN_RATE * (update + DECAY_RATE * before), first_new, second_new


def outer(pseudo_grad, global_fragment, outer_momentum):
    momentum = NESTEROV * outer_momentum + pseudo_grad
    return global_fragment - OUTER_RATE * (pseudo_grad + NESTEROV * momentum), momentum


def half_step(half, states, sums, inverse, held):
    params, first, second = states
    kept, come, far, near = sums
    held_first, held_second = held
    rows = kept.shape[2]
    for lane in range(0, rows, LANES):
        lanes, there = pl.ds(lane, LANES), pl.ds(half * rows + lane, LANES)
        summed = kept[half, :, lanes] + come[half, :, lanes] + near[0, :, lanes] + far[0, :, lanes]
        inner, held_first[lanes, :], held_second[lanes, :] = adam(
            params[0, there, :], first[0, there, :], second[0, there, :], summed.T * inverse[0:1, :]
        )
        yield lanes, there, inner


def send(copies, sems, source, target):
    copies.append(pltpu.make_async_copy(source, target, sems.at[len(copies)]))
    copies[-1].start()


def left_kernel(
    params,
    first,
    second,
    kept,
    come,
    far,
    near,
    inverse,
    scale,
    share,
    global_fragment,
    outer_momentum,
    drift,
    other_drift,
    mix,
    new_params,
    new_first,
    new_second,
    new_global,
    new_momentum,
    held_params,
    held_first,
    held_second,
    held_global,
    held_momentum,
    spread,
    sems,
):
    copies = []
    fresh, momentum = outer((drift[...] + other_drift[...]) * share[0:1, :], global_fragment[...], outer_momentum[...])
    held_global[...] = fresh
    held_momentum[...] = momentum
    send(copies, sems, held_global, new_global)
    send(copies, sems, held_momentum, new_momentum)
    for at in range(FRAGS):
        spread[pl.ds(at, fresh.shape[0], stride=FRAGS), :] = fresh
    for lanes, there, value in half_step(
        0, (params, first, second), (kept, come, far, near), inverse, (held_first, held_second)
    ):
        held_params[lanes, :] = scale[there, :] * value + (1.0 - scale[there, :]) * spread[there, :]
        for source, target in ((held_first, new_first), (held_second, new_second), (held_params, new_params)):
            send(copies, sems, source.at[lanes], target.at[0, there])
    right = pl.ds(mix.shape[0], mix.shape[0])
    mix[...] = (1.0 - scale[right, :]) * spread[right, :]
    for copy in copies:
        copy.wait()


def right_kernel(
    params,
    first,
    second,
    kept,
    come,
    far,
    near,
    inverse,
    scale,
    mix,
    left_params,
    left_first,
    left_second,
    new_params,
    new_first,
    new_second,
    held_params,
    held_first,
    held_second,
    sems,
):
    del left_params, left_first, left_second
    copies = []
    for lanes, there, value in half_step(
        1, (params, first, second), (kept, come, far, near), inverse, (held_first, held_second)
    ):
        held_params[lanes, :] = scale[there, :] * value + mix[lanes, :]
        for source, target in ((held_first, new_first), (held_second, new_second), (held_params, new_params)):
            send(copies, sems, source.at[lanes], target.at[0, there])
    for copy in copies:
        copy.wait()


def hop(value, axis, devices, bit):
    return lax.ppermute(value, axis, [(d, d ^ bit) for d in range(devices)])


def doubling_sum(value, axis, devices):
    bit = devices // 2
    while bit:
        value = value + hop(value, axis, devices, bit)
        bit //= 2
    return value


def fast_body(mesh):
    workers, devices = mesh.shape["worker"], mesh.shape["fsdp"]

    def body(
        params, first, second, global_fragment, outer_momentum, features, cotangent, token_counts, fragment_index
    ):
        rows, width = params.shape[1:]
        pieces, tokens = global_fragment.shape[0], features.shape[1]
        block = functools.partial(jax.ShapeDtypeStruct, dtype=jnp.float32)

        def cost(count):
            return pl.CostEstimate(
                flops=2 * count * tokens * rows * width,
                bytes_accessed=count * rows * (2 * tokens + 4 * width),
                transcendentals=0,
            )

        room = pltpu.CompilerParams(vmem_limit_bytes=ROOM)
        free = pl.CostEstimate(flops=0, bytes_accessed=0, transcendentals=0)
        far_fragment = fragment_index
        far_counts, far_features, far_cotangent, far_params, far_global, far_momentum = (
            pltpu.with_memory_space_constraint(array, pltpu.HBM)
            for array in (
                token_counts,
                features,
                cotangent,
                params,
                global_fragment,
                outer_momentum,
            )
        )
        held_counts = pltpu.SMEM(token_counts.shape, token_counts.dtype)
        held_fragment = pltpu.SMEM(fragment_index.shape, fragment_index.dtype)
        held_piece = pltpu.VMEM(global_fragment.shape, global_fragment.dtype)

        half = rows // 2
        away_far, kept_far, masked = pl.pallas_call(
            functools.partial(first_kernel, (7, 6)),
            out_shape=[block((2, width, half))] * 2 + [jax.ShapeDtypeStruct((tokens, width), jnp.bfloat16)],
            in_specs=[HBM] * 3,
            out_specs=[VMEM] * 3,
            scratch_shapes=[
                held_counts,
                pltpu.VMEM(cotangent.shape, cotangent.dtype),
                pltpu.VMEM((2, tokens, rows), features.dtype),
                pltpu.SemaphoreType.DMA((4,)),
            ],
            compiler_params=room,
            cost_estimate=cost(2),
            name="far_products",
        )(far_counts, far_cotangent, far_features)
        away, kept = pl.pallas_call(
            rest_kernel,
            out_shape=[block((6, width, half))] * 2,
            in_specs=[VMEM, HBM],
            out_specs=[VMEM] * 2,
            scratch_shapes=[pltpu.VMEM((6, tokens, rows), features.dtype), pltpu.SemaphoreType.DMA((6,))],
            compiler_params=room,
            cost_estimate=free,
            name="rest_products",
        )(masked, far_features)

        def add(*terms, name, count=1):
            picks = [pick for _, pick in terms]
            return pl.pallas_call(
                functools.partial(add_kernel, picks),
                out_shape=block((count, width, half)),
                in_specs=[ANY if pick is None else VMEM for pick in picks],
                out_specs=VMEM,
                compiler_params=room,
                cost_estimate=free,
                name=name,
            )(*(array for array, _ in terms))

        def part(number, count=1):
            return slice(number, number + count)

        state, piece = block(params.shape), block(global_fragment.shape)
        come_far = hop(away_far, "fsdp", devices, 1)
        sent = add((kept_far, part(0)), (come_far, part(0)), name="add_a1")
        far_left = hop(sent, "fsdp", devices, 2)
        away, _ = lax.optimization_barrier((away, sent))
        come = hop(away, "fsdp", devices, 1)
        drift, scale, inverse, share = pl.pallas_call(
            functools.partial(drift_kernel, workers),
            out_shape=[piece, block((rows, width)), block((8, width)), block((8, width))],
            in_specs=[HBM] * 4 + [ANY],
            out_specs=[VMEM] * 4,
            scratch_shapes=[
                held_counts,
                held_fragment,
                pltpu.VMEM(params.shape, params.dtype),
                held_piece,
                pltpu.SemaphoreType.DMA((4,)),
            ],
            compiler_params=room,
            cost_estimate=free,
            name="drift",
        )(far_counts, far_fragment, far_params, far_global, sent)
        sent = add((kept_far, part(1)), (come_far, part(1)), (drift, None), name="add_a2")
        far_right = hop(sent, "fsdp", devices, 2)
        passed = add((kept, part(4)), (come, part(4)), (far_left, part(0)), name="add_c1")
        far_left = hop(passed, "fsdp", devices, 4)
        near_left = add((kept, part(2)), (come, part(2)), (sent, None), name="add_n1")
        far_right = add((kept, part(5)), (come, part(5)), (far_right, part(0)), (near_left, None), name="add_c2")
        near_right = add((kept, part(3)), (come, part(3)), (far_right, None), name="add_n2")
        drift, _ = lax.optimization_barrier((drift, sent))
        bit = workers // 2
        drifts = (drift, hop(drift, "worker", workers, bit))
        while bit > 1:
            bit //= 2
            drift = drifts[0] + drifts[1]
            drift, _ = lax.optimization_barrier((drift, near_right))
            drifts = (drift, hop(drift, "worker", workers, bit))
        near_left = hop(near_left, "fsdp", devices, 2)
        far_right = hop(far_right, "fsdp", devices, 4)
        near_right = hop(near_right, "fsdp", devices, 2)
        groups = half // LANES
        held_half = pltpu.VMEM((half, width), jnp.float32)
        mix, *results, new_global, new_momentum = pl.pallas_call(
            left_kernel,
            out_shape=[block((half, width)), state, state, state, piece, piece],
            in_specs=[VMEM] * 14,
            out_specs=[VMEM] + [HBM] * 5,
            scratch_shapes=[held_half] * 3
            + [held_piece] * 2
            + [pltpu.VMEM((rows, width), jnp.float32), pltpu.SemaphoreType.DMA((2 + 3 * groups,))],
            compiler_params=room,
            cost_estimate=pl.CostEstimate(
                flops=30 * half * width, bytes_accessed=40 * half * width, transcendentals=2 * half * width
            ),
            name="left_step",
        )(
            params,
            first,
            second,
            kept,
            come,
            far_left,
            near_left,
            inverse,
            scale,
            share,
            global_fragment,
            outer_momentum,
            *drifts,
        )
        new_params, new_first, new_second = pl.pallas_call(
            right_kernel,
            out_shape=[state] * 3,
            in_specs=[VMEM] * 10 + [HBM] * 3,
            out_specs=[HBM] * 3,
            input_output_aliases={10: 0, 11: 1, 12: 2},
            scratch_shapes=[held_half] * 3 + [pltpu.SemaphoreType.DMA((3 * groups,))],
            compiler_params=room,
            cost_estimate=free,
            name="right_step",
        )(params, first, second, kept, come, far_right, near_right, inverse, scale, mix, *results)
        return new_params, new_first, new_second, new_global, new_momentum

    return body


def plain_body(mesh):
    workers, devices = mesh.shape["worker"], mesh.shape["fsdp"]

    def body(
        params, first, second, global_fragment, outer_momentum, features, cotangent, token_counts, fragment_index
    ):
        rows, width = params.shape[1:]
        tokens = features.shape[1]
        me = lax.axis_index("fsdp")
        count = lax.dynamic_index_in_dim(token_counts, lax.axis_index("worker"), 0, keepdims=False)
        live = count.astype(jnp.float32)
        valid = (me * tokens + lax.iota(jnp.int32, tokens) < count)[:, None]
        masked = jnp.where(valid, cotangent[0], jnp.zeros_like(cotangent[0]))
        term = lax.dot_general(features[0], masked, (((0,), (0,)), ((), ())), preferred_element_type=jnp.float32)
        blocks = jnp.take(term.reshape(devices, rows, width), me ^ jnp.arange(devices, dtype=jnp.int32), axis=0)
        bit = 1
        while bit < devices:
            blocks = blocks.reshape(-1, 2, rows, width)
            blocks = blocks[:, 0] + hop(blocks[:, 1], "fsdp", devices, bit)
            bit *= 2
        gradient = blocks[0] / live
        grouped = (rows // FRAGS, FRAGS, width)
        old = lax.dynamic_index_in_dim(params[0].reshape(grouped), fragment_index[0], 1, keepdims=False)
        drift_sum = doubling_sum(live * (global_fragment - old), "worker", workers)
        total = jnp.sum(token_counts).astype(jnp.float32)
        fresh, momentum = outer(drift_sum / total, global_fragment, outer_momentum)
        inner, first_new, second_new = adam(params[0], first[0], second[0], gradient)
        inner = inner.reshape(grouped)
        piece = lax.dynamic_index_in_dim(inner, fragment_index[0], 1, keepdims=False)
        mixed = MIXING * fresh + (1.0 - MIXING) * piece
        merged = lax.dynamic_update_index_in_dim(inner, mixed, fragment_index[0], 1).reshape(rows, width)
        return merged[None], first_new[None], second_new[None], fresh, momentum

    return body


def solution(mesh):
    devices = mesh.shape["fsdp"]

    def pick(*arrays):
        rows = arrays[0].shape[1]
        body = fast_body(mesh) if devices == 8 and rows % LANES == 0 else plain_body(mesh)
        return body(*arrays)

    state = P("worker", "fsdp", None)
    piece = P("fsdp", None)
    return jax.shard_map(
        pick,
        mesh=mesh,
        in_specs=(state, state, state, piece, piece, state, state, P(), P()),
        out_specs=(state, state, state, piece, piece),
        check_vma=False,
    )
```

```python
import functools

import jax
import jax.numpy as jnp
from jax import lax
from jax.experimental import pallas as pl
from jax.experimental.pallas import tpu as pltpu
from jax.sharding import PartitionSpec as P

FRAGS = 4
LANES = 128
SPARE = 8

BETA_ONE = 0.9
BETA_TWO = 0.95
CORRECT_ONE = 0.6513216
CORRECT_TWO = 0.401263
ADAM_EPS = 1e-08
LEARN_RATE = 0.02
DECAY_RATE = 0.1
NESTEROV = 0.9
OUTER_RATE = 0.7
MIXING = 0.5

VMEM = pl.BlockSpec(memory_space=pltpu.VMEM)
SMEM = pl.BlockSpec(memory_space=pltpu.SMEM)
HBM = pl.BlockSpec(memory_space=pltpu.HBM)
ANY = pl.BlockSpec(memory_space=pl.ANY)
ROOM = 8 << 20


def masked_rows(live, cotangent):
    rows = lax.broadcasted_iota(jnp.int32, cotangent.shape, 0)
    return jnp.where(rows < live, cotangent.astype(jnp.float32), 0.0).astype(jnp.bfloat16)


def columns_of(relative, rows, start, size):
    return pl.ds(pl.multiple_of((lax.axis_index("fsdp") ^ relative) * rows + start, LANES), size)


def product(masked, features):
    return lax.dot_general(masked, features, (((0,), (0,)), ((), ())), preferred_element_type=jnp.float32)


def fetch(sources, targets, sems, start=0):
    copies = [
        pltpu.make_async_copy(source, target, sems.at[start + slot])
        for slot, (source, target) in enumerate(zip(sources, targets))
    ]
    for copy in copies:
        copy.start()
    return copies


def first_kernel(
    workers, order, counts, cotangent, features, away, kept, masked, info, counts_held, cot_held, held, sems
):
    half = away.shape[2]
    small = fetch((counts, cotangent), (counts_held, cot_held), sems)
    columns = [columns_of(q, 2 * half, 0, 2 * half) for q in order]
    blocks = fetch([features.at[0, :, c] for c in columns], [held.at[n] for n in range(len(order))], sems, len(small))
    for copy in small:
        copy.wait()
    tokens = cot_held.shape[1]
    live = counts_held[lax.axis_index("worker")] - lax.axis_index("fsdp") * tokens
    masked[...] = masked_rows(live, cot_held[0])
    count, total = counts_held[lax.axis_index("worker")], counts_held[0]
    for other in range(1, workers):
        total = total + counts_held[other]
    info[0:1, :] = jnp.full((1, info.shape[1]), count.astype(jnp.float32))
    info[1:2, :] = 1.0 / info[0:1, :]
    info[2:3, :] = 1.0 / jnp.full((1, info.shape[1]), total.astype(jnp.float32))
    for slot, into in enumerate((away, kept)):
        blocks[slot].wait()
        for side in (0, 1):
            into[side] = product(masked[...], held[slot, :, side * half : (side + 1) * half])


def rest_kernel(masked, features, *targets):
    half = targets[0].shape[2]
    places = [(4, 0, 0, 4), (4, 1, 0, 5), (2, 0, 0, 2), (2, 1, 0, 3), (0, 0, 0, 0), (0, 1, 0, 1)]
    for q, side, into, at in places:
        for core in (1, 0):
            columns = columns_of(q + core, 2 * half, side * half, half)
            targets[into + 1 - core][at] = product(masked[...], features[0, :, columns])


def drift_kernel(info, fragment, params, global_fragment, after, drift, scale):
    del after
    mine = pl.ds(fragment[0], drift.shape[0], stride=FRAGS)
    drift[...] = info[0:1, :] * (global_fragment[...] - params[0, mine, :])
    scale[...] = jnp.ones_like(scale)
    scale[mine, :] = jnp.full_like(drift, 1.0 - MIXING)


def add_kernel(picks, *refs):
    total = None
    for ref, pick in zip(refs, picks):
        if pick is not None:
            total = ref[pick] if total is None else total + ref[pick]
    refs[-1][...] = total


def adam(before, first, second, gradient):
    first_new = BETA_ONE * first + (1.0 - BETA_ONE) * gradient
    second_new = BETA_TWO * second + (1.0 - BETA_TWO) * gradient * gradient
    update = first_new * (1.0 / CORRECT_ONE) / (jnp.sqrt(second_new * (1.0 / CORRECT_TWO)) + ADAM_EPS)
    return before - LEARN_RATE * (update + DECAY_RATE * before), first_new, second_new


def outer(pseudo_grad, global_fragment, outer_momentum):
    momentum = NESTEROV * outer_momentum + pseudo_grad
    return global_fragment - OUTER_RATE * (pseudo_grad + NESTEROV * momentum), momentum


def near_kernel(first, kept, come, *refs):
    out = refs[-1]
    rows = kept.shape[1]
    if first:
        out[0, :rows] = kept[2] + come[2]
        out[0, rows:] = kept[3, :SPARE] + come[3, :SPARE]
    else:
        out[0] = kept[3, SPARE:] + come[3, SPARE:]


def half_step(half, states, sums, info, held):
    params, first, second = states
    kept, come, far, near = sums
    held_first, held_second = held
    rows = kept.shape[2]
    for lane in range(0, rows, LANES):
        lanes, there = pl.ds(lane, LANES), pl.ds(half * rows + lane, LANES)
        summed = kept[half, :, lanes] + come[half, :, lanes] + near(lanes) + far[0, :, lanes]
        inner, held_first[lanes, :], held_second[lanes, :] = adam(
            params[0, there, :], first[0, there, :], second[0, there, :], summed.T * info[1:2, :]
        )
        yield lanes, there, inner


def send(copies, sems, source, target):
    copies.append(pltpu.make_async_copy(source, target, sems.at[len(copies)]))
    copies[-1].start()


def left_kernel(
    params,
    first,
    second,
    kept,
    come,
    far,
    near,
    info,
    scale,
    global_fragment,
    outer_momentum,
    drift,
    other_drift,
    mix,
    new_params,
    new_first,
    new_second,
    new_global,
    new_momentum,
    held_params,
    held_first,
    held_second,
    held_global,
    held_momentum,
    spread,
    sems,
):
    copies = []
    fresh, momentum = outer((drift[...] + other_drift[...]) * info[2:3, :], global_fragment[...], outer_momentum[...])
    held_global[...] = fresh
    held_momentum[...] = momentum
    send(copies, sems, held_global, new_global)
    send(copies, sems, held_momentum, new_momentum)
    for at in range(FRAGS):
        spread[pl.ds(at, fresh.shape[0], stride=FRAGS), :] = fresh
    for lanes, there, value in half_step(
        0, (params, first, second), (kept, come, far, lambda lanes: near[0, : kept.shape[1], lanes]), info, (held_first, held_second)
    ):
        held_params[lanes, :] = scale[there, :] * value + (1.0 - scale[there, :]) * spread[there, :]
        for source, target in ((held_first, new_first), (held_second, new_second), (held_params, new_params)):
            send(copies, sems, source.at[lanes], target.at[0, there])
    right = pl.ds(mix.shape[0], mix.shape[0])
    mix[...] = (1.0 - scale[right, :]) * spread[right, :]
    for copy in copies:
        copy.wait()


def right_kernel(
    params,
    first,
    second,
    kept,
    come,
    far,
    near,
    other_near,
    info,
    scale,
    mix,
    left_params,
    left_first,
    left_second,
    new_params,
    new_first,
    new_second,
    held_params,
    held_first,
    held_second,
    sems,
):
    del left_params, left_first, left_second
    copies = []

    def joined(lanes):
        return jnp.concatenate([near[0, kept.shape[1] :, lanes], other_near[0, :, lanes]])

    for lanes, there, value in half_step(
        1, (params, first, second), (kept, come, far, joined), info, (held_first, held_second)
    ):
        held_params[lanes, :] = scale[there, :] * value + mix[lanes, :]
        for source, target in ((held_first, new_first), (held_second, new_second), (held_params, new_params)):
            send(copies, sems, source.at[lanes], target.at[0, there])
    for copy in copies:
        copy.wait()


def hop(value, axis, devices, bit):
    return lax.ppermute(value, axis, [(d, d ^ bit) for d in range(devices)])


def doubling_sum(value, axis, devices):
    bit = devices // 2
    while bit:
        value = value + hop(value, axis, devices, bit)
        bit //= 2
    return value


def fast_body(mesh):
    workers, devices = mesh.shape["worker"], mesh.shape["fsdp"]

    def body(
        params, first, second, global_fragment, outer_momentum, features, cotangent, token_counts, fragment_index
    ):
        rows, width = params.shape[1:]
        pieces, tokens = global_fragment.shape[0], features.shape[1]
        block = functools.partial(jax.ShapeDtypeStruct, dtype=jnp.float32)

        def cost(count):
            return pl.CostEstimate(
                flops=2 * count * tokens * rows * width,
                bytes_accessed=count * rows * (2 * tokens + 4 * width),
                transcendentals=0,
            )

        room = pltpu.CompilerParams(vmem_limit_bytes=ROOM)
        free = pl.CostEstimate(flops=0, bytes_accessed=0, transcendentals=0)
        far_counts, far_features, far_cotangent = (
            pltpu.with_memory_space_constraint(array, pltpu.HBM) for array in (token_counts, features, cotangent)
        )
        held_counts = pltpu.SMEM(token_counts.shape, token_counts.dtype)
        held_piece = pltpu.VMEM(global_fragment.shape, global_fragment.dtype)

        half = rows // 2
        away_far, kept_far, masked, info = pl.pallas_call(
            functools.partial(first_kernel, workers, (7, 6)),
            out_shape=[block((2, width, half))] * 2 + [jax.ShapeDtypeStruct((tokens, width), jnp.bfloat16), block((8, width))],
            in_specs=[HBM] * 3,
            out_specs=[VMEM] * 4,
            scratch_shapes=[
                held_counts,
                pltpu.VMEM(cotangent.shape, cotangent.dtype),
                pltpu.VMEM((2, tokens, rows), features.dtype),
                pltpu.SemaphoreType.DMA((4,)),
            ],
            compiler_params=room,
            cost_estimate=cost(2),
            name="far_products",
        )(far_counts, far_cotangent, far_features)
        away, kept = pl.pallas_call(
            rest_kernel,
            out_shape=[block((6, width, half))] * 2,
            in_specs=[VMEM] * 2,
            out_specs=[VMEM] * 2,
            compiler_params=room,
            cost_estimate=free,
            name="rest_products",
        )(masked, features)

        def add(*terms, name, count=1):
            picks = [pick for _, pick in terms]
            return pl.pallas_call(
                functools.partial(add_kernel, picks),
                out_shape=block((count, width, half)),
                in_specs=[ANY if pick is None else VMEM for pick in picks],
                out_specs=VMEM,
                compiler_params=room,
                cost_estimate=free,
                name=name,
            )(*(array for array, _ in terms))

        def part(number, count=1):
            return slice(number, number + count)

        def near_sum(first, after):
            return pl.pallas_call(
                functools.partial(near_kernel, first),
                out_shape=block((1, width + SPARE if first else width - SPARE, half)),
                in_specs=[VMEM, VMEM, ANY],
                out_specs=VMEM,
                compiler_params=room,
                cost_estimate=free,
                name="add_n1" if first else "add_n2",
            )(kept, come, after)

        state, piece = block(params.shape), block(global_fragment.shape)
        come_far = hop(away_far, "fsdp", devices, 1)
        sent = add((kept_far, part(0)), (come_far, part(0)), (fragment_index, None), name="add_a1")
        far_left = hop(sent, "fsdp", devices, 2)
        away, _ = lax.optimization_barrier((away, sent))
        come = hop(away, "fsdp", devices, 1)
        drift, scale = pl.pallas_call(
            drift_kernel,
            out_shape=[piece, block((rows, width))],
            in_specs=[VMEM, SMEM, VMEM, VMEM, ANY],
            out_specs=[VMEM] * 2,
            compiler_params=room,
            cost_estimate=free,
            name="drift",
        )(info, fragment_index, params, global_fragment, sent)
        sent = add((kept_far, part(1)), (come_far, part(1)), name="add_a2")
        far_right = hop(sent, "fsdp", devices, 2)
        passed = add((kept, part(4)), (come, part(4)), (far_left, part(0)), name="add_c1")
        far_left = hop(passed, "fsdp", devices, 4)
        near_left = near_sum(True, sent)
        far_right = add((kept, part(5)), (come, part(5)), (far_right, part(0)), (passed, None), name="add_c2")
        near_right = near_sum(False, far_right)
        drift, _ = lax.optimization_barrier((drift, sent))
        bit = workers // 2
        drifts = (drift, hop(drift, "worker", workers, bit))
        while bit > 1:
            bit //= 2
            drift = drifts[0] + drifts[1]
            drift, _ = lax.optimization_barrier((drift, near_right))
            drifts = (drift, hop(drift, "worker", workers, bit))
        near_left = hop(near_left, "fsdp", devices, 2)
        far_right = hop(far_right, "fsdp", devices, 4)
        near_right = hop(near_right, "fsdp", devices, 2)
        groups = half // LANES
        held_half = pltpu.VMEM((half, width), jnp.float32)
        mix, *results, new_global, new_momentum = pl.pallas_call(
            left_kernel,
            out_shape=[block((half, width)), state, state, state, piece, piece],
            in_specs=[VMEM] * 13,
            out_specs=[VMEM] + [HBM] * 5,
            scratch_shapes=[held_half] * 3
            + [held_piece] * 2
            + [pltpu.VMEM((rows, width), jnp.float32), pltpu.SemaphoreType.DMA((2 + 3 * groups,))],
            compiler_params=room,
            cost_estimate=pl.CostEstimate(
                flops=30 * half * width, bytes_accessed=40 * half * width, transcendentals=2 * half * width
            ),
            name="left_step",
        )(
            params,
            first,
            second,
            kept,
            come,
            far_left,
            near_left,
            info,
            scale,
            global_fragment,
            outer_momentum,
            *drifts,
        )
        new_params, new_first, new_second = pl.pallas_call(
            right_kernel,
            out_shape=[state] * 3,
            in_specs=[VMEM] * 11 + [HBM] * 3,
            out_specs=[HBM] * 3,
            input_output_aliases={11: 0, 12: 1, 13: 2},
            scratch_shapes=[held_half] * 3 + [pltpu.SemaphoreType.DMA((3 * groups,))],
            compiler_params=room,
            cost_estimate=free,
            name="right_step",
        )(params, first, second, kept, come, far_right, near_left, near_right, info, scale, mix, *results)
        return new_params, new_first, new_second, new_global, new_momentum

    return body


def plain_body(mesh):
    workers, devices = mesh.shape["worker"], mesh.shape["fsdp"]

    def body(
        params, first, second, global_fragment, outer_momentum, features, cotangent, token_counts, fragment_index
    ):
        rows, width = params.shape[1:]
        tokens = features.shape[1]
        me = lax.axis_index("fsdp")
        count = lax.dynamic_index_in_dim(token_counts, lax.axis_index("worker"), 0, keepdims=False)
        live = count.astype(jnp.float32)
        valid = (me * tokens + lax.iota(jnp.int32, tokens) < count)[:, None]
        masked = jnp.where(valid, cotangent[0], jnp.zeros_like(cotangent[0]))
        term = lax.dot_general(features[0], masked, (((0,), (0,)), ((), ())), preferred_element_type=jnp.float32)
        blocks = jnp.take(term.reshape(devices, rows, width), me ^ jnp.arange(devices, dtype=jnp.int32), axis=0)
        bit = 1
        while bit < devices:
            blocks = blocks.reshape(-1, 2, rows, width)
            blocks = blocks[:, 0] + hop(blocks[:, 1], "fsdp", devices, bit)
            bit *= 2
        gradient = blocks[0] / live
        grouped = (rows // FRAGS, FRAGS, width)
        old = lax.dynamic_index_in_dim(params[0].reshape(grouped), fragment_index[0], 1, keepdims=False)
        drift_sum = doubling_sum(live * (global_fragment - old), "worker", workers)
        total = jnp.sum(token_counts).astype(jnp.float32)
        fresh, momentum = outer(drift_sum / total, global_fragment, outer_momentum)
        inner, first_new, second_new = adam(params[0], first[0], second[0], gradient)
        inner = inner.reshape(grouped)
        piece = lax.dynamic_index_in_dim(inner, fragment_index[0], 1, keepdims=False)
        mixed = MIXING * fresh + (1.0 - MIXING) * piece
        merged = lax.dynamic_update_index_in_dim(inner, mixed, fragment_index[0], 1).reshape(rows, width)
        return merged[None], first_new[None], second_new[None], fresh, momentum

    return body


def solution(mesh):
    devices = mesh.shape["fsdp"]

    def pick(*arrays):
        rows = arrays[0].shape[1]
        body = fast_body(mesh) if devices == 8 and rows % LANES == 0 else plain_body(mesh)
        return body(*arrays)

    state = P("worker", "fsdp", None)
    piece = P("fsdp", None)
    return jax.shard_map(
        pick,
        mesh=mesh,
        in_specs=(state, state, state, piece, piece, state, state, P(), P()),
        out_specs=(state, state, state, piece, piece),
        check_vma=False,
    )
```

```python
import functools

import jax
import jax.numpy as jnp
from jax import lax
from jax.experimental import pallas as pl
from jax.experimental.pallas import tpu as pltpu
from jax.sharding import PartitionSpec as P

FRAGS = 4
LANES = 128
SPARE = 8

BETA_ONE = 0.9
BETA_TWO = 0.95
CORRECT_ONE = 0.6513216
CORRECT_TWO = 0.401263
ADAM_EPS = 1e-08
LEARN_RATE = 0.02
DECAY_RATE = 0.1
NESTEROV = 0.9
OUTER_RATE = 0.7
MIXING = 0.5

VMEM = pl.BlockSpec(memory_space=pltpu.VMEM)
SMEM = pl.BlockSpec(memory_space=pltpu.SMEM)
HBM = pl.BlockSpec(memory_space=pltpu.HBM)
ANY = pl.BlockSpec(memory_space=pl.ANY)
ROOM = 8 << 20


def masked_rows(live, cotangent):
    rows = lax.broadcasted_iota(jnp.int32, cotangent.shape, 0)
    return jnp.where(rows < live, cotangent.astype(jnp.float32), 0.0).astype(jnp.bfloat16)


def columns_of(relative, rows, start, size):
    return pl.ds(pl.multiple_of((lax.axis_index("fsdp") ^ relative) * rows + start, LANES), size)


def product(masked, features):
    return lax.dot_general(masked, features, (((0,), (0,)), ((), ())), preferred_element_type=jnp.float32)


def fetch(sources, targets, sems, start=0):
    copies = [
        pltpu.make_async_copy(source, target, sems.at[start + slot])
        for slot, (source, target) in enumerate(zip(sources, targets))
    ]
    for copy in copies:
        copy.start()
    return copies


def first_kernel(
    workers, order, counts, cotangent, features, away, kept, masked, info, counts_held, cot_held, held, sems
):
    half = away.shape[2]
    small = fetch((counts, cotangent), (counts_held, cot_held), sems)
    columns = [columns_of(q, 2 * half, 0, 2 * half) for q in order]
    blocks = fetch([features.at[0, :, c] for c in columns], [held.at[n] for n in range(len(order))], sems, len(small))
    for copy in small:
        copy.wait()
    tokens = cot_held.shape[1]
    live = counts_held[lax.axis_index("worker")] - lax.axis_index("fsdp") * tokens
    masked[...] = masked_rows(live, cot_held[0])
    count, total = counts_held[lax.axis_index("worker")], counts_held[0]
    for other in range(1, workers):
        total = total + counts_held[other]
    info[0:1, :] = jnp.full((1, info.shape[1]), count.astype(jnp.float32))
    info[1:2, :] = 1.0 / info[0:1, :]
    info[2:3, :] = 1.0 / jnp.full((1, info.shape[1]), total.astype(jnp.float32))
    for slot, into in enumerate((away, kept)):
        blocks[slot].wait()
        for side in (0, 1):
            into[side] = product(masked[...], held[slot, :, side * half : (side + 1) * half])


def rest_kernel(masked, features, *targets):
    half = targets[0].shape[2]
    places = [(4, 0, 0, 4), (4, 1, 0, 5), (2, 0, 0, 2), (2, 1, 0, 3), (0, 0, 0, 0), (0, 1, 0, 1)]
    for q, side, into, at in places:
        for core in (1, 0):
            columns = columns_of(q + core, 2 * half, side * half, half)
            targets[into + 1 - core][at] = product(masked[...], features[0, :, columns])


def drift_kernel(info, fragment, params, global_fragment, after, drift, scale):
    del after
    mine = pl.ds(fragment[0], drift.shape[0], stride=FRAGS)
    drift[...] = info[0:1, :] * (global_fragment[...] - params[0, mine, :])
    scale[...] = jnp.ones_like(scale)
    scale[mine, :] = jnp.full_like(drift, 1.0 - MIXING)


def add_kernel(picks, *refs):
    total = None
    for ref, pick in zip(refs, picks):
        if pick is not None:
            total = ref[pick] if total is None else total + ref[pick]
    refs[-1][...] = total


def adam(before, first, second, gradient):
    first_new = BETA_ONE * first + (1.0 - BETA_ONE) * gradient
    second_new = BETA_TWO * second + (1.0 - BETA_TWO) * gradient * gradient
    update = first_new * (1.0 / CORRECT_ONE) / (jnp.sqrt(second_new * (1.0 / CORRECT_TWO)) + ADAM_EPS)
    return before - LEARN_RATE * (update + DECAY_RATE * before), first_new, second_new


def outer(pseudo_grad, global_fragment, outer_momentum):
    momentum = NESTEROV * outer_momentum + pseudo_grad
    return global_fragment - OUTER_RATE * (pseudo_grad + NESTEROV * momentum), momentum


def near_kernel(first, kept, come, *refs):
    out = refs[-1]
    rows = kept.shape[1]
    if first:
        out[0, :rows] = kept[2] + come[2]
        out[0, rows:] = kept[3, :SPARE] + come[3, :SPARE]
    else:
        out[0] = kept[3, SPARE:] + come[3, SPARE:]


def half_step(half, states, sums, info, held):
    params, first, second = states
    kept, come, far, near = sums
    held_first, held_second = held
    rows = kept.shape[2]
    for lane in range(0, rows, LANES):
        lanes, there = pl.ds(lane, LANES), pl.ds(half * rows + lane, LANES)
        summed = kept[half, :, lanes] + come[half, :, lanes] + near(lanes) + far[0, :, lanes]
        inner, held_first[lanes, :], held_second[lanes, :] = adam(
            params[0, there, :], first[0, there, :], second[0, there, :], summed.T * info[1:2, :]
        )
        yield lanes, there, inner


def send(copies, sems, source, target):
    copies.append(pltpu.make_async_copy(source, target, sems.at[len(copies)]))
    copies[-1].start()


def left_kernel(
    params, first, second, kept, come, far, near, info, inner, new_first, new_second, held_first, held_second, sems
):
    copies = []
    for lanes, there, value in half_step(
        0,
        (params, first, second),
        (kept, come, far, lambda lanes: near[0, : kept.shape[1], lanes]),
        info,
        (held_first, held_second),
    ):
        inner[lanes, :] = value
        for source, target in ((held_first, new_first), (held_second, new_second)):
            send(copies, sems, source.at[lanes], target.at[0, there])
    for copy in copies:
        copy.wait()


def right_kernel(
    params,
    first,
    second,
    kept,
    come,
    far,
    near,
    other_near,
    info,
    scale,
    inner,
    global_fragment,
    outer_momentum,
    drift,
    other_drift,
    left_first,
    left_second,
    new_params,
    new_first,
    new_second,
    new_global,
    new_momentum,
    held_params,
    held_first,
    held_second,
    held_global,
    held_momentum,
    spread,
    sems,
):
    del left_first, left_second
    copies = []
    fresh, momentum = outer((drift[...] + other_drift[...]) * info[2:3, :], global_fragment[...], outer_momentum[...])
    held_global[...] = fresh
    held_momentum[...] = momentum
    for at in range(FRAGS):
        spread[pl.ds(at, fresh.shape[0], stride=FRAGS), :] = fresh

    def mixed(there, value):
        held_params[there, :] = scale[there, :] * value + (1.0 - scale[there, :]) * spread[there, :]

    left = pl.ds(0, inner.shape[0])
    mixed(left, inner[...])
    send(copies, sems, held_params.at[left], new_params.at[0, left])

    def joined(lanes):
        return jnp.concatenate([near[0, kept.shape[1] :, lanes], other_near[0, :, lanes]])

    for lanes, there, value in half_step(
        1, (params, first, second), (kept, come, far, joined), info, (held_first, held_second)
    ):
        mixed(there, value)
        for source, target in (
            (held_first.at[lanes], new_first),
            (held_second.at[lanes], new_second),
            (held_params.at[there], new_params),
        ):
            send(copies, sems, source, target.at[0, there])
    send(copies, sems, held_global, new_global)
    send(copies, sems, held_momentum, new_momentum)
    for copy in copies:
        copy.wait()


def hop(value, axis, devices, bit):
    return lax.ppermute(value, axis, [(d, d ^ bit) for d in range(devices)])


def doubling_sum(value, axis, devices):
    bit = devices // 2
    while bit:
        value = value + hop(value, axis, devices, bit)
        bit //= 2
    return value


def fast_body(mesh):
    workers, devices = mesh.shape["worker"], mesh.shape["fsdp"]

    def body(
        params, first, second, global_fragment, outer_momentum, features, cotangent, token_counts, fragment_index
    ):
        rows, width = params.shape[1:]
        pieces, tokens = global_fragment.shape[0], features.shape[1]
        block = functools.partial(jax.ShapeDtypeStruct, dtype=jnp.float32)

        def cost(count):
            return pl.CostEstimate(
                flops=2 * count * tokens * rows * width,
                bytes_accessed=count * rows * (2 * tokens + 4 * width),
                transcendentals=0,
            )

        room = pltpu.CompilerParams(vmem_limit_bytes=ROOM)
        free = pl.CostEstimate(flops=0, bytes_accessed=0, transcendentals=0)
        far_counts, far_features, far_cotangent = (
            pltpu.with_memory_space_constraint(array, pltpu.HBM) for array in (token_counts, features, cotangent)
        )
        held_counts = pltpu.SMEM(token_counts.shape, token_counts.dtype)
        held_piece = pltpu.VMEM(global_fragment.shape, global_fragment.dtype)

        half = rows // 2
        away_far, kept_far, masked, info = pl.pallas_call(
            functools.partial(first_kernel, workers, (7, 6)),
            out_shape=[block((2, width, half))] * 2 + [jax.ShapeDtypeStruct((tokens, width), jnp.bfloat16), block((8, width))],
            in_specs=[HBM] * 3,
            out_specs=[VMEM] * 4,
            scratch_shapes=[
                held_counts,
                pltpu.VMEM(cotangent.shape, cotangent.dtype),
                pltpu.VMEM((2, tokens, rows), features.dtype),
                pltpu.SemaphoreType.DMA((4,)),
            ],
            compiler_params=room,
            cost_estimate=cost(2),
            name="far_products",
        )(far_counts, far_cotangent, far_features)
        away, kept = pl.pallas_call(
            rest_kernel,
            out_shape=[block((6, width, half))] * 2,
            in_specs=[VMEM] * 2,
            out_specs=[VMEM] * 2,
            compiler_params=room,
            cost_estimate=free,
            name="rest_products",
        )(masked, features)

        def add(*terms, name, count=1):
            picks = [pick for _, pick in terms]
            return pl.pallas_call(
                functools.partial(add_kernel, picks),
                out_shape=block((count, width, half)),
                in_specs=[ANY if pick is None else VMEM for pick in picks],
                out_specs=VMEM,
                compiler_params=room,
                cost_estimate=free,
                name=name,
            )(*(array for array, _ in terms))

        def part(number, count=1):
            return slice(number, number + count)

        def near_sum(first, after):
            return pl.pallas_call(
                functools.partial(near_kernel, first),
                out_shape=block((1, width + SPARE if first else width - SPARE, half)),
                in_specs=[VMEM, VMEM, ANY],
                out_specs=VMEM,
                compiler_params=room,
                cost_estimate=free,
                name="add_n1" if first else "add_n2",
            )(kept, come, after)

        state, piece = block(params.shape), block(global_fragment.shape)
        come_far = hop(away_far, "fsdp", devices, 1)
        sent = add((kept_far, part(0)), (come_far, part(0)), name="add_a1")
        far_left = hop(sent, "fsdp", devices, 2)
        away, _ = lax.optimization_barrier((away, sent))
        come = hop(away, "fsdp", devices, 1)
        drift, scale = pl.pallas_call(
            drift_kernel,
            out_shape=[piece, block((rows, width))],
            in_specs=[VMEM, SMEM, VMEM, VMEM, ANY],
            out_specs=[VMEM] * 2,
            compiler_params=room,
            cost_estimate=free,
            name="drift",
        )(info, fragment_index, params, global_fragment, sent)
        sent = add((kept_far, part(1)), (come_far, part(1)), (drift, None), name="add_a2")
        far_right = hop(sent, "fsdp", devices, 2)
        passed = add((kept, part(4)), (come, part(4)), (far_left, part(0)), name="add_c1")
        far_left = hop(passed, "fsdp", devices, 4)
        near_left = near_sum(True, sent)
        far_right = add((kept, part(5)), (come, part(5)), (far_right, part(0)), (passed, None), name="add_c2")
        near_right = near_sum(False, far_right)
        drift, _ = lax.optimization_barrier((drift, sent))
        bit = workers // 2
        drifts = (drift, hop(drift, "worker", workers, bit))
        while bit > 1:
            bit //= 2
            drift = drifts[0] + drifts[1]
            drift, _ = lax.optimization_barrier((drift, near_right))
            drifts = (drift, hop(drift, "worker", workers, bit))
        near_left = hop(near_left, "fsdp", devices, 2)
        far_right = hop(far_right, "fsdp", devices, 4)
        near_right = hop(near_right, "fsdp", devices, 2)
        groups = half // LANES
        held_half = pltpu.VMEM((half, width), jnp.float32)
        inner, new_first, new_second = pl.pallas_call(
            left_kernel,
            out_shape=[block((half, width)), state, state],
            in_specs=[VMEM] * 8,
            out_specs=[VMEM] + [HBM] * 2,
            scratch_shapes=[held_half] * 2 + [pltpu.SemaphoreType.DMA((2 * groups,))],
            compiler_params=room,
            cost_estimate=pl.CostEstimate(
                flops=30 * half * width, bytes_accessed=40 * half * width, transcendentals=2 * half * width
            ),
            name="left_step",
        )(params, first, second, kept, come, far_left, near_left, info)
        new_params, new_first, new_second, new_global, new_momentum = pl.pallas_call(
            right_kernel,
            out_shape=[state] * 3 + [piece] * 2,
            in_specs=[VMEM] * 15 + [HBM] * 2,
            out_specs=[HBM] * 5,
            input_output_aliases={15: 1, 16: 2},
            scratch_shapes=[pltpu.VMEM((rows, width), jnp.float32)]
            + [held_half] * 2
            + [held_piece] * 2
            + [pltpu.VMEM((rows, width), jnp.float32), pltpu.SemaphoreType.DMA((3 + 3 * groups,))],
            compiler_params=room,
            cost_estimate=free,
            name="right_step",
        )(
            params,
            first,
            second,
            kept,
            come,
            far_right,
            near_left,
            near_right,
            info,
            scale,
            inner,
            global_fragment,
            outer_momentum,
            *drifts,
            new_first,
            new_second,
        )
        return new_params, new_first, new_second, new_global, new_momentum

    return body


def plain_body(mesh):
    workers, devices = mesh.shape["worker"], mesh.shape["fsdp"]

    def body(
        params, first, second, global_fragment, outer_momentum, features, cotangent, token_counts, fragment_index
    ):
        rows, width = params.shape[1:]
        tokens = features.shape[1]
        me = lax.axis_index("fsdp")
        count = lax.dynamic_index_in_dim(token_counts, lax.axis_index("worker"), 0, keepdims=False)
        live = count.astype(jnp.float32)
        valid = (me * tokens + lax.iota(jnp.int32, tokens) < count)[:, None]
        masked = jnp.where(valid, cotangent[0], jnp.zeros_like(cotangent[0]))
        term = lax.dot_general(features[0], masked, (((0,), (0,)), ((), ())), preferred_element_type=jnp.float32)
        blocks = jnp.take(term.reshape(devices, rows, width), me ^ jnp.arange(devices, dtype=jnp.int32), axis=0)
        bit = 1
        while bit < devices:
            blocks = blocks.reshape(-1, 2, rows, width)
            blocks = blocks[:, 0] + hop(blocks[:, 1], "fsdp", devices, bit)
            bit *= 2
        gradient = blocks[0] / live
        grouped = (rows // FRAGS, FRAGS, width)
        old = lax.dynamic_index_in_dim(params[0].reshape(grouped), fragment_index[0], 1, keepdims=False)
        drift_sum = doubling_sum(live * (global_fragment - old), "worker", workers)
        total = jnp.sum(token_counts).astype(jnp.float32)
        fresh, momentum = outer(drift_sum / total, global_fragment, outer_momentum)
        inner, first_new, second_new = adam(params[0], first[0], second[0], gradient)
        inner = inner.reshape(grouped)
        piece = lax.dynamic_index_in_dim(inner, fragment_index[0], 1, keepdims=False)
        mixed = MIXING * fresh + (1.0 - MIXING) * piece
        merged = lax.dynamic_update_index_in_dim(inner, mixed, fragment_index[0], 1).reshape(rows, width)
        return merged[None], first_new[None], second_new[None], fresh, momentum

    return body


def solution(mesh):
    devices = mesh.shape["fsdp"]

    def pick(*arrays):
        rows = arrays[0].shape[1]
        body = fast_body(mesh) if devices == 8 and rows % LANES == 0 else plain_body(mesh)
        return body(*arrays)

    state = P("worker", "fsdp", None)
    piece = P("fsdp", None)
    return jax.shard_map(
        pick,
        mesh=mesh,
        in_specs=(state, state, state, piece, piece, state, state, P(), P()),
        out_specs=(state, state, state, piece, piece),
        check_vma=False,
    )
```

```python
import functools

import jax
import jax.numpy as jnp
from jax import lax
from jax.experimental import pallas as pl
from jax.experimental.pallas import tpu as pltpu
from jax.sharding import PartitionSpec as P

FRAGS = 4
LANES = 128
SPARE = 8

BETA_ONE = 0.9
BETA_TWO = 0.95
CORRECT_ONE = 0.6513216
CORRECT_TWO = 0.401263
ADAM_EPS = 1e-08
LEARN_RATE = 0.02
DECAY_RATE = 0.1
NESTEROV = 0.9
OUTER_RATE = 0.7
MIXING = 0.5

VMEM = pl.BlockSpec(memory_space=pltpu.VMEM)
SMEM = pl.BlockSpec(memory_space=pltpu.SMEM)
HBM = pl.BlockSpec(memory_space=pltpu.HBM)
ANY = pl.BlockSpec(memory_space=pl.ANY)
ROOM = 8 << 20


def masked_rows(live, cotangent):
    rows = lax.broadcasted_iota(jnp.int32, cotangent.shape, 0)
    return jnp.where(rows < live, cotangent.astype(jnp.float32), 0.0).astype(jnp.bfloat16)


def columns_of(relative, rows, start, size):
    return pl.ds(pl.multiple_of((lax.axis_index("fsdp") ^ relative) * rows + start, LANES), size)


def product(masked, features):
    return lax.dot_general(masked, features, (((0,), (0,)), ((), ())), preferred_element_type=jnp.float32)


def fetch(sources, targets, sems, start=0):
    copies = [
        pltpu.make_async_copy(source, target, sems.at[start + slot])
        for slot, (source, target) in enumerate(zip(sources, targets))
    ]
    for copy in copies:
        copy.start()
    return copies


def first_kernel(
    workers, order, counts, cotangent, features, away, kept, masked, info, counts_held, cot_held, held, sems
):
    half = away.shape[2]
    small = fetch((counts, cotangent), (counts_held, cot_held), sems)
    columns = [columns_of(q, 2 * half, 0, 2 * half) for q in order]
    blocks = fetch([features.at[0, :, c] for c in columns], [held.at[n] for n in range(len(order))], sems, len(small))
    for copy in small:
        copy.wait()
    tokens = cot_held.shape[1]
    live = counts_held[lax.axis_index("worker")] - lax.axis_index("fsdp") * tokens
    masked[...] = masked_rows(live, cot_held[0])
    count, total = counts_held[lax.axis_index("worker")], counts_held[0]
    for other in range(1, workers):
        total = total + counts_held[other]
    info[0:1, :] = jnp.full((1, info.shape[1]), count.astype(jnp.float32))
    info[1:2, :] = 1.0 / info[0:1, :]
    info[2:3, :] = 1.0 / jnp.full((1, info.shape[1]), total.astype(jnp.float32))
    for slot, into in enumerate((away, kept)):
        blocks[slot].wait()
        for side in (0, 1):
            into[side, : masked.shape[1]] = product(masked[...], held[slot, :, side * half : (side + 1) * half])
    away[:, masked.shape[1] :] = jnp.zeros((2, SPARE, half), jnp.float32)


def rest_kernel(masked, features, *targets):
    half = targets[0].shape[2]
    places = [(4, 0, 0, 0), (4, 1, 0, 1), (0, 1, 0, 2), (2, 0, 2, 1), (2, 1, 2, 2), (0, 0, 2, 0)]
    for q, side, into, at in places:
        for core in (1, 0):
            columns = columns_of(q + core, 2 * half, side * half, half)
            targets[into + 1 - core][at] = product(masked[...], features[0, :, columns])


def drift_kernel(info, fragment, params, global_fragment, after, drift, scale):
    del after
    mine = pl.ds(fragment[0], drift.shape[0], stride=FRAGS)
    drift[...] = info[0:1, :] * (global_fragment[...] - params[0, mine, :])
    scale[...] = jnp.ones_like(scale)
    scale[mine, :] = jnp.full_like(drift, 1.0 - MIXING)


def add_kernel(picks, *refs):
    total = None
    for ref, pick in zip(refs, picks):
        if pick is not None:
            total = ref[pick] if total is None else total + ref[pick]
    refs[-1][...] = total


def adam(before, first, second, gradient):
    first_new = BETA_ONE * first + (1.0 - BETA_ONE) * gradient
    second_new = BETA_TWO * second + (1.0 - BETA_TWO) * gradient * gradient
    update = first_new * (1.0 / CORRECT_ONE) / (jnp.sqrt(second_new * (1.0 / CORRECT_TWO)) + ADAM_EPS)
    return before - LEARN_RATE * (update + DECAY_RATE * before), first_new, second_new


def outer(pseudo_grad, global_fragment, outer_momentum):
    momentum = NESTEROV * outer_momentum + pseudo_grad
    return global_fragment - OUTER_RATE * (pseudo_grad + NESTEROV * momentum), momentum


def half_step(half, states, sums, info, held):
    params, first, second = states
    kept, come, far, near = sums
    held_first, held_second = held
    rows = kept.shape[2]
    for lane in range(0, rows, LANES):
        lanes, there = pl.ds(lane, LANES), pl.ds(half * rows + lane, LANES)
        summed = kept[2 * half, :, lanes] + come[2 * half, :, lanes] + near[0, :, lanes] + far[0, :, lanes]
        inner, held_first[lanes, :], held_second[lanes, :] = adam(
            params[0, there, :], first[0, there, :], second[0, there, :], summed.T * info[1:2, :]
        )
        yield lanes, there, inner


def send(copies, sems, source, target):
    copies.append(pltpu.make_async_copy(source, target, sems.at[len(copies)]))
    copies[-1].start()


def left_kernel(
    params,
    first,
    second,
    kept,
    come,
    far,
    near,
    info,
    scale,
    global_fragment,
    outer_momentum,
    drift,
    other_drift,
    mix,
    new_params,
    new_first,
    new_second,
    new_global,
    new_momentum,
    held_params,
    held_first,
    held_second,
    held_global,
    held_momentum,
    spread,
    sems,
):
    copies = []
    fresh, momentum = outer((drift[...] + other_drift[...]) * info[2:3, :], global_fragment[...], outer_momentum[...])
    held_global[...] = fresh
    held_momentum[...] = momentum
    send(copies, sems, held_global, new_global)
    send(copies, sems, held_momentum, new_momentum)
    for at in range(FRAGS):
        spread[pl.ds(at, fresh.shape[0], stride=FRAGS), :] = fresh
    for lanes, there, value in half_step(
        0, (params, first, second), (kept, come, far, near), info, (held_first, held_second)
    ):
        held_params[lanes, :] = scale[there, :] * value + (1.0 - scale[there, :]) * spread[there, :]
        for source, target in ((held_first, new_first), (held_second, new_second), (held_params, new_params)):
            send(copies, sems, source.at[lanes], target.at[0, there])
    right = pl.ds(mix.shape[0], mix.shape[0])
    mix[...] = (1.0 - scale[right, :]) * spread[right, :]
    for copy in copies:
        copy.wait()


def right_kernel(
    params,
    first,
    second,
    kept,
    come,
    far,
    near,
    info,
    scale,
    mix,
    left_params,
    left_first,
    left_second,
    new_params,
    new_first,
    new_second,
    held_params,
    held_first,
    held_second,
    sems,
):
    del left_params, left_first, left_second
    copies = []
    for lanes, there, value in half_step(
        1, (params, first, second), (kept, come, far, near), info, (held_first, held_second)
    ):
        held_params[lanes, :] = scale[there, :] * value + mix[lanes, :]
        for source, target in ((held_first, new_first), (held_second, new_second), (held_params, new_params)):
            send(copies, sems, source.at[lanes], target.at[0, there])
    for copy in copies:
        copy.wait()


def hop(value, axis, devices, bit):
    return lax.ppermute(value, axis, [(d, d ^ bit) for d in range(devices)])


def doubling_sum(value, axis, devices):
    bit = devices // 2
    while bit:
        value = value + hop(value, axis, devices, bit)
        bit //= 2
    return value


def fast_body(mesh):
    workers, devices = mesh.shape["worker"], mesh.shape["fsdp"]

    def body(
        params, first, second, global_fragment, outer_momentum, features, cotangent, token_counts, fragment_index
    ):
        rows, width = params.shape[1:]
        pieces, tokens = global_fragment.shape[0], features.shape[1]
        block = functools.partial(jax.ShapeDtypeStruct, dtype=jnp.float32)

        def cost(count):
            return pl.CostEstimate(
                flops=2 * count * tokens * rows * width,
                bytes_accessed=count * rows * (2 * tokens + 4 * width),
                transcendentals=0,
            )

        room = pltpu.CompilerParams(vmem_limit_bytes=ROOM)
        free = pl.CostEstimate(flops=0, bytes_accessed=0, transcendentals=0)
        far_counts, far_features, far_cotangent = (
            pltpu.with_memory_space_constraint(array, pltpu.HBM) for array in (token_counts, features, cotangent)
        )
        held_counts = pltpu.SMEM(token_counts.shape, token_counts.dtype)
        held_piece = pltpu.VMEM(global_fragment.shape, global_fragment.dtype)

        half = rows // 2
        away_far, kept_far, masked, info = pl.pallas_call(
            functools.partial(first_kernel, workers, (7, 6)),
            out_shape=[
                block((2, width + SPARE, half)),
                block((2, width, half)),
                jax.ShapeDtypeStruct((tokens, width), jnp.bfloat16),
                block((8, width)),
            ],
            in_specs=[HBM] * 3,
            out_specs=[VMEM] * 4,
            scratch_shapes=[
                held_counts,
                pltpu.VMEM(cotangent.shape, cotangent.dtype),
                pltpu.VMEM((2, tokens, rows), features.dtype),
                pltpu.SemaphoreType.DMA((4,)),
            ],
            compiler_params=room,
            cost_estimate=cost(2),
            name="far_products",
        )(far_counts, far_cotangent, far_features)
        away_pass, kept_pass, away, kept = pl.pallas_call(
            rest_kernel,
            out_shape=[block((3, width, half))] * 4,
            in_specs=[VMEM] * 2,
            out_specs=[VMEM] * 4,
            compiler_params=room,
            cost_estimate=free,
            name="rest_products",
        )(masked, features)

        def add(*terms, name, count=1):
            picks = [pick for _, pick in terms]
            return pl.pallas_call(
                functools.partial(add_kernel, picks),
                out_shape=block((count, width, half)),
                in_specs=[ANY if pick is None else VMEM for pick in picks],
                out_specs=VMEM,
                compiler_params=room,
                cost_estimate=free,
                name=name,
            )(*(array for array, _ in terms))

        def part(number, count=1):
            return slice(number, number + count)

        state, piece = block(params.shape), block(global_fragment.shape)
        come_far = hop(away_far, "fsdp", devices, 1)
        sent = add((kept_far, part(0)), (come_far, (part(0), part(0, width))), name="add_a1")
        far_left = hop(sent, "fsdp", devices, 2)
        come_pass = hop(away_pass, "fsdp", devices, 1)
        come = hop(away, "fsdp", devices, 1)
        drift, scale = pl.pallas_call(
            drift_kernel,
            out_shape=[piece, block((rows, width))],
            in_specs=[VMEM, SMEM, VMEM, VMEM, ANY],
            out_specs=[VMEM] * 2,
            compiler_params=room,
            cost_estimate=free,
            name="drift",
        )(info, fragment_index, params, global_fragment, sent)
        sent = add((kept_far, part(1)), (come_far, (part(1), part(0, width))), (drift, None), name="add_a2")
        far_right = hop(sent, "fsdp", devices, 2)
        passed = add((kept_pass, part(0)), (come_pass, part(0)), (far_left, part(0)), name="add_c1")
        far_left = hop(passed, "fsdp", devices, 4)
        near_left = add((kept, part(1)), (come, part(1)), (passed, None), name="add_n1")
        far_right = add((kept_pass, part(1)), (come_pass, part(1)), (far_right, part(0)), (passed, None), name="add_c2")
        near_right = add((kept, part(2)), (come, part(2)), (far_right, None), name="add_n2")
        drift, _ = lax.optimization_barrier((drift, sent))
        bit = workers // 2
        drifts = (drift, hop(drift, "worker", workers, bit))
        while bit > 1:
            bit //= 2
            drift = drifts[0] + drifts[1]
            drift, _ = lax.optimization_barrier((drift, near_right))
            drifts = (drift, hop(drift, "worker", workers, bit))
        near_left = hop(near_left, "fsdp", devices, 2)
        far_right = hop(far_right, "fsdp", devices, 4)
        near_right = hop(near_right, "fsdp", devices, 2)
        groups = half // LANES
        held_half = pltpu.VMEM((half, width), jnp.float32)
        mix, *results, new_global, new_momentum = pl.pallas_call(
            left_kernel,
            out_shape=[block((half, width)), state, state, state, piece, piece],
            in_specs=[VMEM] * 13,
            out_specs=[VMEM] + [HBM] * 5,
            scratch_shapes=[held_half] * 3
            + [held_piece] * 2
            + [pltpu.VMEM((rows, width), jnp.float32), pltpu.SemaphoreType.DMA((2 + 3 * groups,))],
            compiler_params=room,
            cost_estimate=pl.CostEstimate(
                flops=30 * half * width, bytes_accessed=40 * half * width, transcendentals=2 * half * width
            ),
            name="left_step",
        )(
            params,
            first,
            second,
            kept,
            come,
            far_left,
            near_left,
            info,
            scale,
            global_fragment,
            outer_momentum,
            *drifts,
        )
        new_params, new_first, new_second = pl.pallas_call(
            right_kernel,
            out_shape=[state] * 3,
            in_specs=[VMEM] * 10 + [HBM] * 3,
            out_specs=[HBM] * 3,
            input_output_aliases={10: 0, 11: 1, 12: 2},
            scratch_shapes=[held_half] * 3 + [pltpu.SemaphoreType.DMA((3 * groups,))],
            compiler_params=room,
            cost_estimate=free,
            name="right_step",
        )(params, first, second, kept_pass, come_pass, far_right, near_right, info, scale, mix, *results)
        return new_params, new_first, new_second, new_global, new_momentum

    return body


def plain_body(mesh):
    workers, devices = mesh.shape["worker"], mesh.shape["fsdp"]

    def body(
        params, first, second, global_fragment, outer_momentum, features, cotangent, token_counts, fragment_index
    ):
        rows, width = params.shape[1:]
        tokens = features.shape[1]
        me = lax.axis_index("fsdp")
        count = lax.dynamic_index_in_dim(token_counts, lax.axis_index("worker"), 0, keepdims=False)
        live = count.astype(jnp.float32)
        valid = (me * tokens + lax.iota(jnp.int32, tokens) < count)[:, None]
        masked = jnp.where(valid, cotangent[0], jnp.zeros_like(cotangent[0]))
        term = lax.dot_general(features[0], masked, (((0,), (0,)), ((), ())), preferred_element_type=jnp.float32)
        blocks = jnp.take(term.reshape(devices, rows, width), me ^ jnp.arange(devices, dtype=jnp.int32), axis=0)
        bit = 1
        while bit < devices:
            blocks = blocks.reshape(-1, 2, rows, width)
            blocks = blocks[:, 0] + hop(blocks[:, 1], "fsdp", devices, bit)
            bit *= 2
        gradient = blocks[0] / live
        grouped = (rows // FRAGS, FRAGS, width)
        old = lax.dynamic_index_in_dim(params[0].reshape(grouped), fragment_index[0], 1, keepdims=False)
        drift_sum = doubling_sum(live * (global_fragment - old), "worker", workers)
        total = jnp.sum(token_counts).astype(jnp.float32)
        fresh, momentum = outer(drift_sum / total, global_fragment, outer_momentum)
        inner, first_new, second_new = adam(params[0], first[0], second[0], gradient)
        inner = inner.reshape(grouped)
        piece = lax.dynamic_index_in_dim(inner, fragment_index[0], 1, keepdims=False)
        mixed = MIXING * fresh + (1.0 - MIXING) * piece
        merged = lax.dynamic_update_index_in_dim(inner, mixed, fragment_index[0], 1).reshape(rows, width)
        return merged[None], first_new[None], second_new[None], fresh, momentum

    return body


def solution(mesh):
    devices = mesh.shape["fsdp"]

    def pick(*arrays):
        rows = arrays[0].shape[1]
        body = fast_body(mesh) if devices == 8 and rows % LANES == 0 else plain_body(mesh)
        return body(*arrays)

    state = P("worker", "fsdp", None)
    piece = P("fsdp", None)
    return jax.shard_map(
        pick,
        mesh=mesh,
        in_specs=(state, state, state, piece, piece, state, state, P(), P()),
        out_specs=(state, state, state, piece, piece),
        check_vma=False,
    )
```

```python
import functools

import jax
import jax.numpy as jnp
from jax import lax
from jax.experimental import pallas as pl
from jax.experimental.pallas import tpu as pltpu
from jax.sharding import PartitionSpec as P

FRAGS = 4
LANES = 128
SPARE = 8

BETA_ONE = 0.9
BETA_TWO = 0.95
CORRECT_ONE = 0.6513216
CORRECT_TWO = 0.401263
ADAM_EPS = 1e-08
LEARN_RATE = 0.02
DECAY_RATE = 0.1
NESTEROV = 0.9
OUTER_RATE = 0.7
MIXING = 0.5

VMEM = pl.BlockSpec(memory_space=pltpu.VMEM)
SMEM = pl.BlockSpec(memory_space=pltpu.SMEM)
HBM = pl.BlockSpec(memory_space=pltpu.HBM)
ANY = pl.BlockSpec(memory_space=pl.ANY)
ROOM = 8 << 20


def masked_rows(live, cotangent):
    rows = lax.broadcasted_iota(jnp.int32, cotangent.shape, 0)
    return jnp.where(rows < live, cotangent.astype(jnp.float32), 0.0).astype(jnp.bfloat16)


def columns_of(relative, rows, start, size):
    return pl.ds(pl.multiple_of((lax.axis_index("fsdp") ^ relative) * rows + start, LANES), size)


def product(masked, features):
    return lax.dot_general(masked, features, (((0,), (0,)), ((), ())), preferred_element_type=jnp.float32)


def fetch(sources, targets, sems, start=0):
    copies = [
        pltpu.make_async_copy(source, target, sems.at[start + slot])
        for slot, (source, target) in enumerate(zip(sources, targets))
    ]
    for copy in copies:
        copy.start()
    return copies


def first_kernel(
    workers, order, counts, cotangent, features, away, kept, masked, info, counts_held, cot_held, held, sems
):
    half = away.shape[2]
    small = fetch((counts, cotangent), (counts_held, cot_held), sems)
    columns = [columns_of(q, 2 * half, 0, 2 * half) for q in order]
    blocks = fetch([features.at[0, :, c] for c in columns], [held.at[n] for n in range(len(order))], sems, len(small))
    for copy in small:
        copy.wait()
    tokens = cot_held.shape[1]
    live = counts_held[lax.axis_index("worker")] - lax.axis_index("fsdp") * tokens
    masked[...] = masked_rows(live, cot_held[0])
    count, total = counts_held[lax.axis_index("worker")], counts_held[0]
    for other in range(1, workers):
        total = total + counts_held[other]
    info[0:1, :] = jnp.full((1, info.shape[1]), count.astype(jnp.float32))
    info[1:2, :] = 1.0 / info[0:1, :]
    info[2:3, :] = 1.0 / jnp.full((1, info.shape[1]), total.astype(jnp.float32))
    for slot, into in enumerate((away, kept)):
        blocks[slot].wait()
        for side in (0, 1):
            into[side, : masked.shape[1]] = product(masked[...], held[slot, :, side * half : (side + 1) * half])
    away[:, masked.shape[1] :] = jnp.zeros((2, SPARE, half), jnp.float32)


def rest_kernel(masked, features, *targets):
    half = targets[0].shape[2]
    places = [(4, 0, 0, 0), (4, 1, 0, 1), (0, 1, 0, 2), (2, 0, 2, 1), (2, 1, 2, 2), (0, 0, 2, 0)]
    for q, side, into, at in places:
        for core in (1, 0):
            columns = columns_of(q + core, 2 * half, side * half, half)
            targets[into + 1 - core][at] = product(masked[...], features[0, :, columns])


def drift_kernel(info, fragment, params, global_fragment, after, drift, scale):
    del after
    mine = pl.ds(fragment[0], drift.shape[0], stride=FRAGS)
    drift[...] = info[0:1, :] * (global_fragment[...] - params[0, mine, :])
    scale[...] = jnp.ones_like(scale)
    scale[mine, :] = jnp.full_like(drift, 1.0 - MIXING)


def add_kernel(picks, *refs):
    total = None
    for ref, pick in zip(refs, picks):
        if pick is not None:
            total = ref[pick] if total is None else total + ref[pick]
    refs[-1][...] = total


def adam(before, first, second, gradient):
    first_new = BETA_ONE * first + (1.0 - BETA_ONE) * gradient
    second_new = BETA_TWO * second + (1.0 - BETA_TWO) * gradient * gradient
    update = first_new * (1.0 / CORRECT_ONE) / (jnp.sqrt(second_new * (1.0 / CORRECT_TWO)) + ADAM_EPS)
    return before - LEARN_RATE * (update + DECAY_RATE * before), first_new, second_new


def outer(pseudo_grad, global_fragment, outer_momentum):
    momentum = NESTEROV * outer_momentum + pseudo_grad
    return global_fragment - OUTER_RATE * (pseudo_grad + NESTEROV * momentum), momentum


def half_step(half, states, sums, info, held):
    params, first, second = states
    kept, come, far, near = sums
    held_first, held_second = held
    rows = kept.shape[2]
    for lane in range(0, rows, LANES):
        lanes, there = pl.ds(lane, LANES), pl.ds(half * rows + lane, LANES)
        summed = kept[2 * half, :, lanes] + come[2 * half, :, lanes] + near[0, :, lanes] + far[0, :, lanes]
        inner, held_first[lanes, :], held_second[lanes, :] = adam(
            params[0, there, :], first[0, there, :], second[0, there, :], summed.T * info[1:2, :]
        )
        yield lanes, there, inner


def send(copies, sems, source, target):
    copies.append(pltpu.make_async_copy(source, target, sems.at[len(copies)]))
    copies[-1].start()


def left_kernel(
    params,
    first,
    second,
    kept,
    come,
    far,
    near,
    info,
    scale,
    global_fragment,
    outer_momentum,
    drift,
    other_drift,
    mix,
    new_params,
    new_first,
    new_second,
    new_global,
    new_momentum,
    held_params,
    held_first,
    held_second,
    held_global,
    held_momentum,
    spread,
    sems,
):
    copies = []
    fresh, momentum = outer((drift[...] + other_drift[...]) * info[2:3, :], global_fragment[...], outer_momentum[...])
    held_global[...] = fresh
    held_momentum[...] = momentum
    send(copies, sems, held_global, new_global)
    send(copies, sems, held_momentum, new_momentum)
    for at in range(FRAGS):
        spread[pl.ds(at, fresh.shape[0], stride=FRAGS), :] = fresh
    for lanes, there, value in half_step(
        0, (params, first, second), (kept, come, far, near), info, (held_first, held_second)
    ):
        held_params[lanes, :] = scale[there, :] * value + (1.0 - scale[there, :]) * spread[there, :]
        for source, target in ((held_first, new_first), (held_second, new_second), (held_params, new_params)):
            send(copies, sems, source.at[lanes], target.at[0, there])
    right = pl.ds(mix.shape[0], mix.shape[0])
    mix[...] = (1.0 - scale[right, :]) * spread[right, :]
    for copy in copies:
        copy.wait()


def right_kernel(
    params,
    first,
    second,
    kept,
    come,
    far,
    near,
    info,
    scale,
    mix,
    left_params,
    left_first,
    left_second,
    new_params,
    new_first,
    new_second,
    held_params,
    held_first,
    held_second,
    sems,
):
    del left_params, left_first, left_second
    copies = []
    for lanes, there, value in half_step(
        1, (params, first, second), (kept, come, far, near), info, (held_first, held_second)
    ):
        held_params[lanes, :] = scale[there, :] * value + mix[lanes, :]
        for source, target in ((held_first, new_first), (held_second, new_second), (held_params, new_params)):
            send(copies, sems, source.at[lanes], target.at[0, there])
    for copy in copies:
        copy.wait()


def hop(value, axis, devices, bit):
    return lax.ppermute(value, axis, [(d, d ^ bit) for d in range(devices)])


def doubling_sum(value, axis, devices):
    bit = devices // 2
    while bit:
        value = value + hop(value, axis, devices, bit)
        bit //= 2
    return value


def fast_body(mesh):
    workers, devices = mesh.shape["worker"], mesh.shape["fsdp"]

    def body(
        params, first, second, global_fragment, outer_momentum, features, cotangent, token_counts, fragment_index
    ):
        rows, width = params.shape[1:]
        pieces, tokens = global_fragment.shape[0], features.shape[1]
        block = functools.partial(jax.ShapeDtypeStruct, dtype=jnp.float32)

        def cost(count):
            return pl.CostEstimate(
                flops=2 * count * tokens * rows * width,
                bytes_accessed=count * rows * (2 * tokens + 4 * width),
                transcendentals=0,
            )

        room = pltpu.CompilerParams(vmem_limit_bytes=ROOM)
        free = pl.CostEstimate(flops=0, bytes_accessed=0, transcendentals=0)
        far_counts, far_features, far_cotangent = (
            pltpu.with_memory_space_constraint(array, pltpu.HBM) for array in (token_counts, features, cotangent)
        )
        held_counts = pltpu.SMEM(token_counts.shape, token_counts.dtype)
        held_piece = pltpu.VMEM(global_fragment.shape, global_fragment.dtype)

        half = rows // 2
        away_far, kept_far, masked, info = pl.pallas_call(
            functools.partial(first_kernel, workers, (7, 6)),
            out_shape=[
                block((2, width + SPARE, half)),
                block((2, width, half)),
                jax.ShapeDtypeStruct((tokens, width), jnp.bfloat16),
                block((8, width)),
            ],
            in_specs=[HBM] * 3,
            out_specs=[VMEM] * 4,
            scratch_shapes=[
                held_counts,
                pltpu.VMEM(cotangent.shape, cotangent.dtype),
                pltpu.VMEM((2, tokens, rows), features.dtype),
                pltpu.SemaphoreType.DMA((4,)),
            ],
            compiler_params=room,
            cost_estimate=cost(2),
            name="far_products",
        )(far_counts, far_cotangent, far_features)
        away_pass, kept_pass, away, kept = pl.pallas_call(
            rest_kernel,
            out_shape=[block((3, width, half))] * 4,
            in_specs=[VMEM] * 2,
            out_specs=[VMEM] * 4,
            compiler_params=room,
            cost_estimate=free,
            name="rest_products",
        )(masked, features)

        def add(*terms, name, count=1):
            picks = [pick for _, pick in terms]
            return pl.pallas_call(
                functools.partial(add_kernel, picks),
                out_shape=block((count, width, half)),
                in_specs=[ANY if pick is None else VMEM for pick in picks],
                out_specs=VMEM,
                compiler_params=room,
                cost_estimate=free,
                name=name,
            )(*(array for array, _ in terms))

        def part(number, count=1):
            return slice(number, number + count)

        state, piece = block(params.shape), block(global_fragment.shape)
        come_far = hop(away_far, "fsdp", devices, 1)
        sent = add((kept_far, part(0)), (come_far, (part(0), part(0, width))), name="add_a1")
        far_left = hop(sent, "fsdp", devices, 2)
        come_pass = hop(away_pass, "fsdp", devices, 1)
        come = hop(away, "fsdp", devices, 1)
        drift, scale = pl.pallas_call(
            drift_kernel,
            out_shape=[piece, block((rows, width))],
            in_specs=[VMEM, SMEM, VMEM, VMEM, ANY],
            out_specs=[VMEM] * 2,
            compiler_params=room,
            cost_estimate=free,
            name="drift",
        )(info, fragment_index, params, global_fragment, sent)
        sent = add((kept_far, part(1)), (come_far, (part(1), part(0, width))), (drift, None), name="add_a2")
        far_right = hop(sent, "fsdp", devices, 2)
        passed = add((kept_pass, part(0)), (come_pass, part(0)), (far_left, part(0)), name="add_c1")
        far_left = hop(passed, "fsdp", devices, 4)
        near_left = add((kept, part(1)), (come, part(1)), (sent, None), name="add_n1")
        far_right = add((kept_pass, part(1)), (come_pass, part(1)), (far_right, part(0)), (passed, None), name="add_c2")
        near_right = add((kept, part(2)), (come, part(2)), (far_right, None), name="add_n2")
        drift, _ = lax.optimization_barrier((drift, sent))
        bit = workers // 2
        drifts = (drift, hop(drift, "worker", workers, bit))
        while bit > 1:
            bit //= 2
            drift = drifts[0] + drifts[1]
            drift, _ = lax.optimization_barrier((drift, near_right))
            drifts = (drift, hop(drift, "worker", workers, bit))
        near_left = hop(near_left, "fsdp", devices, 2)
        far_right = hop(far_right, "fsdp", devices, 4)
        near_right = hop(near_right, "fsdp", devices, 2)
        groups = half // LANES
        held_half = pltpu.VMEM((half, width), jnp.float32)
        mix, *results, new_global, new_momentum = pl.pallas_call(
            left_kernel,
            out_shape=[block((half, width)), state, state, state, piece, piece],
            in_specs=[VMEM] * 13,
            out_specs=[VMEM] + [HBM] * 5,
            scratch_shapes=[held_half] * 3
            + [held_piece] * 2
            + [pltpu.VMEM((rows, width), jnp.float32), pltpu.SemaphoreType.DMA((2 + 3 * groups,))],
            compiler_params=room,
            cost_estimate=pl.CostEstimate(
                flops=30 * half * width, bytes_accessed=40 * half * width, transcendentals=2 * half * width
            ),
            name="left_step",
        )(
            params,
            first,
            second,
            kept,
            come,
            far_left,
            near_left,
            info,
            scale,
            global_fragment,
            outer_momentum,
            *drifts,
        )
        new_params, new_first, new_second = pl.pallas_call(
            right_kernel,
            out_shape=[state] * 3,
            in_specs=[VMEM] * 10 + [HBM] * 3,
            out_specs=[HBM] * 3,
            input_output_aliases={10: 0, 11: 1, 12: 2},
            scratch_shapes=[held_half] * 3 + [pltpu.SemaphoreType.DMA((3 * groups,))],
            compiler_params=room,
            cost_estimate=free,
            name="right_step",
        )(params, first, second, kept_pass, come_pass, far_right, near_right, info, scale, mix, *results)
        return new_params, new_first, new_second, new_global, new_momentum

    return body


def plain_body(mesh):
    workers, devices = mesh.shape["worker"], mesh.shape["fsdp"]

    def body(
        params, first, second, global_fragment, outer_momentum, features, cotangent, token_counts, fragment_index
    ):
        rows, width = params.shape[1:]
        tokens = features.shape[1]
        me = lax.axis_index("fsdp")
        count = lax.dynamic_index_in_dim(token_counts, lax.axis_index("worker"), 0, keepdims=False)
        live = count.astype(jnp.float32)
        valid = (me * tokens + lax.iota(jnp.int32, tokens) < count)[:, None]
        masked = jnp.where(valid, cotangent[0], jnp.zeros_like(cotangent[0]))
        term = lax.dot_general(features[0], masked, (((0,), (0,)), ((), ())), preferred_element_type=jnp.float32)
        blocks = jnp.take(term.reshape(devices, rows, width), me ^ jnp.arange(devices, dtype=jnp.int32), axis=0)
        bit = 1
        while bit < devices:
            blocks = blocks.reshape(-1, 2, rows, width)
            blocks = blocks[:, 0] + hop(blocks[:, 1], "fsdp", devices, bit)
            bit *= 2
        gradient = blocks[0] / live
        grouped = (rows // FRAGS, FRAGS, width)
        old = lax.dynamic_index_in_dim(params[0].reshape(grouped), fragment_index[0], 1, keepdims=False)
        drift_sum = doubling_sum(live * (global_fragment - old), "worker", workers)
        total = jnp.sum(token_counts).astype(jnp.float32)
        fresh, momentum = outer(drift_sum / total, global_fragment, outer_momentum)
        inner, first_new, second_new = adam(params[0], first[0], second[0], gradient)
        inner = inner.reshape(grouped)
        piece = lax.dynamic_index_in_dim(inner, fragment_index[0], 1, keepdims=False)
        mixed = MIXING * fresh + (1.0 - MIXING) * piece
        merged = lax.dynamic_update_index_in_dim(inner, mixed, fragment_index[0], 1).reshape(rows, width)
        return merged[None], first_new[None], second_new[None], fresh, momentum

    return body


def solution(mesh):
    devices = mesh.shape["fsdp"]

    def pick(*arrays):
        rows = arrays[0].shape[1]
        body = fast_body(mesh) if devices == 8 and rows % LANES == 0 else plain_body(mesh)
        return body(*arrays)

    state = P("worker", "fsdp", None)
    piece = P("fsdp", None)
    return jax.shard_map(
        pick,
        mesh=mesh,
        in_specs=(state, state, state, piece, piece, state, state, P(), P()),
        out_specs=(state, state, state, piece, piece),
        check_vma=False,
    )
```

```python
import functools

import jax
import jax.numpy as jnp
from jax import lax
from jax.experimental import pallas as pl
from jax.experimental.pallas import tpu as pltpu
from jax.sharding import PartitionSpec as P

FRAGS = 4
LANES = 128
SPARE = 8

BETA_ONE = 0.9
BETA_TWO = 0.95
CORRECT_ONE = 0.6513216
CORRECT_TWO = 0.401263
ADAM_EPS = 1e-08
LEARN_RATE = 0.02
DECAY_RATE = 0.1
NESTEROV = 0.9
OUTER_RATE = 0.7
MIXING = 0.5

VMEM = pl.BlockSpec(memory_space=pltpu.VMEM)
SMEM = pl.BlockSpec(memory_space=pltpu.SMEM)
HBM = pl.BlockSpec(memory_space=pltpu.HBM)
ANY = pl.BlockSpec(memory_space=pl.ANY)
ROOM = 8 << 20


def masked_rows(live, cotangent):
    rows = lax.broadcasted_iota(jnp.int32, cotangent.shape, 0)
    return jnp.where(rows < live, cotangent.astype(jnp.float32), 0.0).astype(jnp.bfloat16)


def columns_of(relative, rows, start, size):
    return pl.ds(pl.multiple_of((lax.axis_index("fsdp") ^ relative) * rows + start, LANES), size)


def product(masked, features):
    return lax.dot_general(masked, features, (((0,), (0,)), ((), ())), preferred_element_type=jnp.float32)


def fetch(sources, targets, sems, start=0):
    copies = [
        pltpu.make_async_copy(source, target, sems.at[start + slot])
        for slot, (source, target) in enumerate(zip(sources, targets))
    ]
    for copy in copies:
        copy.start()
    return copies


def first_kernel(
    workers, order, counts, cotangent, features, away, kept, masked, info, counts_held, cot_held, held, sems
):
    half = away.shape[2]
    small = fetch((counts, cotangent), (counts_held, cot_held), sems)
    columns = [columns_of(q, 2 * half, 0, 2 * half) for q in order]
    blocks = fetch([features.at[0, :, c] for c in columns], [held.at[n] for n in range(len(order))], sems, len(small))
    for copy in small:
        copy.wait()
    tokens = cot_held.shape[1]
    live = counts_held[lax.axis_index("worker")] - lax.axis_index("fsdp") * tokens
    masked[...] = masked_rows(live, cot_held[0])
    count, total = counts_held[lax.axis_index("worker")], counts_held[0]
    for other in range(1, workers):
        total = total + counts_held[other]
    info[0:1, :] = jnp.full((1, info.shape[1]), count.astype(jnp.float32))
    info[1:2, :] = 1.0 / info[0:1, :]
    info[2:3, :] = 1.0 / jnp.full((1, info.shape[1]), total.astype(jnp.float32))
    for slot, into in enumerate((away, kept)):
        blocks[slot].wait()
        for side in (0, 1):
            into[side, : masked.shape[1]] = product(masked[...], held[slot, :, side * half : (side + 1) * half])
    away[:, masked.shape[1] :] = jnp.zeros((2, SPARE, half), jnp.float32)


def rest_kernel(masked, features, *targets):
    half = targets[0].shape[2]
    places = [(4, 0, 0, 0), (4, 1, 0, 1), (0, 1, 0, 2), (2, 0, 2, 1), (2, 1, 2, 2), (0, 0, 2, 0)]
    for q, side, into, at in places:
        for core in (1, 0):
            columns = columns_of(q + core, 2 * half, side * half, half)
            targets[into + 1 - core][at] = product(masked[...], features[0, :, columns])


def drift_kernel(info, fragment, params, global_fragment, after, drift, scale, params_held, global_held, sems):
    del after
    copies = fetch((params, global_fragment), (params_held, global_held), sems)
    mine = pl.ds(fragment[0], drift.shape[0], stride=FRAGS)
    scale[...] = jnp.ones_like(scale)
    scale[mine, :] = jnp.full_like(drift, 1.0 - MIXING)
    for copy in copies:
        copy.wait()
    drift[...] = info[0:1, :] * (global_held[...] - params_held[0, mine, :])


def add_kernel(picks, *refs):
    total = None
    for ref, pick in zip(refs, picks):
        if pick is not None:
            total = ref[pick] if total is None else total + ref[pick]
    refs[-1][...] = total


def adam(before, first, second, gradient):
    first_new = BETA_ONE * first + (1.0 - BETA_ONE) * gradient
    second_new = BETA_TWO * second + (1.0 - BETA_TWO) * gradient * gradient
    update = first_new * (1.0 / CORRECT_ONE) / (jnp.sqrt(second_new * (1.0 / CORRECT_TWO)) + ADAM_EPS)
    return before - LEARN_RATE * (update + DECAY_RATE * before), first_new, second_new


def outer(pseudo_grad, global_fragment, outer_momentum):
    momentum = NESTEROV * outer_momentum + pseudo_grad
    return global_fragment - OUTER_RATE * (pseudo_grad + NESTEROV * momentum), momentum


def half_step(half, states, sums, info, held):
    params, first, second = states
    kept, come, far, near = sums
    held_first, held_second = held
    rows = kept.shape[2]
    for lane in range(0, rows, LANES):
        lanes, there = pl.ds(lane, LANES), pl.ds(half * rows + lane, LANES)
        summed = kept[2 * half, :, lanes] + come[2 * half, :, lanes] + near[0, :, lanes] + far[0, :, lanes]
        inner, held_first[lanes, :], held_second[lanes, :] = adam(
            params[0, there, :], first[0, there, :], second[0, there, :], summed.T * info[1:2, :]
        )
        yield lanes, there, inner


def send(copies, sems, source, target):
    copies.append(pltpu.make_async_copy(source, target, sems.at[len(copies)]))
    copies[-1].start()


def left_kernel(
    params,
    first,
    second,
    kept,
    come,
    far,
    near,
    info,
    scale,
    global_fragment,
    outer_momentum,
    drift,
    other_drift,
    mix,
    new_params,
    new_first,
    new_second,
    new_global,
    new_momentum,
    held_params,
    held_first,
    held_second,
    held_global,
    held_momentum,
    spread,
    sems,
):
    copies = []
    fresh, momentum = outer((drift[...] + other_drift[...]) * info[2:3, :], global_fragment[...], outer_momentum[...])
    held_global[...] = fresh
    held_momentum[...] = momentum
    send(copies, sems, held_global, new_global)
    send(copies, sems, held_momentum, new_momentum)
    for at in range(FRAGS):
        spread[pl.ds(at, fresh.shape[0], stride=FRAGS), :] = fresh
    for lanes, there, value in half_step(
        0, (params, first, second), (kept, come, far, near), info, (held_first, held_second)
    ):
        held_params[lanes, :] = scale[there, :] * value + (1.0 - scale[there, :]) * spread[there, :]
        for source, target in ((held_first, new_first), (held_second, new_second), (held_params, new_params)):
            send(copies, sems, source.at[lanes], target.at[0, there])
    right = pl.ds(mix.shape[0], mix.shape[0])
    mix[...] = (1.0 - scale[right, :]) * spread[right, :]
    for copy in copies:
        copy.wait()


def right_kernel(
    params,
    first,
    second,
    kept,
    come,
    far,
    near,
    info,
    scale,
    mix,
    left_params,
    left_first,
    left_second,
    new_params,
    new_first,
    new_second,
    held_params,
    held_first,
    held_second,
    sems,
):
    del left_params, left_first, left_second
    copies = []
    for lanes, there, value in half_step(
        1, (params, first, second), (kept, come, far, near), info, (held_first, held_second)
    ):
        held_params[lanes, :] = scale[there, :] * value + mix[lanes, :]
        for source, target in ((held_first, new_first), (held_second, new_second), (held_params, new_params)):
            send(copies, sems, source.at[lanes], target.at[0, there])
    for copy in copies:
        copy.wait()


def hop(value, axis, devices, bit):
    return lax.ppermute(value, axis, [(d, d ^ bit) for d in range(devices)])


def doubling_sum(value, axis, devices):
    bit = devices // 2
    while bit:
        value = value + hop(value, axis, devices, bit)
        bit //= 2
    return value


def fast_body(mesh):
    workers, devices = mesh.shape["worker"], mesh.shape["fsdp"]

    def body(
        params, first, second, global_fragment, outer_momentum, features, cotangent, token_counts, fragment_index
    ):
        rows, width = params.shape[1:]
        pieces, tokens = global_fragment.shape[0], features.shape[1]
        block = functools.partial(jax.ShapeDtypeStruct, dtype=jnp.float32)

        def cost(count):
            return pl.CostEstimate(
                flops=2 * count * tokens * rows * width,
                bytes_accessed=count * rows * (2 * tokens + 4 * width),
                transcendentals=0,
            )

        room = pltpu.CompilerParams(vmem_limit_bytes=ROOM)
        free = pl.CostEstimate(flops=0, bytes_accessed=0, transcendentals=0)
        far_counts, far_features, far_cotangent, far_params, far_global = (
            pltpu.with_memory_space_constraint(array, pltpu.HBM)
            for array in (token_counts, features, cotangent, params, global_fragment)
        )
        held_counts = pltpu.SMEM(token_counts.shape, token_counts.dtype)
        held_piece = pltpu.VMEM(global_fragment.shape, global_fragment.dtype)

        half = rows // 2
        away_far, kept_far, masked, info = pl.pallas_call(
            functools.partial(first_kernel, workers, (7, 6)),
            out_shape=[
                block((2, width + SPARE, half)),
                block((2, width, half)),
                jax.ShapeDtypeStruct((tokens, width), jnp.bfloat16),
                block((8, width)),
            ],
            in_specs=[HBM] * 3,
            out_specs=[VMEM] * 4,
            scratch_shapes=[
                held_counts,
                pltpu.VMEM(cotangent.shape, cotangent.dtype),
                pltpu.VMEM((2, tokens, rows), features.dtype),
                pltpu.SemaphoreType.DMA((4,)),
            ],
            compiler_params=room,
            cost_estimate=cost(2),
            name="far_products",
        )(far_counts, far_cotangent, far_features)
        away_pass, kept_pass, away, kept = pl.pallas_call(
            rest_kernel,
            out_shape=[block((3, width, half))] * 4,
            in_specs=[VMEM] * 2,
            out_specs=[VMEM] * 4,
            compiler_params=room,
            cost_estimate=free,
            name="rest_products",
        )(masked, features)

        def add(*terms, name, count=1):
            picks = [pick for _, pick in terms]
            return pl.pallas_call(
                functools.partial(add_kernel, picks),
                out_shape=block((count, width, half)),
                in_specs=[ANY if pick is None else VMEM for pick in picks],
                out_specs=VMEM,
                compiler_params=room,
                cost_estimate=free,
                name=name,
            )(*(array for array, _ in terms))

        def part(number, count=1):
            return slice(number, number + count)

        state, piece = block(params.shape), block(global_fragment.shape)
        come_far = hop(away_far, "fsdp", devices, 1)
        sent = add((kept_far, part(0)), (come_far, (part(0), part(0, width))), name="add_a1")
        far_left = hop(sent, "fsdp", devices, 2)
        come_pass = hop(away_pass, "fsdp", devices, 1)
        come = hop(away, "fsdp", devices, 1)
        drift, scale = pl.pallas_call(
            drift_kernel,
            out_shape=[piece, block((rows, width))],
            in_specs=[VMEM, SMEM, HBM, HBM, ANY],
            out_specs=[VMEM] * 2,
            scratch_shapes=[pltpu.VMEM(params.shape, params.dtype), held_piece, pltpu.SemaphoreType.DMA((2,))],
            compiler_params=room,
            cost_estimate=free,
            name="drift",
        )(info, fragment_index, far_params, far_global, sent)
        sent = add((kept_far, part(1)), (come_far, (part(1), part(0, width))), (drift, None), name="add_a2")
        far_right = hop(sent, "fsdp", devices, 2)
        passed = add((kept_pass, part(0)), (come_pass, part(0)), (far_left, part(0)), name="add_c1")
        far_left = hop(passed, "fsdp", devices, 4)
        near_left = add((kept, part(1)), (come, part(1)), (passed, None), name="add_n1")
        far_right = add((kept_pass, part(1)), (come_pass, part(1)), (far_right, part(0)), (passed, None), name="add_c2")
        near_right = add((kept, part(2)), (come, part(2)), (far_right, None), name="add_n2")
        drift, _ = lax.optimization_barrier((drift, sent))
        bit = workers // 2
        drifts = (drift, hop(drift, "worker", workers, bit))
        while bit > 1:
            bit //= 2
            drift = drifts[0] + drifts[1]
            drift, _ = lax.optimization_barrier((drift, near_right))
            drifts = (drift, hop(drift, "worker", workers, bit))
        near_left = hop(near_left, "fsdp", devices, 2)
        far_right = hop(far_right, "fsdp", devices, 4)
        near_right = hop(near_right, "fsdp", devices, 2)
        groups = half // LANES
        held_half = pltpu.VMEM((half, width), jnp.float32)
        mix, *results, new_global, new_momentum = pl.pallas_call(
            left_kernel,
            out_shape=[block((half, width)), state, state, state, piece, piece],
            in_specs=[VMEM] * 13,
            out_specs=[VMEM] + [HBM] * 5,
            scratch_shapes=[held_half] * 3
            + [held_piece] * 2
            + [pltpu.VMEM((rows, width), jnp.float32), pltpu.SemaphoreType.DMA((2 + 3 * groups,))],
            compiler_params=room,
            cost_estimate=pl.CostEstimate(
                flops=30 * half * width, bytes_accessed=40 * half * width, transcendentals=2 * half * width
            ),
            name="left_step",
        )(
            params,
            first,
            second,
            kept,
            come,
            far_left,
            near_left,
            info,
            scale,
            global_fragment,
            outer_momentum,
            *drifts,
        )
        new_params, new_first, new_second = pl.pallas_call(
            right_kernel,
            out_shape=[state] * 3,
            in_specs=[VMEM] * 10 + [HBM] * 3,
            out_specs=[HBM] * 3,
            input_output_aliases={10: 0, 11: 1, 12: 2},
            scratch_shapes=[held_half] * 3 + [pltpu.SemaphoreType.DMA((3 * groups,))],
            compiler_params=room,
            cost_estimate=free,
            name="right_step",
        )(params, first, second, kept_pass, come_pass, far_right, near_right, info, scale, mix, *results)
        return new_params, new_first, new_second, new_global, new_momentum

    return body


def plain_body(mesh):
    workers, devices = mesh.shape["worker"], mesh.shape["fsdp"]

    def body(
        params, first, second, global_fragment, outer_momentum, features, cotangent, token_counts, fragment_index
    ):
        rows, width = params.shape[1:]
        tokens = features.shape[1]
        me = lax.axis_index("fsdp")
        count = lax.dynamic_index_in_dim(token_counts, lax.axis_index("worker"), 0, keepdims=False)
        live = count.astype(jnp.float32)
        valid = (me * tokens + lax.iota(jnp.int32, tokens) < count)[:, None]
        masked = jnp.where(valid, cotangent[0], jnp.zeros_like(cotangent[0]))
        term = lax.dot_general(features[0], masked, (((0,), (0,)), ((), ())), preferred_element_type=jnp.float32)
        blocks = jnp.take(term.reshape(devices, rows, width), me ^ jnp.arange(devices, dtype=jnp.int32), axis=0)
        bit = 1
        while bit < devices:
            blocks = blocks.reshape(-1, 2, rows, width)
            blocks = blocks[:, 0] + hop(blocks[:, 1], "fsdp", devices, bit)
            bit *= 2
        gradient = blocks[0] / live
        grouped = (rows // FRAGS, FRAGS, width)
        old = lax.dynamic_index_in_dim(params[0].reshape(grouped), fragment_index[0], 1, keepdims=False)
        drift_sum = doubling_sum(live * (global_fragment - old), "worker", workers)
        total = jnp.sum(token_counts).astype(jnp.float32)
        fresh, momentum = outer(drift_sum / total, global_fragment, outer_momentum)
        inner, first_new, second_new = adam(params[0], first[0], second[0], gradient)
        inner = inner.reshape(grouped)
        piece = lax.dynamic_index_in_dim(inner, fragment_index[0], 1, keepdims=False)
        mixed = MIXING * fresh + (1.0 - MIXING) * piece
        merged = lax.dynamic_update_index_in_dim(inner, mixed, fragment_index[0], 1).reshape(rows, width)
        return merged[None], first_new[None], second_new[None], fresh, momentum

    return body


def solution(mesh):
    devices = mesh.shape["fsdp"]

    def pick(*arrays):
        rows = arrays[0].shape[1]
        body = fast_body(mesh) if devices == 8 and rows % LANES == 0 else plain_body(mesh)
        return body(*arrays)

    state = P("worker", "fsdp", None)
    piece = P("fsdp", None)
    return jax.shard_map(
        pick,
        mesh=mesh,
        in_specs=(state, state, state, piece, piece, state, state, P(), P()),
        out_specs=(state, state, state, piece, piece),
        check_vma=False,
    )
```

```python
import functools

import jax
import jax.numpy as jnp
from jax import lax
from jax.experimental import pallas as pl
from jax.experimental.pallas import tpu as pltpu
from jax.sharding import PartitionSpec as P

FRAGS = 4
LANES = 128
SPARE = 8

BETA_ONE = 0.9
BETA_TWO = 0.95
CORRECT_ONE = 0.6513216
CORRECT_TWO = 0.401263
ADAM_EPS = 1e-08
LEARN_RATE = 0.02
DECAY_RATE = 0.1
NESTEROV = 0.9
OUTER_RATE = 0.7
MIXING = 0.5

VMEM = pl.BlockSpec(memory_space=pltpu.VMEM)
SMEM = pl.BlockSpec(memory_space=pltpu.SMEM)
HBM = pl.BlockSpec(memory_space=pltpu.HBM)
ANY = pl.BlockSpec(memory_space=pl.ANY)
ROOM = 8 << 20


def masked_rows(live, cotangent):
    rows = lax.broadcasted_iota(jnp.int32, cotangent.shape, 0)
    return jnp.where(rows < live, cotangent.astype(jnp.float32), 0.0).astype(jnp.bfloat16)


def columns_of(relative, rows, start, size):
    return pl.ds(pl.multiple_of((lax.axis_index("fsdp") ^ relative) * rows + start, LANES), size)


def product(masked, features):
    return lax.dot_general(masked, features, (((0,), (0,)), ((), ())), preferred_element_type=jnp.float32)


def fetch(sources, targets, sems, start=0):
    copies = [
        pltpu.make_async_copy(source, target, sems.at[start + slot])
        for slot, (source, target) in enumerate(zip(sources, targets))
    ]
    for copy in copies:
        copy.start()
    return copies


def first_kernel(
    workers, order, counts, cotangent, features, away, kept, masked, info, counts_held, cot_held, held, sems
):
    half = away.shape[2]
    small = fetch((counts, cotangent), (counts_held, cot_held), sems)
    columns = [columns_of(q, 2 * half, 0, 2 * half) for q in order]
    blocks = fetch([features.at[0, :, c] for c in columns], [held.at[n] for n in range(len(order))], sems, len(small))
    for copy in small:
        copy.wait()
    tokens = cot_held.shape[1]
    live = counts_held[lax.axis_index("worker")] - lax.axis_index("fsdp") * tokens
    masked[...] = masked_rows(live, cot_held[0])
    count, total = counts_held[lax.axis_index("worker")], counts_held[0]
    for other in range(1, workers):
        total = total + counts_held[other]
    info[0:1, :] = jnp.full((1, info.shape[1]), count.astype(jnp.float32))
    info[1:2, :] = 1.0 / info[0:1, :]
    info[2:3, :] = 1.0 / jnp.full((1, info.shape[1]), total.astype(jnp.float32))
    for slot, into in enumerate((away, kept)):
        blocks[slot].wait()
        for side in (0, 1):
            into[side, : masked.shape[1]] = product(masked[...], held[slot, :, side * half : (side + 1) * half])
    away[:, masked.shape[1] :] = jnp.zeros((2, SPARE, half), jnp.float32)


def rest_kernel(masked, features, *targets):
    half = targets[0].shape[2]
    places = [(4, 0, 0, 0), (4, 1, 0, 1), (0, 1, 0, 2), (2, 0, 2, 1), (2, 1, 2, 2), (0, 0, 2, 0)]
    for q, side, into, at in places:
        for core in (1, 0):
            columns = columns_of(q + core, 2 * half, side * half, half)
            targets[into + 1 - core][at] = product(masked[...], features[0, :, columns])


def drift_kernel(info, fragment, params, global_fragment, after, drift, scale):
    del after
    mine = pl.ds(fragment[0], drift.shape[0], stride=FRAGS)
    drift[...] = info[0:1, :] * (global_fragment[...] - params[0, mine, :])
    scale[...] = jnp.ones_like(scale)
    scale[mine, :] = jnp.full_like(drift, 1.0 - MIXING)


def add_kernel(picks, *refs):
    total = None
    for ref, pick in zip(refs, picks):
        if pick is not None:
            total = ref[pick] if total is None else total + ref[pick]
    refs[-1][...] = total


def adam(before, first, second, gradient):
    first_new = BETA_ONE * first + (1.0 - BETA_ONE) * gradient
    second_new = BETA_TWO * second + (1.0 - BETA_TWO) * gradient * gradient
    update = first_new * (1.0 / CORRECT_ONE) / (jnp.sqrt(second_new * (1.0 / CORRECT_TWO)) + ADAM_EPS)
    return before - LEARN_RATE * (update + DECAY_RATE * before), first_new, second_new


def outer(pseudo_grad, global_fragment, outer_momentum):
    momentum = NESTEROV * outer_momentum + pseudo_grad
    return global_fragment - OUTER_RATE * (pseudo_grad + NESTEROV * momentum), momentum


def half_step(half, states, sums, info, held):
    params, first, second = states
    kept, come, far, near = sums
    held_first, held_second = held
    rows = kept.shape[2]
    for lane in range(0, rows, LANES):
        lanes, there = pl.ds(lane, LANES), pl.ds(half * rows + lane, LANES)
        summed = kept[2 * half, :, lanes] + come[2 * half, :, lanes] + near[0, :, lanes] + far[0, :, lanes]
        inner, held_first[lanes, :], held_second[lanes, :] = adam(
            params[0, there, :], first[0, there, :], second[0, there, :], summed.T * info[1:2, :]
        )
        yield lanes, there, inner


def send(copies, sems, source, target):
    copies.append(pltpu.make_async_copy(source, target, sems.at[len(copies)]))
    copies[-1].start()


def left_kernel(
    params,
    first,
    second,
    kept,
    come,
    far,
    near,
    info,
    scale,
    global_fragment,
    outer_momentum,
    drift,
    other_drift,
    mix,
    new_params,
    new_first,
    new_second,
    new_global,
    new_momentum,
    held_params,
    held_first,
    held_second,
    held_global,
    held_momentum,
    spread,
    sems,
):
    copies = []
    fresh, momentum = outer((drift[...] + other_drift[...]) * info[2:3, :], global_fragment[...], outer_momentum[...])
    held_global[...] = fresh
    held_momentum[...] = momentum
    send(copies, sems, held_global, new_global)
    send(copies, sems, held_momentum, new_momentum)
    for at in range(FRAGS):
        spread[pl.ds(at, fresh.shape[0], stride=FRAGS), :] = fresh
    for lanes, there, value in half_step(
        0, (params, first, second), (kept, come, far, near), info, (held_first, held_second)
    ):
        held_params[lanes, :] = scale[there, :] * value + (1.0 - scale[there, :]) * spread[there, :]
        for source, target in ((held_first, new_first), (held_second, new_second), (held_params, new_params)):
            send(copies, sems, source.at[lanes], target.at[0, there])
    right = pl.ds(mix.shape[0], mix.shape[0])
    mix[...] = (1.0 - scale[right, :]) * spread[right, :]
    for copy in copies:
        copy.wait()


def right_kernel(
    params,
    first,
    second,
    kept,
    come,
    far,
    near,
    info,
    scale,
    mix,
    left_params,
    left_first,
    left_second,
    new_params,
    new_first,
    new_second,
    held_params,
    held_first,
    held_second,
    sems,
):
    del left_params, left_first, left_second
    copies = []
    for lanes, there, value in half_step(
        1, (params, first, second), (kept, come, far, near), info, (held_first, held_second)
    ):
        held_params[lanes, :] = scale[there, :] * value + mix[lanes, :]
        for source, target in ((held_first, new_first), (held_second, new_second), (held_params, new_params)):
            send(copies, sems, source.at[lanes], target.at[0, there])
    for copy in copies:
        copy.wait()


def hop(value, axis, devices, bit):
    return lax.ppermute(value, axis, [(d, d ^ bit) for d in range(devices)])


def doubling_sum(value, axis, devices):
    bit = devices // 2
    while bit:
        value = value + hop(value, axis, devices, bit)
        bit //= 2
    return value


def fast_body(mesh):
    workers, devices = mesh.shape["worker"], mesh.shape["fsdp"]

    def body(
        params, first, second, global_fragment, outer_momentum, features, cotangent, token_counts, fragment_index
    ):
        rows, width = params.shape[1:]
        pieces, tokens = global_fragment.shape[0], features.shape[1]
        block = functools.partial(jax.ShapeDtypeStruct, dtype=jnp.float32)

        def cost(count):
            return pl.CostEstimate(
                flops=2 * count * tokens * rows * width,
                bytes_accessed=count * rows * (2 * tokens + 4 * width),
                transcendentals=0,
            )

        room = pltpu.CompilerParams(vmem_limit_bytes=ROOM)
        free = pl.CostEstimate(flops=0, bytes_accessed=0, transcendentals=0)
        far_counts, far_features, far_cotangent = (
            pltpu.with_memory_space_constraint(array, pltpu.HBM) for array in (token_counts, features, cotangent)
        )
        held_counts = pltpu.SMEM(token_counts.shape, token_counts.dtype)
        held_piece = pltpu.VMEM(global_fragment.shape, global_fragment.dtype)

        half = rows // 2
        away_far, kept_far, masked, info = pl.pallas_call(
            functools.partial(first_kernel, workers, (7, 6)),
            out_shape=[
                block((2, width + SPARE, half)),
                block((2, width, half)),
                jax.ShapeDtypeStruct((tokens, width), jnp.bfloat16),
                block((8, width)),
            ],
            in_specs=[HBM] * 3,
            out_specs=[VMEM] * 4,
            scratch_shapes=[
                held_counts,
                pltpu.VMEM(cotangent.shape, cotangent.dtype),
                pltpu.VMEM((2, tokens, rows), features.dtype),
                pltpu.SemaphoreType.DMA((4,)),
            ],
            compiler_params=room,
            cost_estimate=cost(2),
            name="far_products",
        )(far_counts, far_cotangent, far_features)
        away_pass, kept_pass, away, kept = pl.pallas_call(
            rest_kernel,
            out_shape=[block((3, width, half))] * 4,
            in_specs=[VMEM] * 2,
            out_specs=[VMEM] * 4,
            compiler_params=room,
            cost_estimate=free,
            name="rest_products",
        )(masked, features)

        def add(*terms, name, count=1):
            picks = [pick for _, pick in terms]
            return pl.pallas_call(
                functools.partial(add_kernel, picks),
                out_shape=block((count, width, half)),
                in_specs=[ANY if pick is None else VMEM for pick in picks],
                out_specs=VMEM,
                compiler_params=room,
                cost_estimate=free,
                name=name,
            )(*(array for array, _ in terms))

        def part(number, count=1):
            return slice(number, number + count)

        state, piece = block(params.shape), block(global_fragment.shape)
        come_far = hop(away_far, "fsdp", devices, 1)
        sent = add((kept_far, part(0)), (come_far, (part(0), part(0, width))), name="add_a1")
        far_left = hop(sent, "fsdp", devices, 2)
        come_pass = hop(away_pass, "fsdp", devices, 1)
        come = hop(away, "fsdp", devices, 1)
        drift, scale = pl.pallas_call(
            drift_kernel,
            out_shape=[piece, block((rows, width))],
            in_specs=[VMEM, SMEM, VMEM, VMEM, ANY],
            out_specs=[VMEM] * 2,
            compiler_params=room,
            cost_estimate=free,
            name="drift",
        )(info, fragment_index, params, global_fragment, sent)
        sent = add((kept_far, part(1)), (come_far, (part(1), part(0, width))), name="add_a2")
        far_right = hop(sent, "fsdp", devices, 2)
        passed = add((kept_pass, part(0)), (come_pass, part(0)), (far_left, part(0)), name="add_c1")
        far_left = hop(passed, "fsdp", devices, 4)
        near_left = add((kept, part(1)), (come, part(1)), (passed, None), name="add_n1")
        far_right = add((kept_pass, part(1)), (come_pass, part(1)), (far_right, part(0)), (passed, None), name="add_c2")
        near_right = add((kept, part(2)), (come, part(2)), (far_right, None), name="add_n2")
        drift, _ = lax.optimization_barrier((drift, sent))
        bit = workers // 2
        drifts = (drift, hop(drift, "worker", workers, bit))
        while bit > 1:
            bit //= 2
            drift = drifts[0] + drifts[1]
            drift, _ = lax.optimization_barrier((drift, near_right))
            drifts = (drift, hop(drift, "worker", workers, bit))
        near_left = hop(near_left, "fsdp", devices, 2)
        far_right = hop(far_right, "fsdp", devices, 4)
        near_right = hop(near_right, "fsdp", devices, 2)
        groups = half // LANES
        held_half = pltpu.VMEM((half, width), jnp.float32)
        mix, *results, new_global, new_momentum = pl.pallas_call(
            left_kernel,
            out_shape=[block((half, width)), state, state, state, piece, piece],
            in_specs=[VMEM] * 13,
            out_specs=[VMEM] + [HBM] * 5,
            scratch_shapes=[held_half] * 3
            + [held_piece] * 2
            + [pltpu.VMEM((rows, width), jnp.float32), pltpu.SemaphoreType.DMA((2 + 3 * groups,))],
            compiler_params=room,
            cost_estimate=pl.CostEstimate(
                flops=30 * half * width, bytes_accessed=40 * half * width, transcendentals=2 * half * width
            ),
            name="left_step",
        )(
            params,
            first,
            second,
            kept,
            come,
            far_left,
            near_left,
            info,
            scale,
            global_fragment,
            outer_momentum,
            *drifts,
        )
        new_params, new_first, new_second = pl.pallas_call(
            right_kernel,
            out_shape=[state] * 3,
            in_specs=[VMEM] * 10 + [HBM] * 3,
            out_specs=[HBM] * 3,
            input_output_aliases={10: 0, 11: 1, 12: 2},
            scratch_shapes=[held_half] * 3 + [pltpu.SemaphoreType.DMA((3 * groups,))],
            compiler_params=room,
            cost_estimate=free,
            name="right_step",
        )(params, first, second, kept_pass, come_pass, far_right, near_right, info, scale, mix, *results)
        return new_params, new_first, new_second, new_global, new_momentum

    return body


def plain_body(mesh):
    workers, devices = mesh.shape["worker"], mesh.shape["fsdp"]

    def body(
        params, first, second, global_fragment, outer_momentum, features, cotangent, token_counts, fragment_index
    ):
        rows, width = params.shape[1:]
        tokens = features.shape[1]
        me = lax.axis_index("fsdp")
        count = lax.dynamic_index_in_dim(token_counts, lax.axis_index("worker"), 0, keepdims=False)
        live = count.astype(jnp.float32)
        valid = (me * tokens + lax.iota(jnp.int32, tokens) < count)[:, None]
        masked = jnp.where(valid, cotangent[0], jnp.zeros_like(cotangent[0]))
        term = lax.dot_general(features[0], masked, (((0,), (0,)), ((), ())), preferred_element_type=jnp.float32)
        blocks = jnp.take(term.reshape(devices, rows, width), me ^ jnp.arange(devices, dtype=jnp.int32), axis=0)
        bit = 1
        while bit < devices:
            blocks = blocks.reshape(-1, 2, rows, width)
            blocks = blocks[:, 0] + hop(blocks[:, 1], "fsdp", devices, bit)
            bit *= 2
        gradient = blocks[0] / live
        grouped = (rows // FRAGS, FRAGS, width)
        old = lax.dynamic_index_in_dim(params[0].reshape(grouped), fragment_index[0], 1, keepdims=False)
        drift_sum = doubling_sum(live * (global_fragment - old), "worker", workers)
        total = jnp.sum(token_counts).astype(jnp.float32)
        fresh, momentum = outer(drift_sum / total, global_fragment, outer_momentum)
        inner, first_new, second_new = adam(params[0], first[0], second[0], gradient)
        inner = inner.reshape(grouped)
        piece = lax.dynamic_index_in_dim(inner, fragment_index[0], 1, keepdims=False)
        mixed = MIXING * fresh + (1.0 - MIXING) * piece
        merged = lax.dynamic_update_index_in_dim(inner, mixed, fragment_index[0], 1).reshape(rows, width)
        return merged[None], first_new[None], second_new[None], fresh, momentum

    return body


def solution(mesh):
    devices = mesh.shape["fsdp"]

    def pick(*arrays):
        rows = arrays[0].shape[1]
        body = fast_body(mesh) if devices == 8 and rows % LANES == 0 else plain_body(mesh)
        return body(*arrays)

    state = P("worker", "fsdp", None)
    piece = P("fsdp", None)
    return jax.shard_map(
        pick,
        mesh=mesh,
        in_specs=(state, state, state, piece, piece, state, state, P(), P()),
        out_specs=(state, state, state, piece, piece),
        check_vma=False,
    )
```

```python
import functools

import jax
import jax.numpy as jnp
from jax import lax
from jax.experimental import pallas as pl
from jax.experimental.pallas import tpu as pltpu
from jax.sharding import PartitionSpec as P

FRAGS = 4
LANES = 128

BETA_ONE = 0.9
BETA_TWO = 0.95
CORRECT_ONE = 0.6513216
CORRECT_TWO = 0.401263
ADAM_EPS = 1e-08
LEARN_RATE = 0.02
DECAY_RATE = 0.1
NESTEROV = 0.9
OUTER_RATE = 0.7
MIXING = 0.5

VMEM = pl.BlockSpec(memory_space=pltpu.VMEM)
SMEM = pl.BlockSpec(memory_space=pltpu.SMEM)
HBM = pl.BlockSpec(memory_space=pltpu.HBM)
ANY = pl.BlockSpec(memory_space=pl.ANY)
ROOM = 8 << 20


def masked_columns(live, cotangent):
    turned = cotangent.astype(jnp.float32).T
    tokens = lax.broadcasted_iota(jnp.int32, turned.shape, 1)
    return jnp.where(tokens < live, turned, 0.0).astype(jnp.bfloat16)


def columns_of(relative, rows, start, size):
    return pl.ds(pl.multiple_of((lax.axis_index("fsdp") ^ relative) * rows + start, LANES), size)


def product(masked, features):
    return jnp.dot(masked, features, preferred_element_type=jnp.float32)


def fetch(sources, targets, sems, start=0):
    copies = [
        pltpu.make_async_copy(source, target, sems.at[start + slot])
        for slot, (source, target) in enumerate(zip(sources, targets))
    ]
    for copy in copies:
        copy.start()
    return copies


def first_kernel(
    workers, order, counts, cotangent, features, away, kept, masked, info, counts_held, cot_held, held, sems
):
    half = away.shape[2]
    small = fetch((counts, cotangent), (counts_held, cot_held), sems)
    columns = [columns_of(q, 2 * half, 0, 2 * half) for q in order]
    blocks = fetch([features.at[0, :, c] for c in columns], [held.at[n] for n in range(len(order))], sems, len(small))
    for copy in small:
        copy.wait()
    tokens = cot_held.shape[1]
    live = counts_held[lax.axis_index("worker")] - lax.axis_index("fsdp") * tokens
    masked[...] = masked_columns(live, cot_held[0])
    for slot, into in enumerate((away, kept)):
        blocks[slot].wait()
        for side in (0, 1):
            into[side] = product(masked[...], held[slot, :, side * half : (side + 1) * half])
    count, total = counts_held[lax.axis_index("worker")], counts_held[0]
    for other in range(1, workers):
        total = total + counts_held[other]
    info[0:1, :] = jnp.full((1, info.shape[1]), count.astype(jnp.float32))
    info[1:2, :] = 1.0 / info[0:1, :]
    info[2:3, :] = 1.0 / jnp.full((1, info.shape[1]), total.astype(jnp.float32))


def rest_kernel(masked, features, *targets):
    half = targets[0].shape[2]
    places = [(4, 0, 0, 4), (4, 1, 0, 5), (2, 0, 0, 2), (2, 1, 0, 3), (0, 0, 0, 0), (0, 1, 0, 1)]
    for q, side, into, at in places:
        for core in (1, 0):
            columns = columns_of(q + core, 2 * half, side * half, half)
            targets[into + 1 - core][at] = product(masked[...], features[0, :, columns])


def drift_kernel(info, fragment, params, global_fragment, after, drift, scale):
    del after
    mine = pl.ds(fragment[0], drift.shape[0], stride=FRAGS)
    drift[...] = info[0:1, :] * (global_fragment[...] - params[0, mine, :])
    scale[...] = jnp.ones_like(scale)
    scale[mine, :] = jnp.full_like(drift, 1.0 - MIXING)


def add_kernel(picks, *refs):
    total = None
    for ref, pick in zip(refs, picks):
        if pick is not None:
            total = ref[pick] if total is None else total + ref[pick]
    refs[-1][...] = total


def adam(before, first, second, gradient):
    first_new = BETA_ONE * first + (1.0 - BETA_ONE) * gradient
    second_new = BETA_TWO * second + (1.0 - BETA_TWO) * gradient * gradient
    update = first_new * (1.0 / CORRECT_ONE) / (jnp.sqrt(second_new * (1.0 / CORRECT_TWO)) + ADAM_EPS)
    return before - LEARN_RATE * (update + DECAY_RATE * before), first_new, second_new


def outer(pseudo_grad, global_fragment, outer_momentum):
    momentum = NESTEROV * outer_momentum + pseudo_grad
    return global_fragment - OUTER_RATE * (pseudo_grad + NESTEROV * momentum), momentum


def half_step(half, states, sums, info, held):
    params, first, second = states
    kept, come, far, near = sums
    held_first, held_second = held
    rows = kept.shape[2]
    for lane in range(0, rows, LANES):
        lanes, there = pl.ds(lane, LANES), pl.ds(half * rows + lane, LANES)
        summed = kept[half, :, lanes] + come[half, :, lanes] + near[0, :, lanes] + far[0, :, lanes]
        inner, held_first[lanes, :], held_second[lanes, :] = adam(
            params[0, there, :], first[0, there, :], second[0, there, :], summed.T * info[1:2, :]
        )
        yield lanes, there, inner


def send(copies, sems, source, target):
    copies.append(pltpu.make_async_copy(source, target, sems.at[len(copies)]))
    copies[-1].start()


def left_kernel(
    params,
    first,
    second,
    kept,
    come,
    far,
    near,
    info,
    scale,
    global_fragment,
    outer_momentum,
    drift,
    other_drift,
    mix,
    new_params,
    new_first,
    new_second,
    new_global,
    new_momentum,
    held_params,
    held_first,
    held_second,
    held_global,
    held_momentum,
    spread,
    sems,
):
    copies = []
    fresh, momentum = outer((drift[...] + other_drift[...]) * info[2:3, :], global_fragment[...], outer_momentum[...])
    held_global[...] = fresh
    held_momentum[...] = momentum
    send(copies, sems, held_global, new_global)
    send(copies, sems, held_momentum, new_momentum)
    for at in range(FRAGS):
        spread[pl.ds(at, fresh.shape[0], stride=FRAGS), :] = fresh
    for lanes, there, value in half_step(
        0, (params, first, second), (kept, come, far, near), info, (held_first, held_second)
    ):
        held_params[lanes, :] = scale[there, :] * value + (1.0 - scale[there, :]) * spread[there, :]
        for source, target in ((held_first, new_first), (held_second, new_second), (held_params, new_params)):
            send(copies, sems, source.at[lanes], target.at[0, there])
    right = pl.ds(mix.shape[0], mix.shape[0])
    mix[...] = (1.0 - scale[right, :]) * spread[right, :]
    for copy in copies:
        copy.wait()


def right_kernel(
    params,
    first,
    second,
    kept,
    come,
    far,
    near,
    info,
    scale,
    mix,
    left_params,
    left_first,
    left_second,
    new_params,
    new_first,
    new_second,
    held_params,
    held_first,
    held_second,
    sems,
):
    del left_params, left_first, left_second
    copies = []
    for lanes, there, value in half_step(
        1, (params, first, second), (kept, come, far, near), info, (held_first, held_second)
    ):
        held_params[lanes, :] = scale[there, :] * value + mix[lanes, :]
        for source, target in ((held_first, new_first), (held_second, new_second), (held_params, new_params)):
            send(copies, sems, source.at[lanes], target.at[0, there])
    for copy in copies:
        copy.wait()


def hop(value, axis, devices, bit):
    return lax.ppermute(value, axis, [(d, d ^ bit) for d in range(devices)])


def doubling_sum(value, axis, devices):
    bit = devices // 2
    while bit:
        value = value + hop(value, axis, devices, bit)
        bit //= 2
    return value


def fast_body(mesh):
    workers, devices = mesh.shape["worker"], mesh.shape["fsdp"]

    def body(
        params, first, second, global_fragment, outer_momentum, features, cotangent, token_counts, fragment_index
    ):
        rows, width = params.shape[1:]
        pieces, tokens = global_fragment.shape[0], features.shape[1]
        block = functools.partial(jax.ShapeDtypeStruct, dtype=jnp.float32)

        def cost(count):
            return pl.CostEstimate(
                flops=2 * count * tokens * rows * width,
                bytes_accessed=count * rows * (2 * tokens + 4 * width),
                transcendentals=0,
            )

        room = pltpu.CompilerParams(vmem_limit_bytes=ROOM)
        free = pl.CostEstimate(flops=0, bytes_accessed=0, transcendentals=0)
        far_counts, far_features, far_cotangent = (
            pltpu.with_memory_space_constraint(array, pltpu.HBM) for array in (token_counts, features, cotangent)
        )
        held_counts = pltpu.SMEM(token_counts.shape, token_counts.dtype)
        held_piece = pltpu.VMEM(global_fragment.shape, global_fragment.dtype)

        half = rows // 2
        away_far, kept_far, masked, info = pl.pallas_call(
            functools.partial(first_kernel, workers, (7, 6)),
            out_shape=[block((2, width, half))] * 2 + [jax.ShapeDtypeStruct((width, tokens), jnp.bfloat16), block((8, width))],
            in_specs=[HBM] * 3,
            out_specs=[VMEM] * 4,
            scratch_shapes=[
                held_counts,
                pltpu.VMEM(cotangent.shape, cotangent.dtype),
                pltpu.VMEM((2, tokens, rows), features.dtype),
                pltpu.SemaphoreType.DMA((4,)),
            ],
            compiler_params=room,
            cost_estimate=cost(2),
            name="far_products",
        )(far_counts, far_cotangent, far_features)
        away, kept = pl.pallas_call(
            rest_kernel,
            out_shape=[block((6, width, half))] * 2,
            in_specs=[VMEM] * 2,
            out_specs=[VMEM] * 2,
            compiler_params=room,
            cost_estimate=free,
            name="rest_products",
        )(masked, features)

        def add(*terms, name, count=1):
            picks = [pick for _, pick in terms]
            return pl.pallas_call(
                functools.partial(add_kernel, picks),
                out_shape=block((count, width, half)),
                in_specs=[ANY if pick is None else VMEM for pick in picks],
                out_specs=VMEM,
                compiler_params=room,
                cost_estimate=free,
                name=name,
            )(*(array for array, _ in terms))

        def part(number, count=1):
            return slice(number, number + count)

        state, piece = block(params.shape), block(global_fragment.shape)
        come_far = hop(away_far, "fsdp", devices, 1)
        sent = add((kept_far, part(0)), (come_far, part(0)), name="add_a1")
        far_left = hop(sent, "fsdp", devices, 2)
        away, _ = lax.optimization_barrier((away, sent))
        come = hop(away, "fsdp", devices, 1)
        drift, scale = pl.pallas_call(
            drift_kernel,
            out_shape=[piece, block((rows, width))],
            in_specs=[VMEM, SMEM, VMEM, VMEM, ANY],
            out_specs=[VMEM] * 2,
            compiler_params=room,
            cost_estimate=free,
            name="drift",
        )(info, fragment_index, params, global_fragment, sent)
        sent = add((kept_far, part(1)), (come_far, part(1)), (drift, None), name="add_a2")
        far_right = hop(sent, "fsdp", devices, 2)
        passed = add((kept, part(4)), (come, part(4)), (far_left, part(0)), name="add_c1")
        far_left = hop(passed, "fsdp", devices, 4)
        near_left = add((kept, part(2)), (come, part(2)), (sent, None), name="add_n1")
        far_right = add((kept, part(5)), (come, part(5)), (far_right, part(0)), (passed, None), name="add_c2")
        near_right = add((kept, part(3)), (come, part(3)), (passed, None), name="add_n2")
        drift, _ = lax.optimization_barrier((drift, sent))
        bit = workers // 2
        drifts = (drift, hop(drift, "worker", workers, bit))
        while bit > 1:
            bit //= 2
            drift = drifts[0] + drifts[1]
            drift, _ = lax.optimization_barrier((drift, near_right))
            drifts = (drift, hop(drift, "worker", workers, bit))
        near_left = hop(near_left, "fsdp", devices, 2)
        far_right = hop(far_right, "fsdp", devices, 4)
        near_right = hop(near_right, "fsdp", devices, 2)
        groups = half // LANES
        held_half = pltpu.VMEM((half, width), jnp.float32)
        mix, *results, new_global, new_momentum = pl.pallas_call(
            left_kernel,
            out_shape=[block((half, width)), state, state, state, piece, piece],
            in_specs=[VMEM] * 13,
            out_specs=[VMEM] + [HBM] * 5,
            scratch_shapes=[held_half] * 3
            + [held_piece] * 2
            + [pltpu.VMEM((rows, width), jnp.float32), pltpu.SemaphoreType.DMA((2 + 3 * groups,))],
            compiler_params=room,
            cost_estimate=pl.CostEstimate(
                flops=30 * half * width, bytes_accessed=40 * half * width, transcendentals=2 * half * width
            ),
            name="left_step",
        )(
            params,
            first,
            second,
            kept,
            come,
            far_left,
            near_left,
            info,
            scale,
            global_fragment,
            outer_momentum,
            *drifts,
        )
        new_params, new_first, new_second = pl.pallas_call(
            right_kernel,
            out_shape=[state] * 3,
            in_specs=[VMEM] * 10 + [HBM] * 3,
            out_specs=[HBM] * 3,
            input_output_aliases={10: 0, 11: 1, 12: 2},
            scratch_shapes=[held_half] * 3 + [pltpu.SemaphoreType.DMA((3 * groups,))],
            compiler_params=room,
            cost_estimate=free,
            name="right_step",
        )(params, first, second, kept, come, far_right, near_right, info, scale, mix, *results)
        return new_params, new_first, new_second, new_global, new_momentum

    return body


def plain_body(mesh):
    workers, devices = mesh.shape["worker"], mesh.shape["fsdp"]

    def body(
        params, first, second, global_fragment, outer_momentum, features, cotangent, token_counts, fragment_index
    ):
        rows, width = params.shape[1:]
        tokens = features.shape[1]
        me = lax.axis_index("fsdp")
        count = lax.dynamic_index_in_dim(token_counts, lax.axis_index("worker"), 0, keepdims=False)
        live = count.astype(jnp.float32)
        valid = (me * tokens + lax.iota(jnp.int32, tokens) < count)[:, None]
        masked = jnp.where(valid, cotangent[0], jnp.zeros_like(cotangent[0]))
        term = lax.dot_general(features[0], masked, (((0,), (0,)), ((), ())), preferred_element_type=jnp.float32)
        blocks = jnp.take(term.reshape(devices, rows, width), me ^ jnp.arange(devices, dtype=jnp.int32), axis=0)
        bit = 1
        while bit < devices:
            blocks = blocks.reshape(-1, 2, rows, width)
            blocks = blocks[:, 0] + hop(blocks[:, 1], "fsdp", devices, bit)
            bit *= 2
        gradient = blocks[0] / live
        grouped = (rows // FRAGS, FRAGS, width)
        old = lax.dynamic_index_in_dim(params[0].reshape(grouped), fragment_index[0], 1, keepdims=False)
        drift_sum = doubling_sum(live * (global_fragment - old), "worker", workers)
        total = jnp.sum(token_counts).astype(jnp.float32)
        fresh, momentum = outer(drift_sum / total, global_fragment, outer_momentum)
        inner, first_new, second_new = adam(params[0], first[0], second[0], gradient)
        inner = inner.reshape(grouped)
        piece = lax.dynamic_index_in_dim(inner, fragment_index[0], 1, keepdims=False)
        mixed = MIXING * fresh + (1.0 - MIXING) * piece
        merged = lax.dynamic_update_index_in_dim(inner, mixed, fragment_index[0], 1).reshape(rows, width)
        return merged[None], first_new[None], second_new[None], fresh, momentum

    return body


def solution(mesh):
    devices = mesh.shape["fsdp"]

    def pick(*arrays):
        rows = arrays[0].shape[1]
        body = fast_body(mesh) if devices == 8 and rows % LANES == 0 else plain_body(mesh)
        return body(*arrays)

    state = P("worker", "fsdp", None)
    piece = P("fsdp", None)
    return jax.shard_map(
        pick,
        mesh=mesh,
        in_specs=(state, state, state, piece, piece, state, state, P(), P()),
        out_specs=(state, state, state, piece, piece),
        check_vma=False,
    )
```

```python
import functools

import jax
import jax.numpy as jnp
from jax import lax
from jax.experimental import pallas as pl
from jax.experimental.pallas import tpu as pltpu
from jax.sharding import PartitionSpec as P

FRAGS = 4
LANES = 128

BETA_ONE = 0.9
BETA_TWO = 0.95
CORRECT_ONE = 0.6513216
CORRECT_TWO = 0.401263
ADAM_EPS = 1e-08
LEARN_RATE = 0.02
DECAY_RATE = 0.1
NESTEROV = 0.9
OUTER_RATE = 0.7
MIXING = 0.5

VMEM = pl.BlockSpec(memory_space=pltpu.VMEM)
SMEM = pl.BlockSpec(memory_space=pltpu.SMEM)
HBM = pl.BlockSpec(memory_space=pltpu.HBM)
ANY = pl.BlockSpec(memory_space=pl.ANY)
ROOM = 8 << 20


def masked_columns(live, cotangent):
    turned = cotangent.astype(jnp.float32).T
    tokens = lax.broadcasted_iota(jnp.int32, turned.shape, 1)
    return jnp.where(tokens < live, turned, 0.0).astype(jnp.bfloat16)


def columns_of(relative, rows, start, size):
    return pl.ds(pl.multiple_of((lax.axis_index("fsdp") ^ relative) * rows + start, LANES), size)


def product(masked, features):
    return jnp.dot(masked, features, preferred_element_type=jnp.float32)


def fetch(sources, targets, sems, start=0):
    copies = [
        pltpu.make_async_copy(source, target, sems.at[start + slot])
        for slot, (source, target) in enumerate(zip(sources, targets))
    ]
    for copy in copies:
        copy.start()
    return copies


def first_kernel(
    workers, order, counts, cotangent, features, away, kept, masked, info, counts_held, cot_held, held, sems
):
    half = away.shape[2]
    small = fetch((counts, cotangent), (counts_held, cot_held), sems)
    columns = [columns_of(q, 2 * half, 0, half) for q in order]
    blocks = fetch([features.at[0, :, c] for c in columns], [held.at[n] for n in range(len(order))], sems, len(small))
    for copy in small:
        copy.wait()
    tokens = cot_held.shape[1]
    live = counts_held[lax.axis_index("worker")] - lax.axis_index("fsdp") * tokens
    masked[...] = masked_columns(live, cot_held[0])
    for slot, into in enumerate((away, kept)):
        blocks[slot].wait()
        into[0] = product(masked[...], held[slot])
    count, total = counts_held[lax.axis_index("worker")], counts_held[0]
    for other in range(1, workers):
        total = total + counts_held[other]
    info[0:1, :] = jnp.full((1, info.shape[1]), count.astype(jnp.float32))
    info[1:2, :] = 1.0 / info[0:1, :]
    info[2:3, :] = 1.0 / jnp.full((1, info.shape[1]), total.astype(jnp.float32))


def rest_kernel(masked, features, away, kept):
    half = away.shape[2]
    for at, (q, side) in enumerate(((0, 0), (0, 1), (2, 0), (2, 1), (4, 0), (4, 1), (6, 1))):
        for core, into in ((1, away), (0, kept)):
            columns = columns_of(q + core, 2 * half, side * half, half)
            into[at] = product(masked[...], features[0, :, columns])


def drift_kernel(info, fragment, params, global_fragment, after, drift, scale):
    del after
    mine = pl.ds(fragment[0], drift.shape[0], stride=FRAGS)
    drift[...] = info[0:1, :] * (global_fragment[...] - params[0, mine, :])
    scale[...] = jnp.ones_like(scale)
    scale[mine, :] = jnp.full_like(drift, 1.0 - MIXING)


def add_kernel(picks, *refs):
    total = None
    for ref, pick in zip(refs, picks):
        if pick is not None:
            total = ref[pick] if total is None else total + ref[pick]
    refs[-1][...] = total


def adam(before, first, second, gradient):
    first_new = BETA_ONE * first + (1.0 - BETA_ONE) * gradient
    second_new = BETA_TWO * second + (1.0 - BETA_TWO) * gradient * gradient
    update = first_new * (1.0 / CORRECT_ONE) / (jnp.sqrt(second_new * (1.0 / CORRECT_TWO)) + ADAM_EPS)
    return before - LEARN_RATE * (update + DECAY_RATE * before), first_new, second_new


def outer(pseudo_grad, global_fragment, outer_momentum):
    momentum = NESTEROV * outer_momentum + pseudo_grad
    return global_fragment - OUTER_RATE * (pseudo_grad + NESTEROV * momentum), momentum


def half_step(half, states, sums, info, held):
    params, first, second = states
    kept, come, far, near = sums
    held_first, held_second = held
    rows = kept.shape[2]
    for lane in range(0, rows, LANES):
        lanes, there = pl.ds(lane, LANES), pl.ds(half * rows + lane, LANES)
        summed = kept[half, :, lanes] + come[half, :, lanes] + near[0, :, lanes] + far[0, :, lanes]
        inner, held_first[lanes, :], held_second[lanes, :] = adam(
            params[0, there, :], first[0, there, :], second[0, there, :], summed.T * info[1:2, :]
        )
        yield lanes, there, inner


def send(copies, sems, source, target):
    copies.append(pltpu.make_async_copy(source, target, sems.at[len(copies)]))
    copies[-1].start()


def left_kernel(
    params,
    first,
    second,
    kept,
    come,
    far,
    near,
    info,
    scale,
    global_fragment,
    outer_momentum,
    drift,
    other_drift,
    mix,
    new_params,
    new_first,
    new_second,
    new_global,
    new_momentum,
    held_params,
    held_first,
    held_second,
    held_global,
    held_momentum,
    spread,
    sems,
):
    copies = []
    fresh, momentum = outer((drift[...] + other_drift[...]) * info[2:3, :], global_fragment[...], outer_momentum[...])
    held_global[...] = fresh
    held_momentum[...] = momentum
    send(copies, sems, held_global, new_global)
    send(copies, sems, held_momentum, new_momentum)
    for at in range(FRAGS):
        spread[pl.ds(at, fresh.shape[0], stride=FRAGS), :] = fresh
    for lanes, there, value in half_step(
        0, (params, first, second), (kept, come, far, near), info, (held_first, held_second)
    ):
        held_params[lanes, :] = scale[there, :] * value + (1.0 - scale[there, :]) * spread[there, :]
        for source, target in ((held_first, new_first), (held_second, new_second), (held_params, new_params)):
            send(copies, sems, source.at[lanes], target.at[0, there])
    right = pl.ds(mix.shape[0], mix.shape[0])
    mix[...] = (1.0 - scale[right, :]) * spread[right, :]
    for copy in copies:
        copy.wait()


def right_kernel(
    params,
    first,
    second,
    kept,
    come,
    far,
    near,
    info,
    scale,
    mix,
    left_params,
    left_first,
    left_second,
    new_params,
    new_first,
    new_second,
    held_params,
    held_first,
    held_second,
    sems,
):
    del left_params, left_first, left_second
    copies = []
    for lanes, there, value in half_step(
        1, (params, first, second), (kept, come, far, near), info, (held_first, held_second)
    ):
        held_params[lanes, :] = scale[there, :] * value + mix[lanes, :]
        for source, target in ((held_first, new_first), (held_second, new_second), (held_params, new_params)):
            send(copies, sems, source.at[lanes], target.at[0, there])
    for copy in copies:
        copy.wait()


def hop(value, axis, devices, bit):
    return lax.ppermute(value, axis, [(d, d ^ bit) for d in range(devices)])


def doubling_sum(value, axis, devices):
    bit = devices // 2
    while bit:
        value = value + hop(value, axis, devices, bit)
        bit //= 2
    return value


def fast_body(mesh):
    workers, devices = mesh.shape["worker"], mesh.shape["fsdp"]

    def body(
        params, first, second, global_fragment, outer_momentum, features, cotangent, token_counts, fragment_index
    ):
        rows, width = params.shape[1:]
        pieces, tokens = global_fragment.shape[0], features.shape[1]
        block = functools.partial(jax.ShapeDtypeStruct, dtype=jnp.float32)

        def cost(count):
            return pl.CostEstimate(
                flops=2 * count * tokens * rows * width,
                bytes_accessed=count * rows * (2 * tokens + 4 * width),
                transcendentals=0,
            )

        room = pltpu.CompilerParams(vmem_limit_bytes=ROOM)
        free = pl.CostEstimate(flops=0, bytes_accessed=0, transcendentals=0)
        far_counts, far_features, far_cotangent = (
            pltpu.with_memory_space_constraint(array, pltpu.HBM) for array in (token_counts, features, cotangent)
        )
        held_counts = pltpu.SMEM(token_counts.shape, token_counts.dtype)
        held_piece = pltpu.VMEM(global_fragment.shape, global_fragment.dtype)

        half = rows // 2
        away_far, kept_far, masked, info = pl.pallas_call(
            functools.partial(first_kernel, workers, (7, 6)),
            out_shape=[block((1, width, half))] * 2 + [jax.ShapeDtypeStruct((width, tokens), jnp.bfloat16), block((8, width))],
            in_specs=[HBM] * 3,
            out_specs=[VMEM] * 4,
            scratch_shapes=[
                held_counts,
                pltpu.VMEM(cotangent.shape, cotangent.dtype),
                pltpu.VMEM((2, tokens, half), features.dtype),
                pltpu.SemaphoreType.DMA((4,)),
            ],
            compiler_params=room,
            cost_estimate=cost(2),
            name="far_products",
        )(far_counts, far_cotangent, far_features)
        away, kept = pl.pallas_call(
            rest_kernel,
            out_shape=[block((7, width, half))] * 2,
            in_specs=[VMEM] * 2,
            out_specs=[VMEM] * 2,
            compiler_params=room,
            cost_estimate=free,
            name="rest_products",
        )(masked, features)

        def add(*terms, name, count=1):
            picks = [pick for _, pick in terms]
            return pl.pallas_call(
                functools.partial(add_kernel, picks),
                out_shape=block((count, width, half)),
                in_specs=[ANY if pick is None else VMEM for pick in picks],
                out_specs=VMEM,
                compiler_params=room,
                cost_estimate=free,
                name=name,
            )(*(array for array, _ in terms))

        def part(number, count=1):
            return slice(number, number + count)

        state, piece = block(params.shape), block(global_fragment.shape)
        come_far = hop(away_far, "fsdp", devices, 1)
        sent = add((kept_far, part(0)), (come_far, part(0)), (fragment_index, None), name="add_a1")
        far_left = hop(sent, "fsdp", devices, 2)
        away, _ = lax.optimization_barrier((away, sent))
        come = hop(away, "fsdp", devices, 1)
        drift, scale = pl.pallas_call(
            drift_kernel,
            out_shape=[piece, block((rows, width))],
            in_specs=[VMEM, SMEM, VMEM, VMEM, ANY],
            out_specs=[VMEM] * 2,
            compiler_params=room,
            cost_estimate=free,
            name="drift",
        )(info, fragment_index, params, global_fragment, sent)
        sent = add((kept, part(6)), (come, part(6)), (drift, None), name="add_a2")
        far_right = hop(sent, "fsdp", devices, 2)
        passed = add((kept, part(4)), (come, part(4)), (far_left, part(0)), name="add_c1")
        far_left = hop(passed, "fsdp", devices, 4)
        near_left = add((kept, part(2)), (come, part(2)), (sent, None), name="add_n1")
        far_right = add((kept, part(5)), (come, part(5)), (far_right, part(0)), (passed, None), name="add_c2")
        near_right = add((kept, part(3)), (come, part(3)), (passed, None), name="add_n2")
        drift, _ = lax.optimization_barrier((drift, sent))
        bit = workers // 2
        drifts = (drift, hop(drift, "worker", workers, bit))
        while bit > 1:
            bit //= 2
            drift = drifts[0] + drifts[1]
            drift, _ = lax.optimization_barrier((drift, near_right))
            drifts = (drift, hop(drift, "worker", workers, bit))
        near_left = hop(near_left, "fsdp", devices, 2)
        far_right = hop(far_right, "fsdp", devices, 4)
        near_right = hop(near_right, "fsdp", devices, 2)
        groups = half // LANES
        held_half = pltpu.VMEM((half, width), jnp.float32)
        mix, *results, new_global, new_momentum = pl.pallas_call(
            left_kernel,
            out_shape=[block((half, width)), state, state, state, piece, piece],
            in_specs=[VMEM] * 13,
            out_specs=[VMEM] + [HBM] * 5,
            scratch_shapes=[held_half] * 3
            + [held_piece] * 2
            + [pltpu.VMEM((rows, width), jnp.float32), pltpu.SemaphoreType.DMA((2 + 3 * groups,))],
            compiler_params=room,
            cost_estimate=pl.CostEstimate(
                flops=30 * half * width, bytes_accessed=40 * half * width, transcendentals=2 * half * width
            ),
            name="left_step",
        )(
            params,
            first,
            second,
            kept,
            come,
            far_left,
            near_left,
            info,
            scale,
            global_fragment,
            outer_momentum,
            *drifts,
        )
        new_params, new_first, new_second = pl.pallas_call(
            right_kernel,
            out_shape=[state] * 3,
            in_specs=[VMEM] * 10 + [HBM] * 3,
            out_specs=[HBM] * 3,
            input_output_aliases={10: 0, 11: 1, 12: 2},
            scratch_shapes=[held_half] * 3 + [pltpu.SemaphoreType.DMA((3 * groups,))],
            compiler_params=room,
            cost_estimate=free,
            name="right_step",
        )(params, first, second, kept, come, far_right, near_right, info, scale, mix, *results)
        return new_params, new_first, new_second, new_global, new_momentum

    return body


def plain_body(mesh):
    workers, devices = mesh.shape["worker"], mesh.shape["fsdp"]

    def body(
        params, first, second, global_fragment, outer_momentum, features, cotangent, token_counts, fragment_index
    ):
        rows, width = params.shape[1:]
        tokens = features.shape[1]
        me = lax.axis_index("fsdp")
        count = lax.dynamic_index_in_dim(token_counts, lax.axis_index("worker"), 0, keepdims=False)
        live = count.astype(jnp.float32)
        valid = (me * tokens + lax.iota(jnp.int32, tokens) < count)[:, None]
        masked = jnp.where(valid, cotangent[0], jnp.zeros_like(cotangent[0]))
        term = lax.dot_general(features[0], masked, (((0,), (0,)), ((), ())), preferred_element_type=jnp.float32)
        blocks = jnp.take(term.reshape(devices, rows, width), me ^ jnp.arange(devices, dtype=jnp.int32), axis=0)
        bit = 1
        while bit < devices:
            blocks = blocks.reshape(-1, 2, rows, width)
            blocks = blocks[:, 0] + hop(blocks[:, 1], "fsdp", devices, bit)
            bit *= 2
        gradient = blocks[0] / live
        grouped = (rows // FRAGS, FRAGS, width)
        old = lax.dynamic_index_in_dim(params[0].reshape(grouped), fragment_index[0], 1, keepdims=False)
        drift_sum = doubling_sum(live * (global_fragment - old), "worker", workers)
        total = jnp.sum(token_counts).astype(jnp.float32)
        fresh, momentum = outer(drift_sum / total, global_fragment, outer_momentum)
        inner, first_new, second_new = adam(params[0], first[0], second[0], gradient)
        inner = inner.reshape(grouped)
        piece = lax.dynamic_index_in_dim(inner, fragment_index[0], 1, keepdims=False)
        mixed = MIXING * fresh + (1.0 - MIXING) * piece
        merged = lax.dynamic_update_index_in_dim(inner, mixed, fragment_index[0], 1).reshape(rows, width)
        return merged[None], first_new[None], second_new[None], fresh, momentum

    return body


def solution(mesh):
    devices = mesh.shape["fsdp"]

    def pick(*arrays):
        rows = arrays[0].shape[1]
        body = fast_body(mesh) if devices == 8 and rows % LANES == 0 else plain_body(mesh)
        return body(*arrays)

    state = P("worker", "fsdp", None)
    piece = P("fsdp", None)
    return jax.shard_map(
        pick,
        mesh=mesh,
        in_specs=(state, state, state, piece, piece, state, state, P(), P()),
        out_specs=(state, state, state, piece, piece),
        check_vma=False,
    )
```

```python
import functools

import jax
import jax.numpy as jnp
from jax import lax
from jax.experimental import pallas as pl
from jax.experimental.pallas import tpu as pltpu
from jax.sharding import PartitionSpec as P

FRAGS = 4
LANES = 128

BETA_ONE = 0.9
BETA_TWO = 0.95
CORRECT_ONE = 0.6513216
CORRECT_TWO = 0.401263
ADAM_EPS = 1e-08
LEARN_RATE = 0.02
DECAY_RATE = 0.1
NESTEROV = 0.9
OUTER_RATE = 0.7
MIXING = 0.5

VMEM = pl.BlockSpec(memory_space=pltpu.VMEM)
SMEM = pl.BlockSpec(memory_space=pltpu.SMEM)
HBM = pl.BlockSpec(memory_space=pltpu.HBM)
ANY = pl.BlockSpec(memory_space=pl.ANY)
ROOM = 8 << 20


def masked_columns(live, cotangent):
    turned = cotangent.astype(jnp.float32).T
    tokens = lax.broadcasted_iota(jnp.int32, turned.shape, 1)
    return jnp.where(tokens < live, turned, 0.0).astype(jnp.bfloat16)


def columns_of(relative, rows, start, size):
    return pl.ds(pl.multiple_of((lax.axis_index("fsdp") ^ relative) * rows + start, LANES), size)


def product(masked, features):
    return jnp.dot(masked, features, preferred_element_type=jnp.float32)


def fetch(sources, targets, sems, start=0):
    copies = [
        pltpu.make_async_copy(source, target, sems.at[start + slot])
        for slot, (source, target) in enumerate(zip(sources, targets))
    ]
    for copy in copies:
        copy.start()
    return copies


def first_kernel(
    workers, order, counts, cotangent, features, away, kept, masked, info, counts_held, cot_held, held, sems
):
    half = away.shape[2]
    small = fetch((counts, cotangent), (counts_held, cot_held), sems)
    columns = [columns_of(q, 2 * half, 0, half) for q in order]
    blocks = fetch([features.at[0, :, c] for c in columns], [held.at[n] for n in range(len(order))], sems, len(small))
    for copy in small:
        copy.wait()
    tokens = cot_held.shape[1]
    live = counts_held[lax.axis_index("worker")] - lax.axis_index("fsdp") * tokens
    masked[...] = masked_columns(live, cot_held[0])
    for slot, into in enumerate((away, kept)):
        blocks[slot].wait()
        into[0] = product(masked[...], held[slot])
    count, total = counts_held[lax.axis_index("worker")], counts_held[0]
    for other in range(1, workers):
        total = total + counts_held[other]
    info[0:1, :] = jnp.full((1, info.shape[1]), count.astype(jnp.float32))
    info[1:2, :] = 1.0 / info[0:1, :]
    info[2:3, :] = 1.0 / jnp.full((1, info.shape[1]), total.astype(jnp.float32))


def rest_kernel(masked, features, away, kept):
    half = away.shape[2]
    for at, (q, side) in enumerate(((0, 0), (0, 1), (2, 0), (2, 1), (4, 0), (4, 1), (6, 1))):
        for core, into in ((1, away), (0, kept)):
            columns = columns_of(q + core, 2 * half, side * half, half)
            into[at] = product(masked[...], features[0, :, columns])


def drift_kernel(info, fragment, params, global_fragment, after, drift, scale):
    del after
    index = fragment[0]
    pieces = drift.shape[0]
    old = params[0, pl.ds(0, pieces, stride=FRAGS), :]
    for at in range(1, FRAGS):
        old = jnp.where(index == at, params[0, pl.ds(at, pieces, stride=FRAGS), :], old)
    drift[...] = info[0:1, :] * (global_fragment[...] - old)
    rows = lax.broadcasted_iota(jnp.int32, scale.shape, 0)
    scale[...] = jnp.where(lax.rem(rows, FRAGS) == index, 1.0 - MIXING, 1.0)


def add_kernel(picks, *refs):
    total = None
    for ref, pick in zip(refs, picks):
        if pick is not None:
            total = ref[pick] if total is None else total + ref[pick]
    refs[-1][...] = total


def adam(before, first, second, gradient):
    first_new = BETA_ONE * first + (1.0 - BETA_ONE) * gradient
    second_new = BETA_TWO * second + (1.0 - BETA_TWO) * gradient * gradient
    update = first_new * (1.0 / CORRECT_ONE) / (jnp.sqrt(second_new * (1.0 / CORRECT_TWO)) + ADAM_EPS)
    return before - LEARN_RATE * (update + DECAY_RATE * before), first_new, second_new


def outer(pseudo_grad, global_fragment, outer_momentum):
    momentum = NESTEROV * outer_momentum + pseudo_grad
    return global_fragment - OUTER_RATE * (pseudo_grad + NESTEROV * momentum), momentum


def half_step(half, states, sums, info, held):
    params, first, second = states
    kept, come, far, near = sums
    held_first, held_second = held
    rows = kept.shape[2]
    for lane in range(0, rows, LANES):
        lanes, there = pl.ds(lane, LANES), pl.ds(half * rows + lane, LANES)
        summed = kept[half, :, lanes] + come[half, :, lanes] + near[0, :, lanes] + far[0, :, lanes]
        inner, held_first[lanes, :], held_second[lanes, :] = adam(
            params[0, there, :], first[0, there, :], second[0, there, :], summed.T * info[1:2, :]
        )
        yield lanes, there, inner


def send(copies, sems, source, target):
    copies.append(pltpu.make_async_copy(source, target, sems.at[len(copies)]))
    copies[-1].start()


def left_kernel(
    params,
    first,
    second,
    kept,
    come,
    far,
    near,
    info,
    scale,
    global_fragment,
    outer_momentum,
    drift,
    other_drift,
    mix,
    new_params,
    new_first,
    new_second,
    new_global,
    new_momentum,
    held_params,
    held_first,
    held_second,
    held_global,
    held_momentum,
    spread,
    sems,
):
    copies = []
    fresh, momentum = outer((drift[...] + other_drift[...]) * info[2:3, :], global_fragment[...], outer_momentum[...])
    held_global[...] = fresh
    held_momentum[...] = momentum
    send(copies, sems, held_global, new_global)
    send(copies, sems, held_momentum, new_momentum)
    for at in range(FRAGS):
        spread[pl.ds(at, fresh.shape[0], stride=FRAGS), :] = fresh
    for lanes, there, value in half_step(
        0, (params, first, second), (kept, come, far, near), info, (held_first, held_second)
    ):
        held_params[lanes, :] = scale[there, :] * value + (1.0 - scale[there, :]) * spread[there, :]
        for source, target in ((held_first, new_first), (held_second, new_second), (held_params, new_params)):
            send(copies, sems, source.at[lanes], target.at[0, there])
    right = pl.ds(mix.shape[0], mix.shape[0])
    mix[...] = (1.0 - scale[right, :]) * spread[right, :]
    for copy in copies:
        copy.wait()


def right_kernel(
    params,
    first,
    second,
    kept,
    come,
    far,
    near,
    info,
    scale,
    mix,
    left_params,
    left_first,
    left_second,
    new_params,
    new_first,
    new_second,
    held_params,
    held_first,
    held_second,
    sems,
):
    del left_params, left_first, left_second
    copies = []
    for lanes, there, value in half_step(
        1, (params, first, second), (kept, come, far, near), info, (held_first, held_second)
    ):
        held_params[lanes, :] = scale[there, :] * value + mix[lanes, :]
        for source, target in ((held_first, new_first), (held_second, new_second), (held_params, new_params)):
            send(copies, sems, source.at[lanes], target.at[0, there])
    for copy in copies:
        copy.wait()


def hop(value, axis, devices, bit):
    return lax.ppermute(value, axis, [(d, d ^ bit) for d in range(devices)])


def doubling_sum(value, axis, devices):
    bit = devices // 2
    while bit:
        value = value + hop(value, axis, devices, bit)
        bit //= 2
    return value


def fast_body(mesh):
    workers, devices = mesh.shape["worker"], mesh.shape["fsdp"]

    def body(
        params, first, second, global_fragment, outer_momentum, features, cotangent, token_counts, fragment_index
    ):
        rows, width = params.shape[1:]
        pieces, tokens = global_fragment.shape[0], features.shape[1]
        block = functools.partial(jax.ShapeDtypeStruct, dtype=jnp.float32)

        def cost(count):
            return pl.CostEstimate(
                flops=2 * count * tokens * rows * width,
                bytes_accessed=count * rows * (2 * tokens + 4 * width),
                transcendentals=0,
            )

        room = pltpu.CompilerParams(vmem_limit_bytes=ROOM)
        free = pl.CostEstimate(flops=0, bytes_accessed=0, transcendentals=0)
        far_counts, far_features, far_cotangent = (
            pltpu.with_memory_space_constraint(array, pltpu.HBM) for array in (token_counts, features, cotangent)
        )
        held_counts = pltpu.SMEM(token_counts.shape, token_counts.dtype)
        held_piece = pltpu.VMEM(global_fragment.shape, global_fragment.dtype)

        half = rows // 2
        away_far, kept_far, masked, info = pl.pallas_call(
            functools.partial(first_kernel, workers, (7, 6)),
            out_shape=[block((1, width, half))] * 2 + [jax.ShapeDtypeStruct((width, tokens), jnp.bfloat16), block((8, width))],
            in_specs=[HBM] * 3,
            out_specs=[VMEM] * 4,
            scratch_shapes=[
                held_counts,
                pltpu.VMEM(cotangent.shape, cotangent.dtype),
                pltpu.VMEM((2, tokens, half), features.dtype),
                pltpu.SemaphoreType.DMA((4,)),
            ],
            compiler_params=room,
            cost_estimate=cost(2),
            name="far_products",
        )(far_counts, far_cotangent, far_features)
        away, kept = pl.pallas_call(
            rest_kernel,
            out_shape=[block((7, width, half))] * 2,
            in_specs=[VMEM] * 2,
            out_specs=[VMEM] * 2,
            compiler_params=room,
            cost_estimate=free,
            name="rest_products",
        )(masked, features)

        def add(*terms, name, count=1):
            picks = [pick for _, pick in terms]
            return pl.pallas_call(
                functools.partial(add_kernel, picks),
                out_shape=block((count, width, half)),
                in_specs=[ANY if pick is None else VMEM for pick in picks],
                out_specs=VMEM,
                compiler_params=room,
                cost_estimate=free,
                name=name,
            )(*(array for array, _ in terms))

        def part(number, count=1):
            return slice(number, number + count)

        state, piece = block(params.shape), block(global_fragment.shape)
        come_far = hop(away_far, "fsdp", devices, 1)
        sent = add((kept_far, part(0)), (come_far, part(0)), (fragment_index, None), name="add_a1")
        far_left = hop(sent, "fsdp", devices, 2)
        away, _ = lax.optimization_barrier((away, sent))
        come = hop(away, "fsdp", devices, 1)
        drift, scale = pl.pallas_call(
            drift_kernel,
            out_shape=[piece, block((rows, width))],
            in_specs=[VMEM, SMEM, VMEM, VMEM, ANY],
            out_specs=[VMEM] * 2,
            compiler_params=room,
            cost_estimate=free,
            name="drift",
        )(info, fragment_index, params, global_fragment, sent)
        sent = add((kept, part(6)), (come, part(6)), (drift, None), name="add_a2")
        far_right = hop(sent, "fsdp", devices, 2)
        passed = add((kept, part(4)), (come, part(4)), (far_left, part(0)), name="add_c1")
        far_left = hop(passed, "fsdp", devices, 4)
        near_left = add((kept, part(2)), (come, part(2)), (sent, None), name="add_n1")
        far_right = add((kept, part(5)), (come, part(5)), (far_right, part(0)), (passed, None), name="add_c2")
        near_right = add((kept, part(3)), (come, part(3)), (passed, None), name="add_n2")
        drift, _ = lax.optimization_barrier((drift, sent))
        bit = workers // 2
        drifts = (drift, hop(drift, "worker", workers, bit))
        while bit > 1:
            bit //= 2
            drift = drifts[0] + drifts[1]
            drift, _ = lax.optimization_barrier((drift, near_right))
            drifts = (drift, hop(drift, "worker", workers, bit))
        near_left = hop(near_left, "fsdp", devices, 2)
        far_right = hop(far_right, "fsdp", devices, 4)
        near_right = hop(near_right, "fsdp", devices, 2)
        groups = half // LANES
        held_half = pltpu.VMEM((half, width), jnp.float32)
        mix, *results, new_global, new_momentum = pl.pallas_call(
            left_kernel,
            out_shape=[block((half, width)), state, state, state, piece, piece],
            in_specs=[VMEM] * 13,
            out_specs=[VMEM] + [HBM] * 5,
            scratch_shapes=[held_half] * 3
            + [held_piece] * 2
            + [pltpu.VMEM((rows, width), jnp.float32), pltpu.SemaphoreType.DMA((2 + 3 * groups,))],
            compiler_params=room,
            cost_estimate=pl.CostEstimate(
                flops=30 * half * width, bytes_accessed=40 * half * width, transcendentals=2 * half * width
            ),
            name="left_step",
        )(
            params,
            first,
            second,
            kept,
            come,
            far_left,
            near_left,
            info,
            scale,
            global_fragment,
            outer_momentum,
            *drifts,
        )
        new_params, new_first, new_second = pl.pallas_call(
            right_kernel,
            out_shape=[state] * 3,
            in_specs=[VMEM] * 10 + [HBM] * 3,
            out_specs=[HBM] * 3,
            input_output_aliases={10: 0, 11: 1, 12: 2},
            scratch_shapes=[held_half] * 3 + [pltpu.SemaphoreType.DMA((3 * groups,))],
            compiler_params=room,
            cost_estimate=free,
            name="right_step",
        )(params, first, second, kept, come, far_right, near_right, info, scale, mix, *results)
        return new_params, new_first, new_second, new_global, new_momentum

    return body


def plain_body(mesh):
    workers, devices = mesh.shape["worker"], mesh.shape["fsdp"]

    def body(
        params, first, second, global_fragment, outer_momentum, features, cotangent, token_counts, fragment_index
    ):
        rows, width = params.shape[1:]
        tokens = features.shape[1]
        me = lax.axis_index("fsdp")
        count = lax.dynamic_index_in_dim(token_counts, lax.axis_index("worker"), 0, keepdims=False)
        live = count.astype(jnp.float32)
        valid = (me * tokens + lax.iota(jnp.int32, tokens) < count)[:, None]
        masked = jnp.where(valid, cotangent[0], jnp.zeros_like(cotangent[0]))
        term = lax.dot_general(features[0], masked, (((0,), (0,)), ((), ())), preferred_element_type=jnp.float32)
        blocks = jnp.take(term.reshape(devices, rows, width), me ^ jnp.arange(devices, dtype=jnp.int32), axis=0)
        bit = 1
        while bit < devices:
            blocks = blocks.reshape(-1, 2, rows, width)
            blocks = blocks[:, 0] + hop(blocks[:, 1], "fsdp", devices, bit)
            bit *= 2
        gradient = blocks[0] / live
        grouped = (rows // FRAGS, FRAGS, width)
        old = lax.dynamic_index_in_dim(params[0].reshape(grouped), fragment_index[0], 1, keepdims=False)
        drift_sum = doubling_sum(live * (global_fragment - old), "worker", workers)
        total = jnp.sum(token_counts).astype(jnp.float32)
        fresh, momentum = outer(drift_sum / total, global_fragment, outer_momentum)
        inner, first_new, second_new = adam(params[0], first[0], second[0], gradient)
        inner = inner.reshape(grouped)
        piece = lax.dynamic_index_in_dim(inner, fragment_index[0], 1, keepdims=False)
        mixed = MIXING * fresh + (1.0 - MIXING) * piece
        merged = lax.dynamic_update_index_in_dim(inner, mixed, fragment_index[0], 1).reshape(rows, width)
        return merged[None], first_new[None], second_new[None], fresh, momentum

    return body


def solution(mesh):
    devices = mesh.shape["fsdp"]

    def pick(*arrays):
        rows = arrays[0].shape[1]
        body = fast_body(mesh) if devices == 8 and rows % LANES == 0 else plain_body(mesh)
        return body(*arrays)

    state = P("worker", "fsdp", None)
    piece = P("fsdp", None)
    return jax.shard_map(
        pick,
        mesh=mesh,
        in_specs=(state, state, state, piece, piece, state, state, P(), P()),
        out_specs=(state, state, state, piece, piece),
        check_vma=False,
    )
```

```python
import functools

import jax
import jax.numpy as jnp
from jax import lax
from jax.experimental import pallas as pl
from jax.experimental.pallas import tpu as pltpu
from jax.sharding import PartitionSpec as P

FRAGS = 4
LANES = 128

BETA_ONE = 0.9
BETA_TWO = 0.95
CORRECT_ONE = 0.6513216
CORRECT_TWO = 0.401263
ADAM_EPS = 1e-08
LEARN_RATE = 0.02
DECAY_RATE = 0.1
NESTEROV = 0.9
OUTER_RATE = 0.7
MIXING = 0.5

VMEM = pl.BlockSpec(memory_space=pltpu.VMEM)
SMEM = pl.BlockSpec(memory_space=pltpu.SMEM)
HBM = pl.BlockSpec(memory_space=pltpu.HBM)
ANY = pl.BlockSpec(memory_space=pl.ANY)
ROOM = 8 << 20


def masked_columns(live, cotangent):
    turned = cotangent.astype(jnp.float32).T
    tokens = lax.broadcasted_iota(jnp.int32, turned.shape, 1)
    return jnp.where(tokens < live, turned, 0.0).astype(jnp.bfloat16)


def columns_of(relative, rows, start, size):
    return pl.ds(pl.multiple_of((lax.axis_index("fsdp") ^ relative) * rows + start, LANES), size)


def product(masked, features):
    return jnp.dot(masked, features, preferred_element_type=jnp.float32)


def fetch(sources, targets, sems, start=0):
    copies = [
        pltpu.make_async_copy(source, target, sems.at[start + slot])
        for slot, (source, target) in enumerate(zip(sources, targets))
    ]
    for copy in copies:
        copy.start()
    return copies


def first_kernel(
    workers, order, counts, cotangent, features, away, kept, masked, info, counts_held, cot_held, held, sems
):
    half = away.shape[2]
    small = fetch((counts, cotangent), (counts_held, cot_held), sems)
    columns = [columns_of(q, 2 * half, 0, half) for q in order]
    blocks = fetch([features.at[0, :, c] for c in columns], [held.at[n] for n in range(len(order))], sems, len(small))
    for copy in small:
        copy.wait()
    tokens = cot_held.shape[1]
    live = counts_held[lax.axis_index("worker")] - lax.axis_index("fsdp") * tokens
    masked[...] = masked_columns(live, cot_held[0])
    for slot, into in enumerate((away, kept)):
        blocks[slot].wait()
        into[0] = product(masked[...], held[slot])
    count, total = counts_held[lax.axis_index("worker")], counts_held[0]
    for other in range(1, workers):
        total = total + counts_held[other]
    info[0:1, :] = jnp.full((1, info.shape[1]), count.astype(jnp.float32))
    info[1:2, :] = 1.0 / info[0:1, :]
    info[2:3, :] = 1.0 / jnp.full((1, info.shape[1]), total.astype(jnp.float32))


def rest_kernel(masked, features, away, kept):
    half = away.shape[2]
    for at, (q, side) in enumerate(((0, 0), (0, 1), (2, 0), (2, 1), (4, 0), (4, 1), (6, 1))):
        for core, into in ((1, away), (0, kept)):
            columns = columns_of(q + core, 2 * half, side * half, half)
            into[at] = product(masked[...], features[0, :, columns])


def drift_kernel(info, fragment, params, global_fragment, after, drift, scale):
    del after
    index = fragment[0]
    pieces = drift.shape[0]
    old = params[0, pl.ds(0, pieces, stride=FRAGS), :]
    for at in range(1, FRAGS):
        old = jnp.where(index == at, params[0, pl.ds(at, pieces, stride=FRAGS), :], old)
    drift[...] = info[0:1, :] * (global_fragment[...] - old)
    rows = lax.broadcasted_iota(jnp.int32, scale.shape, 0)
    scale[...] = jnp.where(lax.rem(rows, FRAGS) == index, 1.0 - MIXING, 1.0)


def add_kernel(picks, *refs):
    total = None
    for ref, pick in zip(refs, picks):
        if pick is not None:
            total = ref[pick] if total is None else total + ref[pick]
    refs[-1][...] = total


def adam(before, first, second, gradient):
    first_new = BETA_ONE * first + (1.0 - BETA_ONE) * gradient
    second_new = BETA_TWO * second + (1.0 - BETA_TWO) * gradient * gradient
    update = first_new * (1.0 / CORRECT_ONE) / (jnp.sqrt(second_new * (1.0 / CORRECT_TWO)) + ADAM_EPS)
    return before - LEARN_RATE * (update + DECAY_RATE * before), first_new, second_new


def outer(pseudo_grad, global_fragment, outer_momentum):
    momentum = NESTEROV * outer_momentum + pseudo_grad
    return global_fragment - OUTER_RATE * (pseudo_grad + NESTEROV * momentum), momentum


def half_step(half, states, sums, info, held):
    params, first, second = states
    kept, come, far, near = sums
    held_first, held_second = held
    rows = kept.shape[2]
    for lane in range(0, rows, LANES):
        lanes, there = pl.ds(lane, LANES), pl.ds(half * rows + lane, LANES)
        summed = kept[half, :, lanes] + come[half, :, lanes] + near[0, :, lanes] + far[0, :, lanes]
        inner, held_first[lanes, :], held_second[lanes, :] = adam(
            params[0, there, :], first[0, there, :], second[0, there, :], summed.T * info[1:2, :]
        )
        yield lanes, there, inner


def send(copies, sems, source, target):
    copies.append(pltpu.make_async_copy(source, target, sems.at[len(copies)]))
    copies[-1].start()


def left_kernel(
    params,
    first,
    second,
    kept,
    come,
    far,
    near,
    info,
    scale,
    global_fragment,
    outer_momentum,
    drift,
    other_drift,
    own,
    first_base,
    second_base,
    base,
    step,
    new_params,
    new_first,
    new_second,
    new_global,
    new_momentum,
    held_params,
    held_first,
    held_second,
    held_global,
    held_momentum,
    spread,
    sems,
):
    copies = []
    fresh, momentum = outer((drift[...] + other_drift[...]) * info[2:3, :], global_fragment[...], outer_momentum[...])
    held_global[...] = fresh
    held_momentum[...] = momentum
    send(copies, sems, held_global, new_global)
    send(copies, sems, held_momentum, new_momentum)
    for at in range(FRAGS):
        spread[pl.ds(at, fresh.shape[0], stride=FRAGS), :] = fresh
    for lanes, there, value in half_step(
        0, (params, first, second), (kept, come, far, near), info, (held_first, held_second)
    ):
        held_params[lanes, :] = scale[there, :] * value + (1.0 - scale[there, :]) * spread[there, :]
        for source, target in ((held_first, new_first), (held_second, new_second), (held_params, new_params)):
            send(copies, sems, source.at[lanes], target.at[0, there])
    rows = own.shape[0]
    for lane in range(0, rows, LANES):
        lanes, there = pl.ds(lane, LANES), pl.ds(rows + lane, LANES)
        own[lanes, :] = (kept[1, :, lanes] + come[1, :, lanes]).T * info[1:2, :]
        first_base[lanes, :] = BETA_ONE * first[0, there, :]
        second_base[lanes, :] = BETA_TWO * second[0, there, :]
        base[lanes, :] = scale[there, :] * ((1.0 - LEARN_RATE * DECAY_RATE) * params[0, there, :]) + (
            1.0 - scale[there, :]
        ) * spread[there, :]
        step[lanes, :] = (LEARN_RATE / CORRECT_ONE) * scale[there, :]
    for copy in copies:
        copy.wait()


def right_kernel(
    far,
    near,
    info,
    own,
    first_base,
    second_base,
    base,
    step,
    left_params,
    left_first,
    left_second,
    new_params,
    new_first,
    new_second,
    held_params,
    held_first,
    held_second,
    sems,
):
    del left_params, left_first, left_second
    copies = []
    rows = own.shape[0]
    for lane in range(0, rows, LANES):
        lanes, there = pl.ds(lane, LANES), pl.ds(rows + lane, LANES)
        gradient = own[lanes, :] + (near[0, :, lanes] + far[0, :, lanes]).T * info[1:2, :]
        first_new = first_base[lanes, :] + (1.0 - BETA_ONE) * gradient
        second_new = second_base[lanes, :] + (1.0 - BETA_TWO) * gradient * gradient
        held_first[lanes, :] = first_new
        held_second[lanes, :] = second_new
        held_params[lanes, :] = base[lanes, :] - step[lanes, :] * first_new / (
            jnp.sqrt(second_new * (1.0 / CORRECT_TWO)) + ADAM_EPS
        )
        for source, target in ((held_first, new_first), (held_second, new_second), (held_params, new_params)):
            send(copies, sems, source.at[lanes], target.at[0, there])
    for copy in copies:
        copy.wait()


def hop(value, axis, devices, bit):
    return lax.ppermute(value, axis, [(d, d ^ bit) for d in range(devices)])


def doubling_sum(value, axis, devices):
    bit = devices // 2
    while bit:
        value = value + hop(value, axis, devices, bit)
        bit //= 2
    return value


def fast_body(mesh):
    workers, devices = mesh.shape["worker"], mesh.shape["fsdp"]

    def body(
        params, first, second, global_fragment, outer_momentum, features, cotangent, token_counts, fragment_index
    ):
        rows, width = params.shape[1:]
        pieces, tokens = global_fragment.shape[0], features.shape[1]
        block = functools.partial(jax.ShapeDtypeStruct, dtype=jnp.float32)

        def cost(count):
            return pl.CostEstimate(
                flops=2 * count * tokens * rows * width,
                bytes_accessed=count * rows * (2 * tokens + 4 * width),
                transcendentals=0,
            )

        room = pltpu.CompilerParams(vmem_limit_bytes=ROOM)
        free = pl.CostEstimate(flops=0, bytes_accessed=0, transcendentals=0)
        far_counts, far_features, far_cotangent = (
            pltpu.with_memory_space_constraint(array, pltpu.HBM) for array in (token_counts, features, cotangent)
        )
        held_counts = pltpu.SMEM(token_counts.shape, token_counts.dtype)
        held_piece = pltpu.VMEM(global_fragment.shape, global_fragment.dtype)

        half = rows // 2
        away_far, kept_far, masked, info = pl.pallas_call(
            functools.partial(first_kernel, workers, (7, 6)),
            out_shape=[block((1, width, half))] * 2 + [jax.ShapeDtypeStruct((width, tokens), jnp.bfloat16), block((8, width))],
            in_specs=[HBM] * 3,
            out_specs=[VMEM] * 4,
            scratch_shapes=[
                held_counts,
                pltpu.VMEM(cotangent.shape, cotangent.dtype),
                pltpu.VMEM((2, tokens, half), features.dtype),
                pltpu.SemaphoreType.DMA((4,)),
            ],
            compiler_params=room,
            cost_estimate=cost(2),
            name="far_products",
        )(far_counts, far_cotangent, far_features)
        away, kept = pl.pallas_call(
            rest_kernel,
            out_shape=[block((7, width, half))] * 2,
            in_specs=[VMEM] * 2,
            out_specs=[VMEM] * 2,
            compiler_params=room,
            cost_estimate=free,
            name="rest_products",
        )(masked, features)

        def add(*terms, name, count=1):
            picks = [pick for _, pick in terms]
            return pl.pallas_call(
                functools.partial(add_kernel, picks),
                out_shape=block((count, width, half)),
                in_specs=[ANY if pick is None else VMEM for pick in picks],
                out_specs=VMEM,
                compiler_params=room,
                cost_estimate=free,
                name=name,
            )(*(array for array, _ in terms))

        def part(number, count=1):
            return slice(number, number + count)

        state, piece = block(params.shape), block(global_fragment.shape)
        come_far = hop(away_far, "fsdp", devices, 1)
        sent = add((kept_far, part(0)), (come_far, part(0)), (fragment_index, None), name="add_a1")
        far_left = hop(sent, "fsdp", devices, 2)
        away, _ = lax.optimization_barrier((away, sent))
        come = hop(away, "fsdp", devices, 1)
        drift, scale = pl.pallas_call(
            drift_kernel,
            out_shape=[piece, block((rows, width))],
            in_specs=[VMEM, SMEM, VMEM, VMEM, ANY],
            out_specs=[VMEM] * 2,
            compiler_params=room,
            cost_estimate=free,
            name="drift",
        )(info, fragment_index, params, global_fragment, sent)
        sent = add((kept, part(6)), (come, part(6)), (drift, None), name="add_a2")
        far_right = hop(sent, "fsdp", devices, 2)
        passed = add((kept, part(4)), (come, part(4)), (far_left, part(0)), name="add_c1")
        far_left = hop(passed, "fsdp", devices, 4)
        near_left = add((kept, part(2)), (come, part(2)), (sent, None), name="add_n1")
        far_right = add((kept, part(5)), (come, part(5)), (far_right, part(0)), (passed, None), name="add_c2")
        near_right = add((kept, part(3)), (come, part(3)), (passed, None), name="add_n2")
        drift, _ = lax.optimization_barrier((drift, sent))
        bit = workers // 2
        drifts = (drift, hop(drift, "worker", workers, bit))
        while bit > 1:
            bit //= 2
            drift = drifts[0] + drifts[1]
            drift, _ = lax.optimization_barrier((drift, near_right))
            drifts = (drift, hop(drift, "worker", workers, bit))
        near_left = hop(near_left, "fsdp", devices, 2)
        far_right = hop(far_right, "fsdp", devices, 4)
        near_right = hop(near_right, "fsdp", devices, 2)
        groups = half // LANES
        held_half = pltpu.VMEM((half, width), jnp.float32)
        own, first_base, second_base, base, step, *results, new_global, new_momentum = pl.pallas_call(
            left_kernel,
            out_shape=[block((half, width))] * 5 + [state] * 3 + [piece] * 2,
            in_specs=[VMEM] * 13,
            out_specs=[VMEM] * 5 + [HBM] * 5,
            scratch_shapes=[held_half] * 3
            + [held_piece] * 2
            + [pltpu.VMEM((rows, width), jnp.float32), pltpu.SemaphoreType.DMA((2 + 3 * groups,))],
            compiler_params=room,
            cost_estimate=pl.CostEstimate(
                flops=30 * half * width, bytes_accessed=40 * half * width, transcendentals=2 * half * width
            ),
            name="left_step",
        )(
            params,
            first,
            second,
            kept,
            come,
            far_left,
            near_left,
            info,
            scale,
            global_fragment,
            outer_momentum,
            *drifts,
        )
        new_params, new_first, new_second = pl.pallas_call(
            right_kernel,
            out_shape=[state] * 3,
            in_specs=[VMEM] * 8 + [HBM] * 3,
            out_specs=[HBM] * 3,
            input_output_aliases={8: 0, 9: 1, 10: 2},
            scratch_shapes=[held_half] * 3 + [pltpu.SemaphoreType.DMA((3 * groups,))],
            compiler_params=room,
            cost_estimate=free,
            name="right_step",
        )(far_right, near_right, info, own, first_base, second_base, base, step, *results)
        return new_params, new_first, new_second, new_global, new_momentum

    return body


def plain_body(mesh):
    workers, devices = mesh.shape["worker"], mesh.shape["fsdp"]

    def body(
        params, first, second, global_fragment, outer_momentum, features, cotangent, token_counts, fragment_index
    ):
        rows, width = params.shape[1:]
        tokens = features.shape[1]
        me = lax.axis_index("fsdp")
        count = lax.dynamic_index_in_dim(token_counts, lax.axis_index("worker"), 0, keepdims=False)
        live = count.astype(jnp.float32)
        valid = (me * tokens + lax.iota(jnp.int32, tokens) < count)[:, None]
        masked = jnp.where(valid, cotangent[0], jnp.zeros_like(cotangent[0]))
        term = lax.dot_general(features[0], masked, (((0,), (0,)), ((), ())), preferred_element_type=jnp.float32)
        blocks = jnp.take(term.reshape(devices, rows, width), me ^ jnp.arange(devices, dtype=jnp.int32), axis=0)
        bit = 1
        while bit < devices:
            blocks = blocks.reshape(-1, 2, rows, width)
            blocks = blocks[:, 0] + hop(blocks[:, 1], "fsdp", devices, bit)
            bit *= 2
        gradient = blocks[0] / live
        grouped = (rows // FRAGS, FRAGS, width)
        old = lax.dynamic_index_in_dim(params[0].reshape(grouped), fragment_index[0], 1, keepdims=False)
        drift_sum = doubling_sum(live * (global_fragment - old), "worker", workers)
        total = jnp.sum(token_counts).astype(jnp.float32)
        fresh, momentum = outer(drift_sum / total, global_fragment, outer_momentum)
        inner, first_new, second_new = adam(params[0], first[0], second[0], gradient)
        inner = inner.reshape(grouped)
        piece = lax.dynamic_index_in_dim(inner, fragment_index[0], 1, keepdims=False)
        mixed = MIXING * fresh + (1.0 - MIXING) * piece
        merged = lax.dynamic_update_index_in_dim(inner, mixed, fragment_index[0], 1).reshape(rows, width)
        return merged[None], first_new[None], second_new[None], fresh, momentum

    return body


def solution(mesh):
    devices = mesh.shape["fsdp"]

    def pick(*arrays):
        rows = arrays[0].shape[1]
        body = fast_body(mesh) if devices == 8 and rows % LANES == 0 else plain_body(mesh)
        return body(*arrays)

    state = P("worker", "fsdp", None)
    piece = P("fsdp", None)
    return jax.shard_map(
        pick,
        mesh=mesh,
        in_specs=(state, state, state, piece, piece, state, state, P(), P()),
        out_specs=(state, state, state, piece, piece),
        check_vma=False,
    )
```

```python
import functools

import jax
import jax.numpy as jnp
from jax import lax
from jax.experimental import pallas as pl
from jax.experimental.pallas import tpu as pltpu
from jax.sharding import PartitionSpec as P

FRAGS = 4
LANES = 128

BETA_ONE = 0.9
BETA_TWO = 0.95
CORRECT_ONE = 0.6513216
CORRECT_TWO = 0.401263
ADAM_EPS = 1e-08
LEARN_RATE = 0.02
DECAY_RATE = 0.1
NESTEROV = 0.9
OUTER_RATE = 0.7
MIXING = 0.5

VMEM = pl.BlockSpec(memory_space=pltpu.VMEM)
SMEM = pl.BlockSpec(memory_space=pltpu.SMEM)
HBM = pl.BlockSpec(memory_space=pltpu.HBM)
ANY = pl.BlockSpec(memory_space=pl.ANY)
ROOM = 8 << 20


def masked_columns(live, cotangent):
    turned = cotangent.astype(jnp.float32).T
    tokens = lax.broadcasted_iota(jnp.int32, turned.shape, 1)
    return jnp.where(tokens < live, turned, 0.0).astype(jnp.bfloat16)


def columns_of(relative, rows, start, size):
    return pl.ds(pl.multiple_of((lax.axis_index("fsdp") ^ relative) * rows + start, LANES), size)


def product(masked, features):
    return jnp.dot(masked, features, preferred_element_type=jnp.float32)


def fetch(sources, targets, sems, start=0):
    copies = [
        pltpu.make_async_copy(source, target, sems.at[start + slot])
        for slot, (source, target) in enumerate(zip(sources, targets))
    ]
    for copy in copies:
        copy.start()
    return copies


def first_kernel(
    workers, order, counts, cotangent, features, away, kept, masked, info, counts_held, cot_held, held, sems
):
    half = away.shape[2]
    small = fetch((counts, cotangent), (counts_held, cot_held), sems)
    columns = [columns_of(q, 2 * half, 0, half) for q in order]
    blocks = fetch([features.at[0, :, c] for c in columns], [held.at[n] for n in range(len(order))], sems, len(small))
    for copy in small:
        copy.wait()
    tokens = cot_held.shape[1]
    live = counts_held[lax.axis_index("worker")] - lax.axis_index("fsdp") * tokens
    masked[...] = masked_columns(live, cot_held[0])
    for slot, into in enumerate((away, kept)):
        blocks[slot].wait()
        into[0] = product(masked[...], held[slot])
    count, total = counts_held[lax.axis_index("worker")], counts_held[0]
    for other in range(1, workers):
        total = total + counts_held[other]
    info[0:1, :] = jnp.full((1, info.shape[1]), count.astype(jnp.float32))
    info[1:2, :] = 1.0 / info[0:1, :]
    info[2:3, :] = 1.0 / jnp.full((1, info.shape[1]), total.astype(jnp.float32))


def rest_kernel(masked, features, away, kept):
    half = away.shape[2]
    for at, (q, side) in enumerate(((0, 0), (0, 1), (2, 0), (2, 1), (4, 0), (4, 1), (6, 1))):
        for core, into in ((1, away), (0, kept)):
            columns = columns_of(q + core, 2 * half, side * half, half)
            into[at] = product(masked[...], features[0, :, columns])


def drift_kernel(info, fragment, params, global_fragment, after, drift, scale):
    del after
    index = fragment[0]
    pieces = drift.shape[0]
    old = params[0, pl.ds(0, pieces, stride=FRAGS), :]
    for at in range(1, FRAGS):
        old = jnp.where(index == at, params[0, pl.ds(at, pieces, stride=FRAGS), :], old)
    drift[...] = info[0:1, :] * (global_fragment[...] - old)
    rows = lax.broadcasted_iota(jnp.int32, scale.shape, 0)
    scale[...] = jnp.where(lax.rem(rows, FRAGS) == index, 1.0 - MIXING, 1.0)


def add_kernel(picks, *refs):
    total = None
    for ref, pick in zip(refs, picks):
        if pick is not None:
            total = ref[pick] if total is None else total + ref[pick]
    refs[-1][...] = total


def adam(before, first, second, gradient):
    first_new = BETA_ONE * first + (1.0 - BETA_ONE) * gradient
    second_new = BETA_TWO * second + (1.0 - BETA_TWO) * gradient * gradient
    update = first_new * (1.0 / CORRECT_ONE) / (jnp.sqrt(second_new * (1.0 / CORRECT_TWO)) + ADAM_EPS)
    return before - LEARN_RATE * (update + DECAY_RATE * before), first_new, second_new


def outer(pseudo_grad, global_fragment, outer_momentum):
    momentum = NESTEROV * outer_momentum + pseudo_grad
    return global_fragment - OUTER_RATE * (pseudo_grad + NESTEROV * momentum), momentum


def half_step(half, states, sums, info, held):
    params, first, second = states
    kept, come, far, near = sums
    held_first, held_second = held
    rows = kept.shape[2]
    for lane in range(0, rows, LANES):
        lanes, there = pl.ds(lane, LANES), pl.ds(half * rows + lane, LANES)
        summed = kept[half, :, lanes] + come[half, :, lanes] + near[0, :, lanes] + far[0, :, lanes]
        inner, held_first[lanes, :], held_second[lanes, :] = adam(
            params[0, there, :], first[0, there, :], second[0, there, :], summed.T * info[1:2, :]
        )
        yield lanes, there, inner


def send(copies, sems, source, target):
    copies.append(pltpu.make_async_copy(source, target, sems.at[len(copies)]))
    copies[-1].start()


def left_kernel(
    params,
    first,
    second,
    kept,
    come,
    far,
    near,
    info,
    scale,
    global_fragment,
    outer_momentum,
    drift,
    other_drift,
    own,
    first_base,
    second_base,
    base,
    step,
    new_params,
    new_first,
    new_second,
    new_global,
    new_momentum,
    held_params,
    held_first,
    held_second,
    held_global,
    held_momentum,
    spread,
    sems,
):
    copies = []
    fresh, momentum = outer((drift[...] + other_drift[...]) * info[2:3, :], global_fragment[...], outer_momentum[...])
    held_global[...] = fresh
    held_momentum[...] = momentum
    send(copies, sems, held_global, new_global)
    send(copies, sems, held_momentum, new_momentum)
    for at in range(FRAGS):
        spread[pl.ds(at, fresh.shape[0], stride=FRAGS), :] = fresh
    for lanes, there, value in half_step(
        0, (params, first, second), (kept, come, far, near), info, (held_first, held_second)
    ):
        held_params[lanes, :] = scale[there, :] * value + (1.0 - scale[there, :]) * spread[there, :]
        for source, target in ((held_first, new_first), (held_second, new_second), (held_params, new_params)):
            send(copies, sems, source.at[lanes], target.at[0, there])
    rows = own.shape[0]
    for lane in range(0, rows, LANES):
        lanes, there = pl.ds(lane, LANES), pl.ds(rows + lane, LANES)
        own[lanes, :] = (kept[1, :, lanes] + come[1, :, lanes]).T * info[1:2, :]
        first_base[lanes, :] = BETA_ONE * first[0, there, :]
        second_base[lanes, :] = BETA_TWO * second[0, there, :]
        base[lanes, :] = scale[there, :] * ((1.0 - LEARN_RATE * DECAY_RATE) * params[0, there, :]) + (
            1.0 - scale[there, :]
        ) * spread[there, :]
        step[lanes, :] = (LEARN_RATE / CORRECT_ONE) * scale[there, :]
    for copy in copies:
        copy.wait()


def right_kernel(
    far,
    near,
    info,
    own,
    first_base,
    second_base,
    base,
    step,
    left_params,
    left_first,
    left_second,
    new_params,
    new_first,
    new_second,
    held_params,
    held_first,
    held_second,
    sems,
):
    del left_params, left_first, left_second
    copies = []
    rows = own.shape[0]
    for lane in range(0, rows, LANES):
        lanes = pl.ds(lane, LANES)
        arrived = (near[0, :, lanes] + far[0, :, lanes]).T * info[1:2, :]
        for at in range(0, LANES, LANES // 2):
            here, there = pl.ds(lane + at, LANES // 2), pl.ds(rows + lane + at, LANES // 2)
            gradient = own[here, :] + arrived[at : at + LANES // 2]
            first_new = first_base[here, :] + (1.0 - BETA_ONE) * gradient
            second_new = second_base[here, :] + (1.0 - BETA_TWO) * gradient * gradient
            held_first[here, :] = first_new
            held_second[here, :] = second_new
            held_params[here, :] = base[here, :] - step[here, :] * first_new / (
                jnp.sqrt(second_new * (1.0 / CORRECT_TWO)) + ADAM_EPS
            )
            for source, target in ((held_first, new_first), (held_second, new_second), (held_params, new_params)):
                send(copies, sems, source.at[here], target.at[0, there])
    for copy in copies:
        copy.wait()


def hop(value, axis, devices, bit):
    return lax.ppermute(value, axis, [(d, d ^ bit) for d in range(devices)])


def doubling_sum(value, axis, devices):
    bit = devices // 2
    while bit:
        value = value + hop(value, axis, devices, bit)
        bit //= 2
    return value


def fast_body(mesh):
    workers, devices = mesh.shape["worker"], mesh.shape["fsdp"]

    def body(
        params, first, second, global_fragment, outer_momentum, features, cotangent, token_counts, fragment_index
    ):
        rows, width = params.shape[1:]
        pieces, tokens = global_fragment.shape[0], features.shape[1]
        block = functools.partial(jax.ShapeDtypeStruct, dtype=jnp.float32)

        def cost(count):
            return pl.CostEstimate(
                flops=2 * count * tokens * rows * width,
                bytes_accessed=count * rows * (2 * tokens + 4 * width),
                transcendentals=0,
            )

        room = pltpu.CompilerParams(vmem_limit_bytes=ROOM)
        free = pl.CostEstimate(flops=0, bytes_accessed=0, transcendentals=0)
        far_counts, far_features, far_cotangent = (
            pltpu.with_memory_space_constraint(array, pltpu.HBM) for array in (token_counts, features, cotangent)
        )
        held_counts = pltpu.SMEM(token_counts.shape, token_counts.dtype)
        held_piece = pltpu.VMEM(global_fragment.shape, global_fragment.dtype)

        half = rows // 2
        away_far, kept_far, masked, info = pl.pallas_call(
            functools.partial(first_kernel, workers, (7, 6)),
            out_shape=[block((1, width, half))] * 2 + [jax.ShapeDtypeStruct((width, tokens), jnp.bfloat16), block((8, width))],
            in_specs=[HBM] * 3,
            out_specs=[VMEM] * 4,
            scratch_shapes=[
                held_counts,
                pltpu.VMEM(cotangent.shape, cotangent.dtype),
                pltpu.VMEM((2, tokens, half), features.dtype),
                pltpu.SemaphoreType.DMA((4,)),
            ],
            compiler_params=room,
            cost_estimate=cost(2),
            name="far_products",
        )(far_counts, far_cotangent, far_features)
        away, kept = pl.pallas_call(
            rest_kernel,
            out_shape=[block((7, width, half))] * 2,
            in_specs=[VMEM] * 2,
            out_specs=[VMEM] * 2,
            compiler_params=room,
            cost_estimate=free,
            name="rest_products",
        )(masked, features)

        def add(*terms, name, count=1):
            picks = [pick for _, pick in terms]
            return pl.pallas_call(
                functools.partial(add_kernel, picks),
                out_shape=block((count, width, half)),
                in_specs=[ANY if pick is None else VMEM for pick in picks],
                out_specs=VMEM,
                compiler_params=room,
                cost_estimate=free,
                name=name,
            )(*(array for array, _ in terms))

        def part(number, count=1):
            return slice(number, number + count)

        state, piece = block(params.shape), block(global_fragment.shape)
        come_far = hop(away_far, "fsdp", devices, 1)
        sent = add((kept_far, part(0)), (come_far, part(0)), (fragment_index, None), name="add_a1")
        far_left = hop(sent, "fsdp", devices, 2)
        away, _ = lax.optimization_barrier((away, sent))
        come = hop(away, "fsdp", devices, 1)
        drift, scale = pl.pallas_call(
            drift_kernel,
            out_shape=[piece, block((rows, width))],
            in_specs=[VMEM, SMEM, VMEM, VMEM, ANY],
            out_specs=[VMEM] * 2,
            compiler_params=room,
            cost_estimate=free,
            name="drift",
        )(info, fragment_index, params, global_fragment, sent)
        sent = add((kept, part(6)), (come, part(6)), (drift, None), name="add_a2")
        far_right = hop(sent, "fsdp", devices, 2)
        passed = add((kept, part(4)), (come, part(4)), (far_left, part(0)), name="add_c1")
        far_left = hop(passed, "fsdp", devices, 4)
        near_left = add((kept, part(2)), (come, part(2)), (sent, None), name="add_n1")
        far_right = add((kept, part(5)), (come, part(5)), (far_right, part(0)), (passed, None), name="add_c2")
        near_right = add((kept, part(3)), (come, part(3)), (passed, None), name="add_n2")
        drift, _ = lax.optimization_barrier((drift, sent))
        bit = workers // 2
        drifts = (drift, hop(drift, "worker", workers, bit))
        while bit > 1:
            bit //= 2
            drift = drifts[0] + drifts[1]
            drift, _ = lax.optimization_barrier((drift, near_right))
            drifts = (drift, hop(drift, "worker", workers, bit))
        near_left = hop(near_left, "fsdp", devices, 2)
        far_right = hop(far_right, "fsdp", devices, 4)
        near_right = hop(near_right, "fsdp", devices, 2)
        groups = half // LANES
        held_half = pltpu.VMEM((half, width), jnp.float32)
        own, first_base, second_base, base, step, *results, new_global, new_momentum = pl.pallas_call(
            left_kernel,
            out_shape=[block((half, width))] * 5 + [state] * 3 + [piece] * 2,
            in_specs=[VMEM] * 13,
            out_specs=[VMEM] * 5 + [HBM] * 5,
            scratch_shapes=[held_half] * 3
            + [held_piece] * 2
            + [pltpu.VMEM((rows, width), jnp.float32), pltpu.SemaphoreType.DMA((2 + 3 * groups,))],
            compiler_params=room,
            cost_estimate=pl.CostEstimate(
                flops=30 * half * width, bytes_accessed=40 * half * width, transcendentals=2 * half * width
            ),
            name="left_step",
        )(
            params,
            first,
            second,
            kept,
            come,
            far_left,
            near_left,
            info,
            scale,
            global_fragment,
            outer_momentum,
            *drifts,
        )
        new_params, new_first, new_second = pl.pallas_call(
            right_kernel,
            out_shape=[state] * 3,
            in_specs=[VMEM] * 8 + [HBM] * 3,
            out_specs=[HBM] * 3,
            input_output_aliases={8: 0, 9: 1, 10: 2},
            scratch_shapes=[held_half] * 3 + [pltpu.SemaphoreType.DMA((6 * groups,))],
            compiler_params=room,
            cost_estimate=free,
            name="right_step",
        )(far_right, near_right, info, own, first_base, second_base, base, step, *results)
        return new_params, new_first, new_second, new_global, new_momentum

    return body


def plain_body(mesh):
    workers, devices = mesh.shape["worker"], mesh.shape["fsdp"]

    def body(
        params, first, second, global_fragment, outer_momentum, features, cotangent, token_counts, fragment_index
    ):
        rows, width = params.shape[1:]
        tokens = features.shape[1]
        me = lax.axis_index("fsdp")
        count = lax.dynamic_index_in_dim(token_counts, lax.axis_index("worker"), 0, keepdims=False)
        live = count.astype(jnp.float32)
        valid = (me * tokens + lax.iota(jnp.int32, tokens) < count)[:, None]
        masked = jnp.where(valid, cotangent[0], jnp.zeros_like(cotangent[0]))
        term = lax.dot_general(features[0], masked, (((0,), (0,)), ((), ())), preferred_element_type=jnp.float32)
        blocks = jnp.take(term.reshape(devices, rows, width), me ^ jnp.arange(devices, dtype=jnp.int32), axis=0)
        bit = 1
        while bit < devices:
            blocks = blocks.reshape(-1, 2, rows, width)
            blocks = blocks[:, 0] + hop(blocks[:, 1], "fsdp", devices, bit)
            bit *= 2
        gradient = blocks[0] / live
        grouped = (rows // FRAGS, FRAGS, width)
        old = lax.dynamic_index_in_dim(params[0].reshape(grouped), fragment_index[0], 1, keepdims=False)
        drift_sum = doubling_sum(live * (global_fragment - old), "worker", workers)
        total = jnp.sum(token_counts).astype(jnp.float32)
        fresh, momentum = outer(drift_sum / total, global_fragment, outer_momentum)
        inner, first_new, second_new = adam(params[0], first[0], second[0], gradient)
        inner = inner.reshape(grouped)
        piece = lax.dynamic_index_in_dim(inner, fragment_index[0], 1, keepdims=False)
        mixed = MIXING * fresh + (1.0 - MIXING) * piece
        merged = lax.dynamic_update_index_in_dim(inner, mixed, fragment_index[0], 1).reshape(rows, width)
        return merged[None], first_new[None], second_new[None], fresh, momentum

    return body


def solution(mesh):
    devices = mesh.shape["fsdp"]

    def pick(*arrays):
        rows = arrays[0].shape[1]
        body = fast_body(mesh) if devices == 8 and rows % LANES == 0 else plain_body(mesh)
        return body(*arrays)

    state = P("worker", "fsdp", None)
    piece = P("fsdp", None)
    return jax.shard_map(
        pick,
        mesh=mesh,
        in_specs=(state, state, state, piece, piece, state, state, P(), P()),
        out_specs=(state, state, state, piece, piece),
        check_vma=False,
    )
```

```python
import functools

import jax
import jax.numpy as jnp
from jax import lax
from jax.experimental import pallas as pl
from jax.experimental.pallas import tpu as pltpu
from jax.sharding import PartitionSpec as P

FRAGS = 4
LANES = 128

BETA_ONE = 0.9
BETA_TWO = 0.95
CORRECT_ONE = 0.6513216
CORRECT_TWO = 0.401263
ADAM_EPS = 1e-08
LEARN_RATE = 0.02
DECAY_RATE = 0.1
NESTEROV = 0.9
OUTER_RATE = 0.7
MIXING = 0.5

VMEM = pl.BlockSpec(memory_space=pltpu.VMEM)
SMEM = pl.BlockSpec(memory_space=pltpu.SMEM)
HBM = pl.BlockSpec(memory_space=pltpu.HBM)
ANY = pl.BlockSpec(memory_space=pl.ANY)
ROOM = 8 << 20


def masked_columns(live, cotangent):
    turned = cotangent.astype(jnp.float32).T
    tokens = lax.broadcasted_iota(jnp.int32, turned.shape, 1)
    return jnp.where(tokens < live, turned, 0.0).astype(jnp.bfloat16)


def columns_of(relative, rows, start, size):
    return pl.ds(pl.multiple_of((lax.axis_index("fsdp") ^ relative) * rows + start, LANES), size)


def product(masked, features):
    return jnp.dot(masked, features, preferred_element_type=jnp.float32)


def fetch(sources, targets, sems, start=0):
    copies = [
        pltpu.make_async_copy(source, target, sems.at[start + slot])
        for slot, (source, target) in enumerate(zip(sources, targets))
    ]
    for copy in copies:
        copy.start()
    return copies


def first_kernel(
    workers, order, counts, cotangent, features, away, kept, masked, info, counts_held, cot_held, held, sems
):
    half = away.shape[2]
    small = fetch((counts, cotangent), (counts_held, cot_held), sems)
    columns = [columns_of(q, 2 * half, 0, half) for q in order]
    blocks = fetch([features.at[0, :, c] for c in columns], [held.at[n] for n in range(len(order))], sems, len(small))
    for copy in small:
        copy.wait()
    tokens = cot_held.shape[1]
    live = counts_held[lax.axis_index("worker")] - lax.axis_index("fsdp") * tokens
    masked[...] = masked_columns(live, cot_held[0])
    for slot, into in enumerate((away, kept)):
        blocks[slot].wait()
        into[0] = product(masked[...], held[slot])
    count, total = counts_held[lax.axis_index("worker")], counts_held[0]
    for other in range(1, workers):
        total = total + counts_held[other]
    info[0:1, :] = jnp.full((1, info.shape[1]), count.astype(jnp.float32))
    info[1:2, :] = jnp.full((1, info.shape[1]), total.astype(jnp.float32))


def rest_kernel(masked, features, away, kept):
    half = away.shape[2]
    for at, (q, side) in enumerate(((0, 0), (0, 1), (2, 0), (2, 1), (4, 0), (4, 1), (6, 1))):
        for core, into in ((1, away), (0, kept)):
            columns = columns_of(q + core, 2 * half, side * half, half)
            into[at] = product(masked[...], features[0, :, columns])


def drift_kernel(info, fragment, params, global_fragment, after, drift, scale, rates):
    del after
    index = fragment[0]
    pieces = drift.shape[0]
    old = params[0, pl.ds(0, pieces, stride=FRAGS), :]
    for at in range(1, FRAGS):
        old = jnp.where(index == at, params[0, pl.ds(at, pieces, stride=FRAGS), :], old)
    drift[...] = info[0:1, :] * (global_fragment[...] - old)
    rates[1:3, :] = 1.0 / info[0:2, :]
    rows = lax.broadcasted_iota(jnp.int32, scale.shape, 0)
    scale[...] = jnp.where(lax.rem(rows, FRAGS) == index, 1.0 - MIXING, 1.0)


def add_kernel(picks, *refs):
    total = None
    for ref, pick in zip(refs, picks):
        if pick is not None:
            total = ref[pick] if total is None else total + ref[pick]
    refs[-1][...] = total


def adam(before, first, second, gradient):
    first_new = BETA_ONE * first + (1.0 - BETA_ONE) * gradient
    second_new = BETA_TWO * second + (1.0 - BETA_TWO) * gradient * gradient
    update = first_new * (1.0 / CORRECT_ONE) / (jnp.sqrt(second_new * (1.0 / CORRECT_TWO)) + ADAM_EPS)
    return before - LEARN_RATE * (update + DECAY_RATE * before), first_new, second_new


def outer(pseudo_grad, global_fragment, outer_momentum):
    momentum = NESTEROV * outer_momentum + pseudo_grad
    return global_fragment - OUTER_RATE * (pseudo_grad + NESTEROV * momentum), momentum


def half_step(half, states, sums, info, held):
    params, first, second = states
    kept, come, far, near = sums
    held_first, held_second = held
    rows = kept.shape[2]
    for lane in range(0, rows, LANES):
        lanes, there = pl.ds(lane, LANES), pl.ds(half * rows + lane, LANES)
        summed = kept[half, :, lanes] + come[half, :, lanes] + near[0, :, lanes] + far[0, :, lanes]
        inner, held_first[lanes, :], held_second[lanes, :] = adam(
            params[0, there, :], first[0, there, :], second[0, there, :], summed.T * info[1:2, :]
        )
        yield lanes, there, inner


def send(copies, sems, source, target):
    copies.append(pltpu.make_async_copy(source, target, sems.at[len(copies)]))
    copies[-1].start()


def left_kernel(
    params,
    first,
    second,
    kept,
    come,
    far,
    near,
    info,
    scale,
    global_fragment,
    outer_momentum,
    drift,
    other_drift,
    own,
    first_base,
    second_base,
    base,
    step,
    new_params,
    new_first,
    new_second,
    new_global,
    new_momentum,
    held_params,
    held_first,
    held_second,
    held_global,
    held_momentum,
    spread,
    sems,
):
    copies = []
    fresh, momentum = outer((drift[...] + other_drift[...]) * info[2:3, :], global_fragment[...], outer_momentum[...])
    held_global[...] = fresh
    held_momentum[...] = momentum
    send(copies, sems, held_global, new_global)
    send(copies, sems, held_momentum, new_momentum)
    for at in range(FRAGS):
        spread[pl.ds(at, fresh.shape[0], stride=FRAGS), :] = fresh
    for lanes, there, value in half_step(
        0, (params, first, second), (kept, come, far, near), info, (held_first, held_second)
    ):
        held_params[lanes, :] = scale[there, :] * value + (1.0 - scale[there, :]) * spread[there, :]
        for source, target in ((held_first, new_first), (held_second, new_second), (held_params, new_params)):
            send(copies, sems, source.at[lanes], target.at[0, there])
    rows = own.shape[0]
    for lane in range(0, rows, LANES):
        lanes, there = pl.ds(lane, LANES), pl.ds(rows + lane, LANES)
        own[lanes, :] = (kept[1, :, lanes] + come[1, :, lanes]).T * info[1:2, :]
        first_base[lanes, :] = BETA_ONE * first[0, there, :]
        second_base[lanes, :] = BETA_TWO * second[0, there, :]
        base[lanes, :] = scale[there, :] * ((1.0 - LEARN_RATE * DECAY_RATE) * params[0, there, :]) + (
            1.0 - scale[there, :]
        ) * spread[there, :]
        step[lanes, :] = (LEARN_RATE / CORRECT_ONE) * scale[there, :]
    for copy in copies:
        copy.wait()


def right_kernel(
    far,
    near,
    info,
    own,
    first_base,
    second_base,
    base,
    step,
    left_params,
    left_first,
    left_second,
    new_params,
    new_first,
    new_second,
    held_params,
    held_first,
    held_second,
    sems,
):
    del left_params, left_first, left_second
    copies = []
    rows = own.shape[0]
    for lane in range(0, rows, LANES):
        lanes, there = pl.ds(lane, LANES), pl.ds(rows + lane, LANES)
        gradient = own[lanes, :] + (near[0, :, lanes] + far[0, :, lanes]).T * info[1:2, :]
        first_new = first_base[lanes, :] + (1.0 - BETA_ONE) * gradient
        second_new = second_base[lanes, :] + (1.0 - BETA_TWO) * gradient * gradient
        held_first[lanes, :] = first_new
        held_second[lanes, :] = second_new
        held_params[lanes, :] = base[lanes, :] - step[lanes, :] * first_new / (
            jnp.sqrt(second_new * (1.0 / CORRECT_TWO)) + ADAM_EPS
        )
        for source, target in ((held_first, new_first), (held_second, new_second), (held_params, new_params)):
            send(copies, sems, source.at[lanes], target.at[0, there])
    for copy in copies:
        copy.wait()


def hop(value, axis, devices, bit):
    return lax.ppermute(value, axis, [(d, d ^ bit) for d in range(devices)])


def doubling_sum(value, axis, devices):
    bit = devices // 2
    while bit:
        value = value + hop(value, axis, devices, bit)
        bit //= 2
    return value


def fast_body(mesh):
    workers, devices = mesh.shape["worker"], mesh.shape["fsdp"]

    def body(
        params, first, second, global_fragment, outer_momentum, features, cotangent, token_counts, fragment_index
    ):
        rows, width = params.shape[1:]
        pieces, tokens = global_fragment.shape[0], features.shape[1]
        block = functools.partial(jax.ShapeDtypeStruct, dtype=jnp.float32)

        def cost(count):
            return pl.CostEstimate(
                flops=2 * count * tokens * rows * width,
                bytes_accessed=count * rows * (2 * tokens + 4 * width),
                transcendentals=0,
            )

        room = pltpu.CompilerParams(vmem_limit_bytes=ROOM)
        free = pl.CostEstimate(flops=0, bytes_accessed=0, transcendentals=0)
        far_counts, far_features, far_cotangent = (
            pltpu.with_memory_space_constraint(array, pltpu.HBM) for array in (token_counts, features, cotangent)
        )
        held_counts = pltpu.SMEM(token_counts.shape, token_counts.dtype)
        held_piece = pltpu.VMEM(global_fragment.shape, global_fragment.dtype)

        half = rows // 2
        away_far, kept_far, masked, info = pl.pallas_call(
            functools.partial(first_kernel, workers, (7, 6)),
            out_shape=[block((1, width, half))] * 2 + [jax.ShapeDtypeStruct((width, tokens), jnp.bfloat16), block((8, width))],
            in_specs=[HBM] * 3,
            out_specs=[VMEM] * 4,
            scratch_shapes=[
                held_counts,
                pltpu.VMEM(cotangent.shape, cotangent.dtype),
                pltpu.VMEM((2, tokens, half), features.dtype),
                pltpu.SemaphoreType.DMA((4,)),
            ],
            compiler_params=room,
            cost_estimate=cost(2),
            name="far_products",
        )(far_counts, far_cotangent, far_features)
        away, kept = pl.pallas_call(
            rest_kernel,
            out_shape=[block((7, width, half))] * 2,
            in_specs=[VMEM] * 2,
            out_specs=[VMEM] * 2,
            compiler_params=room,
            cost_estimate=free,
            name="rest_products",
        )(masked, features)

        def add(*terms, name, count=1):
            picks = [pick for _, pick in terms]
            return pl.pallas_call(
                functools.partial(add_kernel, picks),
                out_shape=block((count, width, half)),
                in_specs=[ANY if pick is None else VMEM for pick in picks],
                out_specs=VMEM,
                compiler_params=room,
                cost_estimate=free,
                name=name,
            )(*(array for array, _ in terms))

        def part(number, count=1):
            return slice(number, number + count)

        state, piece = block(params.shape), block(global_fragment.shape)
        come_far = hop(away_far, "fsdp", devices, 1)
        sent = add((kept_far, part(0)), (come_far, part(0)), (fragment_index, None), name="add_a1")
        far_left = hop(sent, "fsdp", devices, 2)
        away, _ = lax.optimization_barrier((away, sent))
        come = hop(away, "fsdp", devices, 1)
        drift, scale, rates = pl.pallas_call(
            drift_kernel,
            out_shape=[piece, block((rows, width)), block((8, width))],
            in_specs=[VMEM, SMEM, VMEM, VMEM, ANY],
            out_specs=[VMEM] * 3,
            compiler_params=room,
            cost_estimate=free,
            name="drift",
        )(info, fragment_index, params, global_fragment, sent)
        sent = add((kept, part(6)), (come, part(6)), (drift, None), name="add_a2")
        far_right = hop(sent, "fsdp", devices, 2)
        passed = add((kept, part(4)), (come, part(4)), (far_left, part(0)), name="add_c1")
        far_left = hop(passed, "fsdp", devices, 4)
        near_left = add((kept, part(2)), (come, part(2)), (sent, None), name="add_n1")
        far_right = add((kept, part(5)), (come, part(5)), (far_right, part(0)), (passed, None), name="add_c2")
        near_right = add((kept, part(3)), (come, part(3)), (passed, None), name="add_n2")
        drift, _ = lax.optimization_barrier((drift, sent))
        bit = workers // 2
        drifts = (drift, hop(drift, "worker", workers, bit))
        while bit > 1:
            bit //= 2
            drift = drifts[0] + drifts[1]
            drift, _ = lax.optimization_barrier((drift, near_right))
            drifts = (drift, hop(drift, "worker", workers, bit))
        near_left = hop(near_left, "fsdp", devices, 2)
        far_right = hop(far_right, "fsdp", devices, 4)
        near_right = hop(near_right, "fsdp", devices, 2)
        groups = half // LANES
        held_half = pltpu.VMEM((half, width), jnp.float32)
        own, first_base, second_base, base, step, *results, new_global, new_momentum = pl.pallas_call(
            left_kernel,
            out_shape=[block((half, width))] * 5 + [state] * 3 + [piece] * 2,
            in_specs=[VMEM] * 13,
            out_specs=[VMEM] * 5 + [HBM] * 5,
            scratch_shapes=[held_half] * 3
            + [held_piece] * 2
            + [pltpu.VMEM((rows, width), jnp.float32), pltpu.SemaphoreType.DMA((2 + 3 * groups,))],
            compiler_params=room,
            cost_estimate=pl.CostEstimate(
                flops=30 * half * width, bytes_accessed=40 * half * width, transcendentals=2 * half * width
            ),
            name="left_step",
        )(
            params,
            first,
            second,
            kept,
            come,
            far_left,
            near_left,
            rates,
            scale,
            global_fragment,
            outer_momentum,
            *drifts,
        )
        new_params, new_first, new_second = pl.pallas_call(
            right_kernel,
            out_shape=[state] * 3,
            in_specs=[VMEM] * 8 + [HBM] * 3,
            out_specs=[HBM] * 3,
            input_output_aliases={8: 0, 9: 1, 10: 2},
            scratch_shapes=[held_half] * 3 + [pltpu.SemaphoreType.DMA((3 * groups,))],
            compiler_params=room,
            cost_estimate=free,
            name="right_step",
        )(far_right, near_right, rates, own, first_base, second_base, base, step, *results)
        return new_params, new_first, new_second, new_global, new_momentum

    return body


def plain_body(mesh):
    workers, devices = mesh.shape["worker"], mesh.shape["fsdp"]

    def body(
        params, first, second, global_fragment, outer_momentum, features, cotangent, token_counts, fragment_index
    ):
        rows, width = params.shape[1:]
        tokens = features.shape[1]
        me = lax.axis_index("fsdp")
        count = lax.dynamic_index_in_dim(token_counts, lax.axis_index("worker"), 0, keepdims=False)
        live = count.astype(jnp.float32)
        valid = (me * tokens + lax.iota(jnp.int32, tokens) < count)[:, None]
        masked = jnp.where(valid, cotangent[0], jnp.zeros_like(cotangent[0]))
        term = lax.dot_general(features[0], masked, (((0,), (0,)), ((), ())), preferred_element_type=jnp.float32)
        blocks = jnp.take(term.reshape(devices, rows, width), me ^ jnp.arange(devices, dtype=jnp.int32), axis=0)
        bit = 1
        while bit < devices:
            blocks = blocks.reshape(-1, 2, rows, width)
            blocks = blocks[:, 0] + hop(blocks[:, 1], "fsdp", devices, bit)
            bit *= 2
        gradient = blocks[0] / live
        grouped = (rows // FRAGS, FRAGS, width)
        old = lax.dynamic_index_in_dim(params[0].reshape(grouped), fragment_index[0], 1, keepdims=False)
        drift_sum = doubling_sum(live * (global_fragment - old), "worker", workers)
        total = jnp.sum(token_counts).astype(jnp.float32)
        fresh, momentum = outer(drift_sum / total, global_fragment, outer_momentum)
        inner, first_new, second_new = adam(params[0], first[0], second[0], gradient)
        inner = inner.reshape(grouped)
        piece = lax.dynamic_index_in_dim(inner, fragment_index[0], 1, keepdims=False)
        mixed = MIXING * fresh + (1.0 - MIXING) * piece
        merged = lax.dynamic_update_index_in_dim(inner, mixed, fragment_index[0], 1).reshape(rows, width)
        return merged[None], first_new[None], second_new[None], fresh, momentum

    return body


def solution(mesh):
    devices = mesh.shape["fsdp"]

    def pick(*arrays):
        rows = arrays[0].shape[1]
        body = fast_body(mesh) if devices == 8 and rows % LANES == 0 else plain_body(mesh)
        return body(*arrays)

    state = P("worker", "fsdp", None)
    piece = P("fsdp", None)
    return jax.shard_map(
        pick,
        mesh=mesh,
        in_specs=(state, state, state, piece, piece, state, state, P(), P()),
        out_specs=(state, state, state, piece, piece),
        check_vma=False,
    )
```
